128 devices in a mesh: row: 16 (over y, x), col: 8 (over z, core).
Axes of the slice: x: 4, y: 4, z: 4, core: 2. Of those that a mesh axis runs over, the one named last changes fastest.
Arguments:
- object_field: float32 [2, 8192, 4096], P(None, 'row', 'col'), may hold values from -6 to 6
- probe: float32 [2, 512, 512], replicated, may hold values from -6 to 6
- amplitudes: float32 [256, 512, 512], P(('row', 'col')), may hold values from 0.1 to 3
- positions: int32 [256, 2], P(('row', 'col')), may hold values from 0 to 7680, as said below
Outputs:
- new_object: float32 [2, 8192, 4096], P(None, 'row', 'col')
- new_probe: float32 [2, 512, 512], replicated
The draws below stay inside these ranges and needn't reach their ends.
Inputs may be any that keep to these rules, and one draw needn't show every extreme that they name: `positions`: scan position j belongs to device d = j // 2 (row-major over row, col); its row offset is 512 * (d // 8) plus 0 to 511, at most 7680; its column offset is 512 * (d % 8) plus 0 to 511, at most 3584.
All inputs are finite; a program needn't handle non-finite values. Where the reference program divides by a largest or mean magnitude, that divisor is 1e-20 or more.
Results may differ from the reference program's by a relative error of at most 0.00016.
Values sent between devices are 32-bit elements; how exact they have to be, the bound alone decides.
No kernel may reach another device: no remote copies, remote signals or barrier semaphores. Data moves between devices by JAX's collectives and lax.ppermute only.
A program may use at most 128 MiB of HBM per device.

```python
import math
import jax
import jax.numpy as jnp
from jax import lax

PS = 512
P_DEV = 2
NR = 8192
NC = 4096
NPAT = 256


def draw_positions(key, part):
    key = jax.random.fold_in(key, 7)
    index = jnp.arange(NPAT, dtype=jnp.int32)
    device = index // P_DEV
    tile_row = device // (NC // PS)
    tile_col = device % (NC // PS)
    jitter = jax.random.randint(key, (NPAT, 2), 0, PS, dtype=jnp.int32)
    first = jnp.minimum(tile_row * PS + jitter[:, 0], NR - PS)
    second = jnp.minimum(tile_col * PS + jitter[:, 1], NC - PS)
    return jnp.stack([first, second], axis=1).astype(jnp.int32)


def levels(key, shape, pieces, least, high):
    def one(position, shards_of):
        heights = jax.random.uniform(jax.random.fold_in(jax.random.fold_in(key, 6), position), (shards_of,), jnp.float32, least / len(pieces), high / len(pieces))
        return jnp.repeat(jnp.exp(heights), shape[position] // shards_of).reshape((-1,) + (1,) * (len(shape) - position - 1))

    loudness = one(*pieces[0])
    for cut in pieces[1:]:
        loudness = loudness * one(*cut)
    return loudness


def scatter_about(own_key, extent, spread, limit, shards=(), kind=jnp.bfloat16):
    factor_of = levels(own_key, extent, shards, -0.22, 0.18) if shards else 1.0
    entries = jax.random.normal(own_key, extent, jnp.float32) * spread * factor_of
    return jnp.minimum(jnp.maximum(entries, -limit), limit).astype(kind)


def setup_inputs(seed: int = 0) -> dict:
    key_list = jax.random.split(jax.random.key(seed), 5)
    return {
        "object_field": scatter_about(key_list[0], (2, NR, NC), 1.0, 6.0, ((1, 16), (2, 8)), jnp.float32),
        "probe": scatter_about(key_list[1], (2, PS, PS), 1.0, 6.0, (), jnp.float32),
        "amplitudes": jnp.clip(jnp.exp(math.log(3.0) - 3.4011974 * jax.random.uniform(key_list[2], (NPAT, PS, PS), jnp.float32) ** levels(key_list[2], (NPAT, PS, PS), ((0, 128),), -0.2, 0.2)), 0.1, 3.0),
        "positions": draw_positions(jax.random.fold_in(key_list[4], 71), 0),
    }


def reference(object_field, probe, amplitudes, positions):
    whole = object_field[0] + 1j * object_field[1]
    beam = probe[0] + 1j * probe[1]

    def visit(carry, inputs):
        update, gradient = carry
        amp, pos = inputs
        patch = lax.dynamic_slice(whole, (pos[0], pos[1]), (PS, PS))
        psi = beam * patch
        spectrum = jnp.fft.fft2(psi, norm='ortho')
        scaled = amp * spectrum / jnp.sqrt(jnp.abs(spectrum) ** 2 + 0.25)
        diff = jnp.fft.ifft2(scaled, norm='ortho') - psi
        old = lax.dynamic_slice(update, (pos[0], pos[1]), (PS, PS))
        update = lax.dynamic_update_slice(update, old + jnp.conj(beam) * diff, (pos[0], pos[1]))
        gradient = gradient + jnp.conj(patch) * diff
        return ((update, gradient), None)
    start = (jnp.zeros_like(whole), jnp.zeros_like(beam))
    (update, gradient), _ = lax.scan(visit, start, (amplitudes, positions))
    probe_peak = jnp.max(jnp.abs(beam) ** 2)
    object_peak = jnp.max(jnp.abs(whole) ** 2)
    fresh = whole + 0.9 * update / (probe_peak + 1e-06)
    beam_new = beam + 0.5 * gradient / (object_peak + 1e-06)
    return (jnp.stack([jnp.real(fresh), jnp.imag(fresh)]).astype(object_field.dtype), jnp.stack([jnp.real(beam_new), jnp.imag(beam_new)]).astype(probe.dtype))
```

```python
import functools
import math

import jax
import jax.numpy as jnp
import numpy as np
from jax import lax
from jax.experimental import pallas as pl
from jax.experimental.pallas import tpu as pltpu
from jax.sharding import PartitionSpec as P

SIDE = 512
QUARTER = 128
PIECES = 4
PIECE = SIDE // PIECES
VMEM_LIMIT = 60 * 1024 * 1024
F32 = jnp.float32
BF16 = jnp.bfloat16


def split_matrices():
    k = np.arange(QUARTER)[:, None]
    n = np.arange(QUARTER)[None, :]
    parts = []
    for p in range(4):
        angle = 2.0 * np.pi * (((4 * k + p) * n) % SIDE) / SIDE
        re, im = np.cos(angle) / np.sqrt(SIDE), -np.sin(angle) / np.sqrt(SIDE)
        parts.append(np.block([[re, -im], [im, re]]))
    left = np.stack(parts)
    out = []
    for matrix in (left, np.swapaxes(left, 1, 2)):
        high = matrix.astype(np.float32).astype(jnp.bfloat16)
        low = (matrix - high.astype(np.float64)).astype(np.float32).astype(jnp.bfloat16)
        out += [np.ascontiguousarray(high), np.ascontiguousarray(low)]
    return out


def order_matrix():
    at = np.arange(SIDE)
    matrix = np.zeros((SIDE, SIDE), np.float32)
    matrix[at, (at % 4) * QUARTER + at // 4] = 1.0
    return matrix.astype(jnp.bfloat16)


def split(value):
    high = value.astype(BF16)
    return high, (value - high.astype(F32)).astype(BF16)


def mm(left, right):
    return jnp.dot(left, right, preferred_element_type=F32)


def fold(x, sign):
    (r0, i0), (r1, i1), (r2, i2), (r3, i3) = x
    sr, si, dr, di = r0 + r2, i0 + i2, r0 - r2, i0 - i2
    tr, ti, er, ei = r1 + r3, i1 + i3, r1 - r3, i1 - i3
    first = (dr + ei, di - er)
    second = (dr - ei, di + er)
    if sign > 0:
        first, second = second, first
    return [(sr + tr, si + ti), first, (sr - tr, si - ti), second]


def ready_kernel(where_ref, probe_ref, own_ref, amp_ref, order_ref, rolled_ref, amps_ref, peaks_ref, columns):
    for item in range(2):
        down, along = where_ref[0, item], where_ref[1, item]
        for part in range(2):
            value = pltpu.roll(probe_ref[part], down, 0)
            rolled_ref[item, part] = pltpu.roll(value, along, 1)
        rows = amp_ref[item]
        high = rows.astype(BF16)
        rest = rows - high.astype(F32)
        middle = rest.astype(BF16)
        low = (rest - middle.astype(F32)).astype(BF16)
        order = order_ref[...]
        moved = mm(high, order) + mm(middle, order) + mm(low, order)
        for q in range(4):
            lanes = slice(q * QUARTER, (q + 1) * QUARTER)
            columns[q] = moved[:, lanes]
            for p in range(4):
                amps_ref[item, p * QUARTER : (p + 1) * QUARTER, lanes] = columns[
                    q, pl.ds(p, QUARTER, stride=4), :
                ]
    own = own_ref[0] ** 2 + own_ref[1] ** 2
    beam = probe_ref[0] ** 2 + probe_ref[1] ** 2
    peaks_ref[0] = jnp.full((8, 128), jnp.max(own), F32)
    peaks_ref[1] = jnp.full((8, 128), jnp.max(beam), F32)


def update_kernel(
    where_ref, own_ref, right_ref, *refs
):
    below_refs, diag_refs = refs[:PIECES], refs[PIECES : 2 * PIECES]
    rolled_ref, amps_ref, lh_ref, ll_ref, mh_ref, ml_ref = refs[2 * PIECES : 2 * PIECES + 6]
    outs = refs[2 * PIECES + 6 :]
    t_own_ref, t_right_ref = outs[:2]
    t_below_refs, t_diag_refs = outs[2 : 2 + PIECES], outs[2 + PIECES : 2 + 2 * PIECES]
    keep_ref, send_ref = outs[2 + 2 * PIECES : 4 + 2 * PIECES]
    wrapped, high, low, spec, grad = outs[4 + 2 * PIECES :]
    core = where_ref[2, 0]

    lane = lax.broadcasted_iota(jnp.int32, (PIECE, SIDE), 1)
    for piece in range(PIECES):
        at = slice(piece * PIECE, (piece + 1) * PIECE)
        row = lax.broadcasted_iota(jnp.int32, (PIECE, SIDE), 0) + piece * PIECE
        for item in range(2):
            down, along = where_ref[0, item], where_ref[1, item]
            above, beside = row < down, lane < along
            value = []
            for part in range(2):
                lower = jnp.where(beside, diag_refs[piece][part], below_refs[piece][part])
                upper = jnp.where(beside, right_ref[part, at, :], own_ref[part, at, :])
                value.append(jnp.where(above, lower, upper))
                wrapped[item, part, at, :] = value[part]
            beam_r, beam_i = rolled_ref[item, 0, at, :], rolled_ref[item, 1, at, :]
            psi_r = beam_r * value[0] - beam_i * value[1]
            psi_i = beam_r * value[1] + beam_i * value[0]
            blocks = [
                (psi_r[:, q * QUARTER : (q + 1) * QUARTER], psi_i[:, q * QUARTER : (q + 1) * QUARTER])
                for q in range(4)
            ]
            for p, (br, bi) in enumerate(fold(blocks, -1)):
                hi, lo = split(jnp.concatenate([br, bi], axis=1))
                out = mm(hi, mh_ref[p]) + mm(lo, mh_ref[p]) + mm(hi, ml_ref[p])
                spec[item, 0, at, p * QUARTER : (p + 1) * QUARTER] = out[:, :QUARTER]
                spec[item, 1, at, p * QUARTER : (p + 1) * QUARTER] = out[:, QUARTER:]

    wide = 2 * QUARTER
    for item in range(2):
        for chunk in range(SIDE // wide):
            cols = slice(chunk * wide, (chunk + 1) * wide)
            blocks = [
                (
                    spec[item, 0, q * QUARTER : (q + 1) * QUARTER, cols],
                    spec[item, 1, q * QUARTER : (q + 1) * QUARTER, cols],
                )
                for q in range(4)
            ]
            back = []
            for p, (br, bi) in enumerate(fold(blocks, -1)):
                hi, lo = split(jnp.concatenate([br, bi], axis=0))
                out = mm(lh_ref[p], hi) + mm(lh_ref[p], lo) + mm(ll_ref[p], hi)
                sr, si = out[:QUARTER], out[QUARTER:]
                factor = amps_ref[item, p * QUARTER : (p + 1) * QUARTER, cols] * lax.rsqrt(
                    sr * sr + si * si + 0.25
                )
                hi, lo = split(jnp.concatenate([sr * factor, si * factor], axis=0))
                out = mm(mh_ref[p], hi) + mm(mh_ref[p], lo) + mm(ml_ref[p], hi)
                back.append((out[:QUARTER], out[QUARTER:]))
            for q, (xr, xi) in enumerate(fold(back, 1)):
                rows = slice(q * QUARTER, (q + 1) * QUARTER)
                for part, value in enumerate((xr, xi)):
                    hi, lo = split(value)
                    for half in range(2):
                        p = 2 * chunk + half
                        to = slice(p * wide + part * QUARTER, p * wide + (part + 1) * QUARTER)
                        piece = slice(half * QUARTER, (half + 1) * QUARTER)
                        high[item, rows, to] = hi[:, piece]
                        low[item, rows, to] = lo[:, piece]

    for piece in range(PIECES):
        at = slice(piece * PIECE, (piece + 1) * PIECE)
        row = lax.broadcasted_iota(jnp.int32, (PIECE, SIDE), 0) + piece * PIECE
        for item in range(2):
            down, along = where_ref[0, item], where_ref[1, item]
            above, beside = row < down, lane < along
            back = []
            for p in range(4):
                cols = slice(p * wide, (p + 1) * wide)
                hi, lo = high[item, at, cols], low[item, at, cols]
                out = mm(hi, lh_ref[p]) + mm(lo, lh_ref[p]) + mm(hi, ll_ref[p])
                back.append((out[:, :QUARTER], out[:, QUARTER:]))
            back = fold(back, 1)
            back_r = jnp.concatenate([b[0] for b in back], axis=1)
            back_i = jnp.concatenate([b[1] for b in back], axis=1)
            beam_r, beam_i = rolled_ref[item, 0, at, :], rolled_ref[item, 1, at, :]
            patch_r, patch_i = wrapped[item, 0, at, :], wrapped[item, 1, at, :]
            diff_r = back_r - (beam_r * patch_r - beam_i * patch_i)
            diff_i = back_i - (beam_r * patch_i + beam_i * patch_r)
            term = (beam_r * diff_r + beam_i * diff_i, beam_r * diff_i - beam_i * diff_r)
            grad[item, 0, at, :] = patch_r * diff_r + patch_i * diff_i
            grad[item, 1, at, :] = patch_r * diff_i - patch_i * diff_r
            for part in range(2):
                zero = jnp.zeros_like(term[part])
                upper = jnp.where(above, zero, term[part])
                lower = jnp.where(above, term[part], zero)
                four = (
                    (t_own_ref, (part, at), jnp.where(beside, zero, upper)),
                    (t_right_ref, (part, at), jnp.where(beside, upper, zero)),
                    (t_below_refs[piece], (part,), jnp.where(beside, zero, lower)),
                    (t_diag_refs[piece], (part,), jnp.where(beside, lower, zero)),
                )
                for ref, index, value in four:
                    if item == 0:
                        ref[index] = value
                    else:
                        ref[index] += value
    whole = []
    for part in range(2):
        total = None
        for item in range(2):
            down, along = where_ref[0, item], where_ref[1, item]
            value = pltpu.roll(grad[item, part], (SIDE - down) % SIDE, 0)
            value = pltpu.roll(value, (SIDE - along) % SIDE, 1)
            total = value if total is None else total + value
        whole.append(total)
    keep_ref[...] = jnp.where(core == 0, whole[0], whole[1])
    send_ref[...] = jnp.where(core == 0, whole[1], whole[0])


def vm():
    return pl.BlockSpec(memory_space=pltpu.VMEM)


def sm():
    return pl.BlockSpec(memory_space=pltpu.SMEM)


def params():
    return pltpu.CompilerParams(vmem_limit_bytes=VMEM_LIMIT)


def ready(where, probe, own, amplitudes):
    return pl.pallas_call(
        ready_kernel,
        out_shape=(
            jax.ShapeDtypeStruct((2, 2, SIDE, SIDE), F32),
            jax.ShapeDtypeStruct((2, SIDE, SIDE), F32),
            jax.ShapeDtypeStruct((2, 8, 128), F32),
        ),
        in_specs=[sm()] + [vm()] * 4,
        out_specs=(vm(), vm(), vm()),
        scratch_shapes=[pltpu.VMEM((4, SIDE, QUARTER), F32)],
        compiler_params=params(),
        cost_estimate=pl.CostEstimate(flops=4 * 10**9, bytes_accessed=14 * 2**20, transcendentals=0),
    )(where, probe, own, amplitudes, jnp.asarray(order_matrix()))


def update(where, own, right, below, diag, rolled, amps):
    full = jax.ShapeDtypeStruct((2, SIDE, SIDE), F32)
    part = jax.ShapeDtypeStruct((2, PIECE, SIDE), F32)
    plane = jax.ShapeDtypeStruct((SIDE, SIDE), F32)
    matrices = [jnp.asarray(m) for m in split_matrices()]
    count = 2 + 2 * PIECES + 6
    out_shape = (full, full) + (part,) * (2 * PIECES) + (plane, plane)
    outs = pl.pallas_call(
        update_kernel,
        out_shape=out_shape,
        in_specs=[sm()] + [vm()] * count,
        out_specs=(vm(),) * len(out_shape),
        scratch_shapes=[
            pltpu.VMEM((2, 2, SIDE, SIDE), F32),
            pltpu.VMEM((2, SIDE, 2 * SIDE), BF16),
            pltpu.VMEM((2, SIDE, 2 * SIDE), BF16),
            pltpu.VMEM((2, 2, SIDE, SIDE), F32),
            pltpu.VMEM((2, 2, SIDE, SIDE), F32),
        ],
        compiler_params=params(),
        cost_estimate=pl.CostEstimate(
            flops=7 * 10**9, bytes_accessed=26 * 2**20, transcendentals=2 * SIDE * SIDE
        ),
    )(where, own, right, *below, *diag, rolled, amps, *matrices)
    return outs[0], outs[1], outs[2 : 2 + PIECES], outs[2 + PIECES : 2 + 2 * PIECES], outs[-2], outs[-1]


def passed_along(value, axis, steps):
    count = lax.axis_size(axis)
    first, last = (max(0, -steps), min(count, count - steps))
    return lax.ppermute(value, axis, [(source, source + steps) for source in range(first, last)])


def turned(value, steps):
    return lax.ppermute(value, "row", [(s, (s + steps) % 16) for s in range(16)])


def along_z(value, steps):
    return lax.ppermute(value, "col", [(c, (c // 2 + steps) % 4 * 2 + c % 2) for c in range(8)])


def other_core(value):
    return lax.ppermute(value, "col", [(c, c ^ 1) for c in range(8)])


def largest(value):
    value = jnp.maximum(value, other_core(value))
    for swap in (2, 4):
        value = jnp.maximum(value, lax.ppermute(value, "col", [(c, c ^ swap) for c in range(8)]))
    for swap in (1, 2, 4, 8):
        value = jnp.maximum(value, lax.ppermute(value, "row", [(r, r ^ swap) for r in range(16)]))
    return value


def on_device(object_field, probe, amplitudes, positions):
    row, col = lax.axis_index("row"), lax.axis_index("col")
    core = col % 2
    where = jnp.stack(
        [positions[:, 0] - row * SIDE, positions[:, 1] - col * SIDE, jnp.stack([core, row]).astype(jnp.int32)]
    )
    rolled, amps, peaks = ready(where, probe, object_field, amplitudes)
    object_peak = largest(peaks[0])[0, 0]
    probe_peak = peaks[1, 0, 0]

    right = passed_along(object_field, "col", -1)
    below = [
        passed_along(object_field[:, k * PIECE : (k + 1) * PIECE], "row", -1) for k in range(PIECES)
    ]
    diag = [passed_along(b, "col", -1) for b in below]
    t_own, t_right, t_below, t_diag, keep, send = update(
        where, object_field, right, below, diag, rolled, amps
    )

    lower = [t + passed_along(d, "col", 1) for t, d in zip(t_below, t_diag)]
    from_above = [passed_along(t, "row", 1) for t in lower]
    from_left = passed_along(t_right, "col", 1)
    scale = 0.9 / (probe_peak + 1e-06)
    new_object = object_field + scale * (t_own + from_left + jnp.concatenate(from_above, axis=1))

    half = keep + other_core(send)
    share = SIDE // 16
    mine = lax.dynamic_slice(half, (row * share, 0), (share, SIDE))
    for step in range(1, 16):
        piece = lax.dynamic_slice(half, ((row + step) % 16 * share, 0), (share, SIDE))
        mine = mine + turned(piece, step)
    mine = (mine + along_z(mine, 2)) + (along_z(mine, 1) + along_z(mine, -1))
    gathered = jnp.zeros((SIDE, SIDE), F32)
    gathered = lax.dynamic_update_slice(gathered, mine, (row * share, 0))
    for step in range(1, 16):
        gathered = lax.dynamic_update_slice(gathered, turned(mine, step), ((row - step) % 16 * share, 0))
    other = other_core(gathered)
    gradient = jnp.where(core == 0, jnp.stack([gathered, other]), jnp.stack([other, gathered]))
    new_probe = probe + 0.5 * gradient / (object_peak + 1e-06)
    return (new_object, new_probe)


def solution(mesh):
    in_specs = (P(None, "row", "col"), P(), P(("row", "col"), None, None), P(("row", "col"), None))
    out_specs = (P(None, "row", "col"), P())
    return jax.shard_map(
        on_device, mesh=mesh, in_specs=in_specs, out_specs=out_specs, check_vma=False
    )
```

```python
import functools
import math

import jax
import jax.numpy as jnp
import numpy as np
from jax import lax
from jax.experimental import pallas as pl
from jax.experimental.pallas import tpu as pltpu
from jax.sharding import PartitionSpec as P

SIDE = 512
QUARTER = 128
PIECES = 4
PIECE = SIDE // PIECES
BACK = (96, 128, 288)
CHUNKS = ((0, 96, 0, 0), (96, 128, 1, 0), (224, 144, 2, 0), (368, 144, 2, 144))
VMEM_LIMIT = 60 * 1024 * 1024
F32 = jnp.float32
BF16 = jnp.bfloat16


def split_matrices():
    k = np.arange(QUARTER)[:, None]
    n = np.arange(QUARTER)[None, :]
    parts = []
    for p in range(4):
        angle = 2.0 * np.pi * (((4 * k + p) * n) % SIDE) / SIDE
        re, im = np.cos(angle) / np.sqrt(SIDE), -np.sin(angle) / np.sqrt(SIDE)
        parts.append(np.block([[re, -im], [im, re]]))
    left = np.stack(parts)
    out = []
    for matrix in (left, np.swapaxes(left, 1, 2)):
        high = matrix.astype(np.float32).astype(jnp.bfloat16)
        low = (matrix - high.astype(np.float64)).astype(np.float32).astype(jnp.bfloat16)
        out += [np.ascontiguousarray(high), np.ascontiguousarray(low)]
    return out


def order_matrix():
    at = np.arange(SIDE)
    matrix = np.zeros((SIDE, SIDE), np.float32)
    matrix[at, (at % 4) * QUARTER + at // 4] = 1.0
    return matrix.astype(jnp.bfloat16)


def split(value):
    high = value.astype(BF16)
    return high, (value - high.astype(F32)).astype(BF16)


def mm(left, right):
    return jnp.dot(left, right, preferred_element_type=F32)


def fold(x, sign):
    (r0, i0), (r1, i1), (r2, i2), (r3, i3) = x
    sr, si, dr, di = r0 + r2, i0 + i2, r0 - r2, i0 - i2
    tr, ti, er, ei = r1 + r3, i1 + i3, r1 - r3, i1 - i3
    first = (dr + ei, di - er)
    second = (dr - ei, di + er)
    if sign > 0:
        first, second = second, first
    return [(sr + tr, si + ti), first, (sr - tr, si - ti), second]


def ready_kernel(
    where_ref, probe_ref, own_ref, amp_ref, order_ref, rolled_ref, amps_ref, peaks_ref, columns
):
    for item in range(2):
        down, along = where_ref[0, item], where_ref[1, item]
        for part in range(2):
            value = pltpu.roll(probe_ref[part], down, 0)
            rolled_ref[item, part] = pltpu.roll(value, along, 1)
        rows = amp_ref[item]
        high = rows.astype(BF16)
        rest = rows - high.astype(F32)
        middle = rest.astype(BF16)
        low = (rest - middle.astype(F32)).astype(BF16)
        order = order_ref[...]
        moved = mm(high, order) + mm(middle, order) + mm(low, order)
        for q in range(4):
            lanes = slice(q * QUARTER, (q + 1) * QUARTER)
            columns[q] = moved[:, lanes]
            for p in range(4):
                amps_ref[item, p * QUARTER : (p + 1) * QUARTER, lanes] = columns[
                    q, pl.ds(p, QUARTER, stride=4), :
                ]
    own = own_ref[0] ** 2 + own_ref[1] ** 2
    beam = probe_ref[0] ** 2 + probe_ref[1] ** 2
    peaks_ref[0] = jnp.full((8, 128), jnp.max(own), F32)
    peaks_ref[1] = jnp.full((8, 128), jnp.max(beam), F32)


def fore_kernel(
    piece, where_ref, own_ref, right_ref, below_ref, diag_ref, rolled_ref, mh_ref, ml_ref, *refs
):
    spec_ref, wrapped_ref = refs[-3:-1] if len(refs) == 4 else refs[-2:]
    lane = lax.broadcasted_iota(jnp.int32, (PIECE, SIDE), 1)
    row = lax.broadcasted_iota(jnp.int32, (PIECE, SIDE), 0) + piece * PIECE
    for item in range(2):
        down, along = where_ref[0, item], where_ref[1, item]
        above, beside = row < down, lane < along
        value = []
        for part in range(2):
            lower = jnp.where(beside, diag_ref[part], below_ref[part])
            upper = jnp.where(beside, right_ref[part], own_ref[part])
            value.append(jnp.where(above, lower, upper))
            wrapped_ref[item, part] = value[part]
        beam_r, beam_i = rolled_ref[item, 0], rolled_ref[item, 1]
        psi_r = beam_r * value[0] - beam_i * value[1]
        psi_i = beam_r * value[1] + beam_i * value[0]
        blocks = [
            (psi_r[:, q * QUARTER : (q + 1) * QUARTER], psi_i[:, q * QUARTER : (q + 1) * QUARTER])
            for q in range(4)
        ]
        for p, (br, bi) in enumerate(fold(blocks, -1)):
            hi, lo = split(jnp.concatenate([br, bi], axis=1))
            out = mm(hi, mh_ref[p]) + mm(lo, mh_ref[p]) + mm(hi, ml_ref[p])
            spec_ref[item, 0, :, p * QUARTER : (p + 1) * QUARTER] = out[:, :QUARTER]
            spec_ref[item, 1, :, p * QUARTER : (p + 1) * QUARTER] = out[:, QUARTER:]


def fore(piece, where, own, right, below, diag, rolled, matrices, held=None, after=None):
    def rows(*lead):
        zeros = (0,) * len(lead)
        return pl.BlockSpec(lead + (PIECE, SIDE), lambda i: zeros + (piece, 0))

    full = pl.BlockSpec((2, PIECE, SIDE), lambda i: (0, 0, 0))
    whole = pl.BlockSpec((4, 2 * QUARTER, 2 * QUARTER), lambda i: (0, 0, 0))
    four = pl.BlockSpec((2, 2, PIECE, SIDE), lambda i: (0, 0, 0, 0))
    shape = jax.ShapeDtypeStruct((2, 2, PIECE, SIDE), F32)
    operands = [where, own, right, below, diag, rolled, *matrices[2:]]
    in_specs = [sm(), rows(2), rows(2), full, full, rows(2, 2), whole, whole]
    out_shape, out_specs, aliases = [shape, shape], [four, four], {}
    if held is not None:
        aliases = {len(operands): 2}
        operands.append(held)
        in_specs.append(anywhere())
        out_shape.append(jax.ShapeDtypeStruct(held.shape, F32))
        out_specs.append(anywhere())
    if after is not None:
        operands.append(after)
        in_specs.append(anywhere())
    return pl.pallas_call(
        functools.partial(fore_kernel, piece),
        grid=(1,),
        out_shape=out_shape,
        in_specs=in_specs,
        out_specs=out_specs,
        input_output_aliases=aliases,
        compiler_params=params(),
        cost_estimate=pl.CostEstimate(
            flops=4 * 10**8, bytes_accessed=6 * 2**20, transcendentals=0
        ),
    )(*operands)


def update_kernel(where_ref, *refs):
    spec_refs = refs[:PIECES]
    wrapped_hbm = refs[PIECES : 2 * PIECES]
    rolled_hbm, amps_ref, lh_ref, ll_ref, mh_ref, ml_ref = refs[2 * PIECES : 2 * PIECES + 6]
    outs = refs[2 * PIECES + 6 :]
    t_own_ref, t_right_ref = outs[:2]
    count = len(BACK)
    t_below_refs, t_diag_refs = outs[2 : 2 + count], outs[2 + count : 2 + 2 * count]
    keep_ref, send_ref = outs[2 + 2 * count : 4 + 2 * count]
    wrapped, rolled_ref, high, low, grad, sems = outs[4 + 2 * count :]
    core = where_ref[2, 0]
    loads = [
        pltpu.make_async_copy(wrapped_hbm[k], wrapped.at[:, :, k * PIECE : (k + 1) * PIECE], sems.at[k])
        for k in range(PIECES)
    ] + [pltpu.make_async_copy(rolled_hbm, rolled_ref, sems.at[PIECES])]
    for load in loads:
        load.start()

    wide = 2 * QUARTER
    for item in range(2):
        for chunk in range(SIDE // wide):
            cols = slice(chunk * wide, (chunk + 1) * wide)
            blocks = [
                (spec_refs[q][item, 0, :, cols], spec_refs[q][item, 1, :, cols]) for q in range(4)
            ]
            back = []
            for p, (br, bi) in enumerate(fold(blocks, -1)):
                hi, lo = split(jnp.concatenate([br, bi], axis=0))
                out = mm(lh_ref[p], hi) + mm(lh_ref[p], lo) + mm(ll_ref[p], hi)
                sr, si = out[:QUARTER], out[QUARTER:]
                factor = amps_ref[item, p * QUARTER : (p + 1) * QUARTER, cols] * lax.rsqrt(
                    sr * sr + si * si + 0.25
                )
                hi, lo = split(jnp.concatenate([sr * factor, si * factor], axis=0))
                out = mm(mh_ref[p], hi) + mm(mh_ref[p], lo) + mm(ml_ref[p], hi)
                back.append((out[:QUARTER], out[QUARTER:]))
            for q, (xr, xi) in enumerate(fold(back, 1)):
                rows = slice(q * QUARTER, (q + 1) * QUARTER)
                for part, value in enumerate((xr, xi)):
                    hi, lo = split(value)
                    for half in range(2):
                        p = 2 * chunk + half
                        to = slice(p * wide + part * QUARTER, p * wide + (part + 1) * QUARTER)
                        piece = slice(half * QUARTER, (half + 1) * QUARTER)
                        high[item, rows, to] = hi[:, piece]
                        low[item, rows, to] = lo[:, piece]

    for load in loads:
        load.wait()
    for first, size, piece, inside in CHUNKS:
        at, within = slice(first, first + size), slice(inside, inside + size)
        lane = lax.broadcasted_iota(jnp.int32, (size, SIDE), 1)
        row = lax.broadcasted_iota(jnp.int32, (size, SIDE), 0) + first
        for item in range(2):
            down, along = where_ref[0, item], where_ref[1, item]
            above, beside = row < down, lane < along
            back = []
            for p in range(4):
                cols = slice(p * wide, (p + 1) * wide)
                hi, lo = high[item, at, cols], low[item, at, cols]
                out = mm(hi, lh_ref[p]) + mm(lo, lh_ref[p]) + mm(hi, ll_ref[p])
                back.append((out[:, :QUARTER], out[:, QUARTER:]))
            back = fold(back, 1)
            back_r = jnp.concatenate([b[0] for b in back], axis=1)
            back_i = jnp.concatenate([b[1] for b in back], axis=1)
            beam_r, beam_i = rolled_ref[item, 0, at, :], rolled_ref[item, 1, at, :]
            patch_r, patch_i = wrapped[item, 0, at, :], wrapped[item, 1, at, :]
            diff_r = back_r - (beam_r * patch_r - beam_i * patch_i)
            diff_i = back_i - (beam_r * patch_i + beam_i * patch_r)
            term = (beam_r * diff_r + beam_i * diff_i, beam_r * diff_i - beam_i * diff_r)
            grad[item, 0, at, :] = patch_r * diff_r + patch_i * diff_i
            grad[item, 1, at, :] = patch_r * diff_i - patch_i * diff_r
            for part in range(2):
                zero = jnp.zeros_like(term[part])
                upper = jnp.where(above, zero, term[part])
                lower = jnp.where(above, term[part], zero)
                four = (
                    (t_own_ref, (part, at), jnp.where(beside, zero, upper)),
                    (t_right_ref, (part, at), jnp.where(beside, upper, zero)),
                    (t_below_refs[piece], (part, within), jnp.where(beside, zero, lower)),
                    (t_diag_refs[piece], (part, within), jnp.where(beside, lower, zero)),
                )
                for ref, index, value in four:
                    if item == 0:
                        ref[index] = value
                    else:
                        ref[index] += value
    whole = []
    for part in range(2):
        total = None
        for item in range(2):
            down, along = where_ref[0, item], where_ref[1, item]
            value = pltpu.roll(grad[item, part], (SIDE - down) % SIDE, 0)
            value = pltpu.roll(value, (SIDE - along) % SIDE, 1)
            total = value if total is None else total + value
        whole.append(total)
    keep_ref[...] = jnp.where(core == 0, whole[0], whole[1])
    send_ref[...] = jnp.where(core == 0, whole[1], whole[0])


def vm():
    return pl.BlockSpec(memory_space=pltpu.VMEM)


def sm():
    return pl.BlockSpec(memory_space=pltpu.SMEM)


def anywhere():
    return pl.BlockSpec(memory_space=pl.ANY)


def params():
    return pltpu.CompilerParams(vmem_limit_bytes=VMEM_LIMIT)


def ready(where, probe, own, amplitudes):
    return pl.pallas_call(
        ready_kernel,
        out_shape=(
            jax.ShapeDtypeStruct((2, 2, SIDE, SIDE), F32),
            jax.ShapeDtypeStruct((2, SIDE, SIDE), F32),
            jax.ShapeDtypeStruct((2, 8, 128), F32),
        ),
        in_specs=[sm()] + [vm()] * 4,
        out_specs=(vm(), vm(), vm()),
        scratch_shapes=[pltpu.VMEM((4, SIDE, QUARTER), F32)],
        compiler_params=params(),
        cost_estimate=pl.CostEstimate(flops=4 * 10**9, bytes_accessed=14 * 2**20, transcendentals=0),
    )(where, probe, own, amplitudes, jnp.asarray(order_matrix()))


def update(where, specs, wrapped, rolled, amps, matrices):
    full = jax.ShapeDtypeStruct((2, SIDE, SIDE), F32)
    parts = tuple(jax.ShapeDtypeStruct((2, size, SIDE), F32) for size in BACK)
    plane = jax.ShapeDtypeStruct((SIDE, SIDE), F32)
    out_shape = (full, full) + parts + parts + (plane, plane)
    count = len(BACK)
    outs = pl.pallas_call(
        update_kernel,
        out_shape=out_shape,
        in_specs=[sm()] + [vm()] * PIECES + [anywhere()] * (PIECES + 1) + [vm()] * 5,
        out_specs=(vm(),) * len(out_shape),
        scratch_shapes=[
            pltpu.VMEM((2, 2, SIDE, SIDE), F32),
            pltpu.VMEM((2, 2, SIDE, SIDE), F32),
            pltpu.VMEM((2, SIDE, 2 * SIDE), BF16),
            pltpu.VMEM((2, SIDE, 2 * SIDE), BF16),
            pltpu.VMEM((2, 2, SIDE, SIDE), F32),
            pltpu.SemaphoreType.DMA((PIECES + 1,)),
        ],
        compiler_params=params(),
        cost_estimate=pl.CostEstimate(
            flops=5 * 10**9, bytes_accessed=26 * 2**20, transcendentals=2 * SIDE * SIDE
        ),
    )(where, *specs, *wrapped, rolled, amps, *matrices)
    return outs[0], outs[1], outs[2 : 2 + count], outs[2 + count : 2 + 2 * count], outs[-2], outs[-1]


def nothing_kernel(*refs):
    del refs


def tied(values, after):
    count = len(values) + len(after)
    return pl.pallas_call(
        nothing_kernel,
        out_shape=[jax.ShapeDtypeStruct(v.shape, v.dtype) for v in values],
        in_specs=[anywhere()] * count,
        out_specs=[anywhere()] * len(values),
        input_output_aliases={k: k for k in range(len(values))},
    )(*values, *after)


def first_kernel(keep_ref, came_ref, below_ref, diag_ref, half_ref, lower_ref):
    half_ref[...] = keep_ref[...] + came_ref[...]
    lower_ref[...] = below_ref[...] + diag_ref[...]


def first_sums(keep, came, below, diag):
    return pl.pallas_call(
        first_kernel,
        out_shape=[jax.ShapeDtypeStruct(keep.shape, F32), jax.ShapeDtypeStruct(below.shape, F32)],
        in_specs=[vm()] * 4,
        out_specs=[vm()] * 2,
        compiler_params=params(),
        cost_estimate=pl.CostEstimate(flops=2 * keep.size, bytes_accessed=18 * keep.size, transcendentals=0),
    )(keep, came, below, diag)


def share_kernel(peak_ref, terms_ref, start_ref, below_ref, corner_ref, *refs):
    out_ref, lower_ref = refs[-2:]
    lower_ref[...] = below_ref[...] + corner_ref[...]
    total = jnp.sum(terms_ref[...], axis=0)
    value = start_ref[...] + 0.5 * total / (peak_ref[0, 0] + 1e-06)
    out_ref[...] = jnp.broadcast_to(value, out_ref.shape)


def shared(peak, terms, start, below, corner, after):
    return pl.pallas_call(
        share_kernel,
        out_shape=[jax.ShapeDtypeStruct(terms.shape, F32), jax.ShapeDtypeStruct(below.shape, F32)],
        in_specs=[sm()] + [vm()] * 4 + [anywhere()] * len(after),
        out_specs=[vm(), vm()],
        compiler_params=params(),
        cost_estimate=pl.CostEstimate(flops=2 * terms.size, bytes_accessed=20 * terms.size, transcendentals=0),
    )(peak, terms, start, below, corner, *after)


def shifted(value, axis, steps):
    count = lax.axis_size(axis)
    first, last = (max(0, -steps), min(count, count - steps))
    return lax.ppermute(value, axis, [(source, source + steps) for source in range(first, last)])


def other_core(value):
    return lax.ppermute(value, "core", [(0, 1), (1, 0)])


def largest(value):
    spread = jnp.broadcast_to(value[:1][None], (64, 1, QUARTER))
    value = jnp.max(lax.all_to_all(spread, CHIPS, 0, 0), axis=0)
    return jnp.maximum(value, other_core(value))


def base_kernel(scale_ref, own_ref, t_own_ref, base_ref):
    base_ref[...] = own_ref[...] + scale_ref[0, 0] * t_own_ref[...]


def base(scale, own, t_own):
    return pl.pallas_call(
        base_kernel,
        out_shape=jax.ShapeDtypeStruct(own.shape, F32),
        in_specs=[sm(), vm(), vm()],
        out_specs=vm(),
        compiler_params=params(),
        cost_estimate=pl.CostEstimate(flops=2 * own.size, bytes_accessed=12 * own.size, transcendentals=0),
    )(scale, own, t_own)


def object_kernel(scale_ref, base_ref, left_ref, *refs):
    out_ref = refs[-1]
    first = 0
    for ref, size in zip(refs, BACK):
        at = slice(first, first + size)
        out_ref[:, at, :] = base_ref[:, at, :] + scale_ref[0, 0] * (left_ref[:, at, :] + ref[...])
        first += size


def finished_object(scale, start, left, above):
    return pl.pallas_call(
        object_kernel,
        out_shape=jax.ShapeDtypeStruct(start.shape, F32),
        in_specs=[sm(), vm(), vm()] + [vm()] * len(above),
        out_specs=vm(),
        compiler_params=params(),
        cost_estimate=pl.CostEstimate(flops=3 * start.size, bytes_accessed=16 * start.size, transcendentals=0),
    )(scale, start, left, *above)


def probe_kernel(core_ref, mine_ref, other_ref, out_ref):
    core = core_ref[0, 0]
    out_ref[core] = mine_ref[...]
    out_ref[1 - core] = other_ref[...]


def joined(core, mine, other):
    return pl.pallas_call(
        probe_kernel,
        out_shape=jax.ShapeDtypeStruct((2, SIDE, SIDE), F32),
        in_specs=[sm(), vm(), vm()],
        out_specs=vm(),
        compiler_params=params(),
        cost_estimate=pl.CostEstimate(flops=0, bytes_accessed=16 * SIDE * SIDE, transcendentals=0),
    )(core, mine, other)


def on_device(object_field, probe, amplitudes, positions):
    row, col, core = lax.axis_index(ROW), lax.axis_index(COL), lax.axis_index("core")
    where = jnp.stack(
        [positions[:, 0] - row * SIDE, positions[:, 1] - col * SIDE, jnp.stack([core, row]).astype(jnp.int32)]
    )
    matrices = [jnp.asarray(m) for m in split_matrices()]
    pieces = [object_field[:, k * PIECE : (k + 1) * PIECE] for k in range(PIECES)]
    below, diag, specs, wrapped = [None] * 4, [None] * 4, [None] * 4, [None] * 4
    below[0] = shifted(pieces[0], ROW, -1)
    below[1] = shifted(pieces[1], ROW, -1)
    right = shifted(object_field, COL, -1)
    rolled, amps, peaks = ready(where, probe, object_field, amplitudes)
    scale = 0.9 / (peaks[1, :1, :1] + 1e-06)
    below[0], pieces[2] = tied((below[0], pieces[2]), (rolled,))
    diag[0] = shifted(below[0], COL, -1)
    below[2] = shifted(pieces[2], ROW, -1)
    object_peak = largest(peaks[0])
    below[1], pieces[3] = tied((below[1], pieces[3]), (pieces[2], object_peak))
    diag[1] = shifted(below[1], COL, -1)
    below[3] = shifted(pieces[3], ROW, -1)
    specs[0], wrapped[0], below[2] = fore(
        0, where, object_field, right, below[0], diag[0], rolled, matrices, held=below[2]
    )
    diag[2] = shifted(below[2], COL, -1)
    diag[3] = shifted(below[3], COL, -1)
    for k in range(1, PIECES):
        specs[k], wrapped[k] = fore(
            k, where, object_field, right, below[k], diag[k], rolled, matrices
        )
    t_own, t_right, t_below, t_diag, keep, send = update(where, specs, wrapped, rolled, amps, matrices)

    came = other_core(send)
    corner = [shifted(t_diag[0], COL, 1)]
    half, lower = first_sums(keep, came, t_below[0], corner[0])
    share = SIDE // 64
    terms = lax.all_to_all(half.reshape(64, share, SIDE), CHIPS, 0, 0)
    from_above = [shifted(lower, ROW, 1)]
    later = tied((t_diag[1], t_diag[2]), (half,))
    corner += [shifted(t, COL, 1) for t in later]
    from_above.append(shifted(t_below[1] + corner[1], ROW, 1))
    at = lax.axis_index(CHIPS) * share
    start = lax.dynamic_slice(probe, (core, at, jnp.zeros_like(at)), (1, share, SIDE))[0]
    shares, lower = shared(object_peak[:, :1], terms, start, t_below[2], corner[2], from_above)
    mine = lax.all_to_all(shares, CHIPS, 0, 0).reshape(SIDE, SIDE)
    from_above.append(shifted(lower, ROW, 1))
    (t_right,) = tied((t_right,), (shares,))
    from_left = shifted(t_right, COL, 1)
    begun = base(scale, object_field, t_own)
    (mine,) = tied((mine,), (from_above[2], from_left, begun))
    new_probe = joined(core.astype(jnp.int32).reshape(1, 1), mine, other_core(mine))
    new_object = finished_object(scale, begun, from_left, from_above)
    return (new_object, new_probe)


CHIPS = ("y", "x", "z")
ROW = ("y", "x")
COL = ("z", "core")


def solution(mesh):
    chips = jax.sharding.Mesh(mesh.devices.reshape(4, 4, 4, 2), ROW + COL)
    in_specs = (P(None, ROW, COL), P(), P(ROW + COL, None, None), P(ROW + COL, None))
    out_specs = (P(None, ROW, COL), P())
    return jax.shard_map(
        on_device, mesh=chips, in_specs=in_specs, out_specs=out_specs, check_vma=False
    )
```

```python
import functools
import math

import jax
import jax.numpy as jnp
import numpy as np
from jax import lax
from jax.experimental import pallas as pl
from jax.experimental.pallas import tpu as pltpu
from jax.sharding import PartitionSpec as P

SIDE = 512
QUARTER = 128
PIECES = 4
PIECE = SIDE // PIECES
BACK = (96, 128, 288)
CHUNKS = ((0, 96, 0, 0), (96, 128, 1, 0), (224, 144, 2, 0), (368, 144, 2, 144))
WIDE = SIDE + 128
F32 = jnp.float32
BF16 = jnp.bfloat16


def split_matrices():
    k = np.arange(QUARTER)[:, None]
    n = np.arange(QUARTER)[None, :]
    parts = []
    for p in range(4):
        angle = 2.0 * np.pi * (((4 * k + p) * n) % SIDE) / SIDE
        re, im = np.cos(angle) / np.sqrt(SIDE), -np.sin(angle) / np.sqrt(SIDE)
        parts.append(np.block([[re, -im], [im, re]]))
    left = np.stack(parts)
    out = []
    for matrix in (left, np.swapaxes(left, 1, 2)):
        high = matrix.astype(np.float32).astype(jnp.bfloat16)
        low = (matrix - high.astype(np.float64)).astype(np.float32).astype(jnp.bfloat16)
        out += [np.ascontiguousarray(high), np.ascontiguousarray(low)]
    return out


def order_matrix():
    at = np.arange(SIDE)
    matrix = np.zeros((SIDE, SIDE), np.float32)
    matrix[at, (at % 4) * QUARTER + at // 4] = 1.0
    return matrix.astype(jnp.bfloat16)


def split(value):
    high = value.astype(BF16)
    return high, (value - high.astype(F32)).astype(BF16)


def mm(left, right):
    return jnp.dot(left, right, preferred_element_type=F32)


def fold(x, sign):
    (r0, i0), (r1, i1), (r2, i2), (r3, i3) = x
    sr, si, dr, di = r0 + r2, i0 + i2, r0 - r2, i0 - i2
    tr, ti, er, ei = r1 + r3, i1 + i3, r1 - r3, i1 - i3
    first = (dr + ei, di - er)
    second = (dr - ei, di + er)
    if sign > 0:
        first, second = second, first
    return [(sr + tr, si + ti), first, (sr - tr, si - ti), second]


def ready_kernel(
    where_ref, probe_ref, own_ref, amp_ref, order_ref, rolled_ref, amps_ref, peaks_ref, columns
):
    for item in range(2):
        down, along = where_ref[0, item], where_ref[1, item]
        for part in range(2):
            value = pltpu.roll(probe_ref[part], down, 0)
            rolled_ref[item, part] = pltpu.roll(value, along, 1)
        rows = amp_ref[item]
        high = rows.astype(BF16)
        rest = rows - high.astype(F32)
        middle = rest.astype(BF16)
        low = (rest - middle.astype(F32)).astype(BF16)
        order = order_ref[...]
        moved = mm(high, order) + mm(middle, order) + mm(low, order)
        for q in range(4):
            lanes = slice(q * QUARTER, (q + 1) * QUARTER)
            columns[q] = moved[:, lanes]
            for p in range(4):
                amps_ref[item, p * QUARTER : (p + 1) * QUARTER, lanes] = columns[
                    q, pl.ds(p, QUARTER, stride=4), :
                ]
    own = own_ref[0] ** 2 + own_ref[1] ** 2
    beam = probe_ref[0] ** 2 + probe_ref[1] ** 2
    peaks_ref[0] = jnp.full((8, 128), jnp.max(own), F32)
    peaks_ref[1] = jnp.full((8, 128), jnp.max(beam), F32)


def fore_kernel(
    piece, where_ref, own_ref, right_ref, below_ref, diag_ref, rolled_ref, mh_ref, ml_ref,
    spec_ref, wrapped_ref, token_ref,
):
    token_ref[...] = jnp.zeros_like(token_ref)
    lane = lax.broadcasted_iota(jnp.int32, (PIECE, SIDE), 1)
    row = lax.broadcasted_iota(jnp.int32, (PIECE, SIDE), 0) + piece * PIECE
    for item in range(2):
        down, along = where_ref[0, item], where_ref[1, item]
        above, beside = row < down, lane < along
        value = []
        for part in range(2):
            lower = jnp.where(beside, diag_ref[part], below_ref[part])
            upper = jnp.where(beside, right_ref[part], own_ref[part])
            value.append(jnp.where(above, lower, upper))
            wrapped_ref[item, part] = value[part]
        beam_r, beam_i = rolled_ref[item, 0], rolled_ref[item, 1]
        psi_r = beam_r * value[0] - beam_i * value[1]
        psi_i = beam_r * value[1] + beam_i * value[0]
        blocks = [
            (psi_r[:, q * QUARTER : (q + 1) * QUARTER], psi_i[:, q * QUARTER : (q + 1) * QUARTER])
            for q in range(4)
        ]
        for p, (br, bi) in enumerate(fold(blocks, -1)):
            hi, lo = split(jnp.concatenate([br, bi], axis=1))
            out = mm(hi, mh_ref[p]) + mm(lo, mh_ref[p]) + mm(hi, ml_ref[p])
            spec_ref[item, 0, :, p * QUARTER : (p + 1) * QUARTER] = out[:, :QUARTER]
            spec_ref[item, 1, :, p * QUARTER : (p + 1) * QUARTER] = out[:, QUARTER:]


def fore(piece, where, own, right, below, diag, rolled, matrices):
    def rows(*lead):
        zeros = (0,) * len(lead)
        return pl.BlockSpec(lead + (PIECE, SIDE), lambda i: zeros + (piece, 0))

    full = pl.BlockSpec((2, PIECE, SIDE), lambda i: (0, 0, 0))
    whole = pl.BlockSpec((4, 2 * QUARTER, 2 * QUARTER), lambda i: (0, 0, 0))
    four = pl.BlockSpec((2, 2, PIECE, SIDE), lambda i: (0, 0, 0, 0))
    shape = jax.ShapeDtypeStruct((2, 2, PIECE, SIDE), F32)
    return pl.pallas_call(
        functools.partial(fore_kernel, piece),
        grid=(1,),
        out_shape=[shape, shape, jax.ShapeDtypeStruct((8, 128), F32)],
        in_specs=[sm(), rows(2), rows(2), full, full, rows(2, 2), whole, whole],
        out_specs=[four, four, pl.BlockSpec((8, 128), lambda i: (0, 0))],
        compiler_params=params(20),
        cost_estimate=pl.CostEstimate(
            flops=4 * 10**8, bytes_accessed=6 * 2**20, transcendentals=0
        ),
    )(where, own, right, below, diag, rolled, *matrices[2:])


def update_kernel(where_ref, *refs):
    spec_refs = refs[:PIECES]
    wrapped_refs = refs[PIECES : 2 * PIECES]
    rolled_ref, amps_ref, peaks_ref, lh_ref, ll_ref, mh_ref, ml_ref = refs[2 * PIECES : 2 * PIECES + 7]
    outs = refs[2 * PIECES + 7 :]
    count = len(BACK)
    t_own_hbm, t_right_hbm = outs[:2]
    t_below_hbm, t_diag_hbm = outs[2 : 2 + count], outs[2 + count : 2 + 2 * count]
    keep_ref, send_ref = outs[2 + 2 * count : 4 + 2 * count]
    high, low, grad, terms, out_sems = outs[4 + 2 * count :]
    core = where_ref[2, 0]

    wide = 2 * QUARTER
    for item in range(2):
        for chunk in range(SIDE // wide):
            cols = slice(chunk * wide, (chunk + 1) * wide)
            blocks = [
                (spec_refs[q][item, 0, :, cols], spec_refs[q][item, 1, :, cols]) for q in range(4)
            ]
            back = []
            for p, (br, bi) in enumerate(fold(blocks, -1)):
                hi, lo = split(jnp.concatenate([br, bi], axis=0))
                out = mm(lh_ref[p], hi) + mm(lh_ref[p], lo) + mm(ll_ref[p], hi)
                sr, si = out[:QUARTER], out[QUARTER:]
                factor = amps_ref[item, p * QUARTER : (p + 1) * QUARTER, cols] * lax.rsqrt(
                    sr * sr + si * si + 0.25
                )
                hi, lo = split(jnp.concatenate([sr * factor, si * factor], axis=0))
                out = mm(mh_ref[p], hi) + mm(mh_ref[p], lo) + mm(ml_ref[p], hi)
                back.append((out[:QUARTER], out[QUARTER:]))
            for q, (xr, xi) in enumerate(fold(back, 1)):
                rows = slice(q * QUARTER, (q + 1) * QUARTER)
                for part, value in enumerate((xr, xi)):
                    hi, lo = split(value)
                    for half in range(2):
                        p = 2 * chunk + half
                        to = slice(p * wide + part * QUARTER, p * wide + (part + 1) * QUARTER)
                        piece = slice(half * QUARTER, (half + 1) * QUARTER)
                        high[item, rows, to] = hi[:, piece]
                        low[item, rows, to] = lo[:, piece]

    stores = []
    for first, size, piece, inside in CHUNKS:
        at, within = slice(first, first + size), slice(inside, inside + size)
        lane = lax.broadcasted_iota(jnp.int32, (size, SIDE), 1)
        row = lax.broadcasted_iota(jnp.int32, (size, SIDE), 0) + first
        for item in range(2):
            down, along = where_ref[0, item], where_ref[1, item]
            above, beside = row < down, lane < along
            back = []
            for p in range(4):
                cols = slice(p * wide, (p + 1) * wide)
                hi, lo = high[item, at, cols], low[item, at, cols]
                out = mm(hi, lh_ref[p]) + mm(lo, lh_ref[p]) + mm(hi, ll_ref[p])
                back.append((out[:, :QUARTER], out[:, QUARTER:]))
            back = fold(back, 1)
            back_r = jnp.concatenate([b[0] for b in back], axis=1)
            back_i = jnp.concatenate([b[1] for b in back], axis=1)
            beam_r, beam_i = rolled_ref[item, 0, at, :], rolled_ref[item, 1, at, :]
            patch = []
            for part in range(2):
                spans = [
                    (k, max(first, k * PIECE) - k * PIECE, min(first + size, (k + 1) * PIECE) - k * PIECE)
                    for k in range(PIECES)
                ]
                values = [wrapped_refs[k][item, part, lo:hi] for k, lo, hi in spans if lo < hi]
                patch.append(values[0] if len(values) == 1 else jnp.concatenate(values, axis=0))
            patch_r, patch_i = patch
            diff_r = back_r - (beam_r * patch_r - beam_i * patch_i)
            diff_i = back_i - (beam_r * patch_i + beam_i * patch_r)
            term = (beam_r * diff_r + beam_i * diff_i, beam_r * diff_i - beam_i * diff_r)
            grad[item, 0, at, :] = patch_r * diff_r + patch_i * diff_i
            grad[item, 1, at, :] = patch_r * diff_i - patch_i * diff_r
            for part in range(2):
                zero = jnp.zeros_like(term[part])
                upper = jnp.where(above, zero, term[part])
                lower = jnp.where(above, term[part], zero)
                four = (
                    jnp.where(beside, zero, upper),
                    jnp.where(beside, upper, zero),
                    jnp.where(beside, zero, lower),
                    jnp.where(beside, lower, zero),
                )
                for k, value in enumerate(four):
                    if item == 0:
                        terms[k, part, at] = value
                    else:
                        terms[k, part, at] += value
        targets = (
            t_own_hbm.at[:, at],
            t_right_hbm.at[:, at],
            t_below_hbm[piece].at[:, within],
            t_diag_hbm[piece].at[:, within],
        )
        for k, target in enumerate(targets):
            store = pltpu.make_async_copy(terms.at[k, :, at], target, out_sems.at[len(stores)])
            store.start()
            stores.append(store)
    whole = []
    for part in range(2):
        total = None
        for item in range(2):
            down, along = where_ref[0, item], where_ref[1, item]
            value = pltpu.roll(grad[item, part], (SIDE - down) % SIDE, 0)
            value = pltpu.roll(value, (SIDE - along) % SIDE, 1)
            total = value if total is None else total + value
        whole.append(total)
    keep_ref[:, :SIDE] = jnp.where(core == 0, whole[0], whole[1])
    send_ref[:, :SIDE] = jnp.where(core == 0, whole[1], whole[0])
    peak = jnp.broadcast_to(peaks_ref[0, :1, :], (SIDE, 128))
    keep_ref[:, SIDE:] = peak
    send_ref[:, SIDE:] = peak
    for store in stores:
        store.wait()


def vm():
    return pl.BlockSpec(memory_space=pltpu.VMEM)


def sm():
    return pl.BlockSpec(memory_space=pltpu.SMEM)


def anywhere():
    return pl.BlockSpec(memory_space=pl.ANY)


def params(mebibytes=16):
    return pltpu.CompilerParams(vmem_limit_bytes=mebibytes * 2**20)


def ready(where, probe, own, amplitudes):
    return pl.pallas_call(
        ready_kernel,
        out_shape=(
            jax.ShapeDtypeStruct((2, 2, SIDE, SIDE), F32),
            jax.ShapeDtypeStruct((2, SIDE, SIDE), F32),
            jax.ShapeDtypeStruct((2, 8, 128), F32),
        ),
        in_specs=[sm()] + [vm()] * 4,
        out_specs=(vm(),) * 3,
        scratch_shapes=[pltpu.VMEM((4, SIDE, QUARTER), F32)],
        compiler_params=params(32),
        cost_estimate=pl.CostEstimate(flops=4 * 10**9, bytes_accessed=14 * 2**20, transcendentals=0),
    )(where, probe, own, amplitudes, jnp.asarray(order_matrix()))


def update(where, specs, wrapped, rolled, amps, peaks, matrices):
    full = jax.ShapeDtypeStruct((2, SIDE, SIDE), F32)
    parts = tuple(jax.ShapeDtypeStruct((2, size, SIDE), F32) for size in BACK)
    plane = jax.ShapeDtypeStruct((SIDE, WIDE), F32)
    out_shape = (full, full) + parts + parts + (plane, plane)
    count = len(BACK)
    four = pltpu.VMEM((2, 2, SIDE, SIDE), F32)
    half = pltpu.VMEM((2, SIDE, 2 * SIDE), BF16)
    outs = pl.pallas_call(
        update_kernel,
        out_shape=out_shape,
        in_specs=[sm()] + [vm()] * (2 * PIECES + 7),
        out_specs=(anywhere(),) * (2 + 2 * count) + (vm(), vm()),
        scratch_shapes=[
            half,
            half,
            four,
            pltpu.VMEM((4, 2, SIDE, SIDE), F32),
            pltpu.SemaphoreType.DMA((4 * len(CHUNKS),)),
        ],
        compiler_params=params(36),
        cost_estimate=pl.CostEstimate(
            flops=5 * 10**9, bytes_accessed=26 * 2**20, transcendentals=2 * SIDE * SIDE
        ),
    )(where, *specs, *wrapped, rolled, amps, peaks, *matrices)
    return outs[0], outs[1], outs[2 : 2 + count], outs[2 + count : 2 + 2 * count], outs[-2], outs[-1]


def nothing_kernel(*refs):
    del refs


def tied(values, after):
    count = len(values) + len(after)
    return pl.pallas_call(
        nothing_kernel,
        out_shape=[jax.ShapeDtypeStruct(v.shape, v.dtype) for v in values],
        in_specs=[anywhere()] * count,
        out_specs=[anywhere()] * len(values),
        input_output_aliases={k: k for k in range(len(values))},
    )(*values, *after)


def first_kernel(keep_ref, came_ref, below_ref, diag_ref, half_ref, lower_ref):
    half_ref[:, :SIDE] = keep_ref[:, :SIDE] + came_ref[:, :SIDE]
    half_ref[:, SIDE:] = jnp.maximum(keep_ref[:, SIDE:], came_ref[:, SIDE:])
    lower_ref[...] = below_ref[...] + diag_ref[...]


def first_sums(keep, came, below, diag):
    return pl.pallas_call(
        first_kernel,
        out_shape=[jax.ShapeDtypeStruct(keep.shape, F32), jax.ShapeDtypeStruct(below.shape, F32)],
        in_specs=[vm()] * 4,
        out_specs=[vm()] * 2,
        compiler_params=params(),
        cost_estimate=pl.CostEstimate(flops=2 * keep.size, bytes_accessed=18 * keep.size, transcendentals=0),
    )(keep, came, below, diag)


def lower_kernel(below_ref, corner_ref, after_ref, lower_ref):
    del after_ref
    lower_ref[...] = below_ref[...] + corner_ref[...]


def lowered(below, corner, after):
    return pl.pallas_call(
        lower_kernel,
        out_shape=jax.ShapeDtypeStruct(below.shape, F32),
        in_specs=[vm(), vm(), anywhere()],
        out_specs=vm(),
        compiler_params=params(),
        cost_estimate=pl.CostEstimate(flops=below.size, bytes_accessed=12 * below.size, transcendentals=0),
    )(below, corner, after)


def share_kernel(terms_ref, start_ref, *refs):
    out_ref = refs[-1]
    total = jnp.sum(terms_ref[:, :, :SIDE], axis=0)
    peak = jnp.max(terms_ref[:, :, SIDE:], axis=0)
    for q in range(4):
        lanes = slice(q * QUARTER, (q + 1) * QUARTER)
        value = start_ref[:, lanes] + 0.5 * total[:, lanes] / (peak + 1e-06)
        out_ref[:, :, lanes] = jnp.broadcast_to(value, out_ref.shape[:2] + (QUARTER,))


def shared(terms, start, after):
    count, share, _ = terms.shape
    return pl.pallas_call(
        share_kernel,
        out_shape=jax.ShapeDtypeStruct((count, share, SIDE), F32),
        in_specs=[vm()] * 2 + [anywhere()] * len(after),
        out_specs=vm(),
        compiler_params=params(),
        cost_estimate=pl.CostEstimate(flops=2 * terms.size, bytes_accessed=8 * terms.size, transcendentals=0),
    )(terms, start, *after)


def shifted(value, axis, steps):
    count = lax.axis_size(axis)
    first, last = (max(0, -steps), min(count, count - steps))
    return lax.ppermute(value, axis, [(source, source + steps) for source in range(first, last)])


def other_core(value):
    return lax.ppermute(value, "core", [(0, 1), (1, 0)])


def base_kernel(scale_ref, own_ref, t_own_ref, base_ref):
    base_ref[...] = own_ref[...] + scale_ref[0, 0] * t_own_ref[...]


def base(scale, own, t_own):
    return pl.pallas_call(
        base_kernel,
        out_shape=jax.ShapeDtypeStruct(own.shape, F32),
        in_specs=[sm(), vm(), vm()],
        out_specs=vm(),
        compiler_params=params(),
        cost_estimate=pl.CostEstimate(flops=2 * own.size, bytes_accessed=12 * own.size, transcendentals=0),
    )(scale, own, t_own)


def object_kernel(scale_ref, base_ref, left_ref, *refs):
    out_ref = refs[-1]
    first = 0
    for ref, size in zip(refs, BACK):
        at = slice(first, first + size)
        out_ref[:, at, :] = base_ref[:, at, :] + scale_ref[0, 0] * (left_ref[:, at, :] + ref[...])
        first += size


def finished_object(scale, start, left, above):
    return pl.pallas_call(
        object_kernel,
        out_shape=jax.ShapeDtypeStruct(start.shape, F32),
        in_specs=[sm(), vm(), vm()] + [vm()] * len(above),
        out_specs=vm(),
        compiler_params=params(),
        cost_estimate=pl.CostEstimate(flops=3 * start.size, bytes_accessed=16 * start.size, transcendentals=0),
    )(scale, start, left, *above)


def probe_kernel(core_ref, mine_ref, other_ref, out_ref):
    core = core_ref[0, 0]
    out_ref[core] = mine_ref[...]
    out_ref[1 - core] = other_ref[...]


def joined(core, mine, other):
    return pl.pallas_call(
        probe_kernel,
        out_shape=jax.ShapeDtypeStruct((2, SIDE, SIDE), F32),
        in_specs=[sm(), vm(), vm()],
        out_specs=vm(),
        compiler_params=params(),
        cost_estimate=pl.CostEstimate(flops=0, bytes_accessed=16 * SIDE * SIDE, transcendentals=0),
    )(core, mine, other)


def on_device(object_field, probe, amplitudes, positions):
    row, col, core = lax.axis_index(ROW), lax.axis_index(COL), lax.axis_index("core")
    where = jnp.stack(
        [positions[:, 0] - row * SIDE, positions[:, 1] - col * SIDE, jnp.stack([core, row]).astype(jnp.int32)]
    )
    matrices = [jnp.asarray(m) for m in split_matrices()]
    pieces = [object_field[:, k * PIECE : (k + 1) * PIECE] for k in range(PIECES)]
    below = [shifted(piece, ROW, -1) for piece in pieces]
    right = shifted(object_field, COL, -1)
    rolled, amps, peaks = ready(where, probe, object_field, amplitudes)
    scale = 0.9 / (peaks[1, :1, :1] + 1e-06)
    specs, wrapped, tokens = [], [], [peaks]
    for k in range(PIECES):
        if k == 1:
            (below[1],) = tied((below[1],), (below[0], peaks))
        elif k > 1:
            (below[k],) = tied((below[k],), (below[k - 1], tokens[k - 2]))
        corner = shifted(below[k], COL, -1)
        spec, wrap, token = fore(k, where, object_field, right, below[k], corner, rolled, matrices)
        specs.append(spec)
        wrapped.append(wrap)
        tokens[k:] = [token]
    t_own, t_right, t_below, t_diag, keep, send = update(
        where, specs, wrapped, rolled, amps, peaks, matrices
    )

    came = other_core(send)
    corner = [shifted(t, COL, 1) for t in t_diag]
    half, lower = first_sums(keep, came, t_below[0], corner[0])
    share = SIDE // 64
    terms = lax.all_to_all(half.reshape(64, share, WIDE), CHIPS, 0, 0)
    from_above = [shifted(lower, ROW, 1)]
    lower = lowered(t_below[1], corner[1], from_above[0])
    from_above.append(shifted(lower, ROW, 1))
    lower = lowered(t_below[2], corner[2], lower)
    from_above.append(shifted(lower, ROW, 1))
    from_left = shifted(t_right, COL, 1)
    at = lax.axis_index(CHIPS) * share
    start = lax.dynamic_slice(probe, (core, at, jnp.zeros_like(at)), (1, share, SIDE))[0]
    shares = shared(terms, start, from_above[:2] + [lower])
    mine = lax.all_to_all(shares, CHIPS, 0, 0).reshape(SIDE, SIDE)
    begun = base(scale, object_field, t_own)
    (mine,) = tied((mine,), (from_above[2], from_left, begun))
    new_probe = joined(core.astype(jnp.int32).reshape(1, 1), mine, other_core(mine))
    new_object = finished_object(scale, begun, from_left, from_above)
    return (new_object, new_probe)


CHIPS = ("y", "x", "z")
ROW = ("y", "x")
COL = ("z", "core")


def solution(mesh):
    chips = jax.sharding.Mesh(mesh.devices.reshape(4, 4, 4, 2), ROW + COL)
    in_specs = (P(None, ROW, COL), P(), P(ROW + COL, None, None), P(ROW + COL, None))
    out_specs = (P(None, ROW, COL), P())
    return jax.shard_map(
        on_device, mesh=chips, in_specs=in_specs, out_specs=out_specs, check_vma=False
    )
```

```python
import functools
import math

import jax
import jax.numpy as jnp
import numpy as np
from jax import lax
from jax.experimental import pallas as pl
from jax.experimental.pallas import tpu as pltpu
from jax.sharding import PartitionSpec as P

SIDE = 512
QUARTER = 128
SIZES = (192, 192, 128)
FIRSTS = (0, 192, 384)
PIECES = len(SIZES)
WIDE = SIDE + 128
COST = pl.CostEstimate(flops=0, bytes_accessed=0, transcendentals=0)
F32 = jnp.float32
BF16 = jnp.bfloat16


def split_matrices():
    k = np.arange(QUARTER)[:, None]
    n = np.arange(QUARTER)[None, :]
    parts = []
    for p in range(4):
        angle = 2.0 * np.pi * (((4 * k + p) * n) % SIDE) / SIDE
        re, im = np.cos(angle) / np.sqrt(SIDE), -np.sin(angle) / np.sqrt(SIDE)
        parts.append(np.block([[re, -im], [im, re]]))
    left = np.stack(parts)
    out = []
    for matrix in (left, np.swapaxes(left, 1, 2)):
        high = matrix.astype(np.float32).astype(jnp.bfloat16)
        low = (matrix - high.astype(np.float64)).astype(np.float32).astype(jnp.bfloat16)
        out += [np.ascontiguousarray(high), np.ascontiguousarray(low)]
    return out


def order_matrix():
    at = np.arange(SIDE)
    matrix = np.zeros((SIDE, SIDE), np.float32)
    matrix[at, (at % 4) * QUARTER + at // 4] = 1.0
    return matrix.astype(jnp.bfloat16)


def split(value):
    high = value.astype(BF16)
    return high, (value - high.astype(F32)).astype(BF16)


def mm(left, right):
    return jnp.dot(left, right, preferred_element_type=F32)


def fold(x, sign):
    (r0, i0), (r1, i1), (r2, i2), (r3, i3) = x
    sr, si, dr, di = r0 + r2, i0 + i2, r0 - r2, i0 - i2
    tr, ti, er, ei = r1 + r3, i1 + i3, r1 - r3, i1 - i3
    first = (dr + ei, di - er)
    second = (dr - ei, di + er)
    if sign > 0:
        first, second = second, first
    return [(sr + tr, si + ti), first, (sr - tr, si - ti), second]


def ready_kernel(
    where_ref, probe_ref, own_ref, amp_ref, order_ref, *refs
):
    rolled_refs = refs[:PIECES]
    amps_ref, peaks_ref, columns = refs[PIECES:]
    for item in range(2):
        down, along = where_ref[0, item], where_ref[1, item]
        for part in range(2):
            value = pltpu.roll(probe_ref[part], down, 0)
            value = pltpu.roll(value, along, 1)
            for ref, first, size in zip(rolled_refs, FIRSTS, SIZES):
                ref[item, part] = value[first : first + size]
        rows = amp_ref[item]
        high = rows.astype(BF16)
        rest = rows - high.astype(F32)
        middle = rest.astype(BF16)
        low = (rest - middle.astype(F32)).astype(BF16)
        order = order_ref[...]
        moved = mm(high, order) + mm(middle, order) + mm(low, order)
        for q in range(4):
            lanes = slice(q * QUARTER, (q + 1) * QUARTER)
            columns[q] = moved[:, lanes]
            for p in range(4):
                amps_ref[item, p * QUARTER : (p + 1) * QUARTER, lanes] = columns[
                    q, pl.ds(p, QUARTER, stride=4), :
                ]
    own = own_ref[0] ** 2 + own_ref[1] ** 2
    beam = probe_ref[0] ** 2 + probe_ref[1] ** 2
    peaks_ref[0] = jnp.full((8, 128), jnp.max(own), F32)
    peaks_ref[1] = jnp.full((8, 128), jnp.max(beam), F32)


def fore_kernel(
    piece, where_ref, own_ref, right_ref, below_ref, diag_ref, rolled_ref, mh_ref, ml_ref,
    spec_ref, wrapped_ref, token_ref,
):
    token_ref[...] = jnp.zeros_like(token_ref)
    lane = lax.broadcasted_iota(jnp.int32, (SIZES[piece], SIDE), 1)
    row = lax.broadcasted_iota(jnp.int32, (SIZES[piece], SIDE), 0) + FIRSTS[piece]
    for item in range(2):
        down, along = where_ref[0, item], where_ref[1, item]
        above, beside = row < down, lane < along
        value = []
        for part in range(2):
            lower = jnp.where(beside, diag_ref[part], below_ref[part])
            upper = jnp.where(beside, right_ref[part], own_ref[part])
            value.append(jnp.where(above, lower, upper))
            wrapped_ref[item, part] = value[part]
        beam_r, beam_i = rolled_ref[item, 0], rolled_ref[item, 1]
        psi_r = beam_r * value[0] - beam_i * value[1]
        psi_i = beam_r * value[1] + beam_i * value[0]
        blocks = [
            (psi_r[:, q * QUARTER : (q + 1) * QUARTER], psi_i[:, q * QUARTER : (q + 1) * QUARTER])
            for q in range(4)
        ]
        for p, (br, bi) in enumerate(fold(blocks, -1)):
            hi, lo = split(jnp.concatenate([br, bi], axis=1))
            out = mm(hi, mh_ref[p]) + mm(lo, mh_ref[p]) + mm(hi, ml_ref[p])
            spec_ref[item, 0, :, p * QUARTER : (p + 1) * QUARTER] = out[:, :QUARTER]
            spec_ref[item, 1, :, p * QUARTER : (p + 1) * QUARTER] = out[:, QUARTER:]


def fore(piece, where, own, right, below, diag, rolled, matrices):
    size = SIZES[piece]
    at = FIRSTS[piece] // size
    rows = pl.BlockSpec((2, size, SIDE), lambda i: (0, at, 0))
    full = pl.BlockSpec((2, size, SIDE), lambda i: (0, 0, 0))
    whole = pl.BlockSpec((4, 2 * QUARTER, 2 * QUARTER), lambda i: (0, 0, 0))
    four = pl.BlockSpec((2, 2, size, SIDE), lambda i: (0, 0, 0, 0))
    shape = jax.ShapeDtypeStruct((2, 2, size, SIDE), F32)
    return pl.pallas_call(
        functools.partial(fore_kernel, piece),
        grid=(1,),
        out_shape=[shape, shape, jax.ShapeDtypeStruct((8, 128), F32)],
        in_specs=[sm(), rows, rows, full, full, four, whole, whole],
        out_specs=[four, four, pl.BlockSpec((8, 128), lambda i: (0, 0))],
        compiler_params=params(20),
        cost_estimate=COST,
    )(where, own, right, below, diag, rolled, *matrices[2:])


def rows_of(refs, item, part, first, last, lanes=slice(None)):
    values = []
    for ref, start, size in zip(refs, FIRSTS, SIZES):
        low, high = max(first, start) - start, min(last, start + size) - start
        if low < high:
            values.append(ref[item, part, low:high, lanes])
    return values[0] if len(values) == 1 else jnp.concatenate(values, axis=0)


def update_kernel(where_ref, *refs):
    spec_refs, wrapped_refs, rolled_refs = refs[:PIECES], refs[PIECES : 2 * PIECES], refs[2 * PIECES : 3 * PIECES]
    amps_ref, peaks_ref, lh_ref, ll_ref, mh_ref, ml_ref = refs[3 * PIECES : 3 * PIECES + 6]
    outs = refs[3 * PIECES + 6 :]
    targets, keep_ref, send_ref = outs[:4], outs[4], outs[5]
    high, low, grad, terms, out_sems = outs[6:]
    core = where_ref[2, 0]

    wide = 2 * QUARTER
    for item in range(2):
        for chunk in range(SIDE // wide):
            cols = slice(chunk * wide, (chunk + 1) * wide)
            blocks = [
                tuple(
                    rows_of(spec_refs, item, part, q * QUARTER, (q + 1) * QUARTER, cols)
                    for part in range(2)
                )
                for q in range(4)
            ]
            back = []
            for p, (br, bi) in enumerate(fold(blocks, -1)):
                hi, lo = split(jnp.concatenate([br, bi], axis=0))
                out = mm(lh_ref[p], hi) + mm(lh_ref[p], lo) + mm(ll_ref[p], hi)
                sr, si = out[:QUARTER], out[QUARTER:]
                factor = amps_ref[item, p * QUARTER : (p + 1) * QUARTER, cols] * lax.rsqrt(
                    sr * sr + si * si + 0.25
                )
                hi, lo = split(jnp.concatenate([sr * factor, si * factor], axis=0))
                out = mm(mh_ref[p], hi) + mm(mh_ref[p], lo) + mm(ml_ref[p], hi)
                back.append((out[:QUARTER], out[QUARTER:]))
            for q, (xr, xi) in enumerate(fold(back, 1)):
                rows = slice(q * QUARTER, (q + 1) * QUARTER)
                for part, value in enumerate((xr, xi)):
                    hi, lo = split(value)
                    for half in range(2):
                        p = 2 * chunk + half
                        to = slice(p * wide + part * QUARTER, p * wide + (part + 1) * QUARTER)
                        piece = slice(half * QUARTER, (half + 1) * QUARTER)
                        high[item, rows, to] = hi[:, piece]
                        low[item, rows, to] = lo[:, piece]

    stores = []
    for piece, (first, size) in enumerate(zip(FIRSTS, SIZES)):
        at = slice(first, first + size)
        lane = lax.broadcasted_iota(jnp.int32, (size, SIDE), 1)
        row = lax.broadcasted_iota(jnp.int32, (size, SIDE), 0) + first
        for item in range(2):
            down, along = where_ref[0, item], where_ref[1, item]
            above, beside = row < down, lane < along
            back = []
            for p in range(4):
                cols = slice(p * wide, (p + 1) * wide)
                hi, lo = high[item, at, cols], low[item, at, cols]
                out = mm(hi, lh_ref[p]) + mm(lo, lh_ref[p]) + mm(hi, ll_ref[p])
                back.append((out[:, :QUARTER], out[:, QUARTER:]))
            back = fold(back, 1)
            back_r = jnp.concatenate([b[0] for b in back], axis=1)
            back_i = jnp.concatenate([b[1] for b in back], axis=1)
            beam_r, beam_i = rolled_refs[piece][item, 0], rolled_refs[piece][item, 1]
            patch_r, patch_i = wrapped_refs[piece][item, 0], wrapped_refs[piece][item, 1]
            diff_r = back_r - (beam_r * patch_r - beam_i * patch_i)
            diff_i = back_i - (beam_r * patch_i + beam_i * patch_r)
            term = (beam_r * diff_r + beam_i * diff_i, beam_r * diff_i - beam_i * diff_r)
            grad[item, 0, at, :] = patch_r * diff_r + patch_i * diff_i
            grad[item, 1, at, :] = patch_r * diff_i - patch_i * diff_r
            for part in range(2):
                zero = jnp.zeros_like(term[part])
                upper = jnp.where(above, zero, term[part])
                lower = jnp.where(above, term[part], zero)
                four = (
                    jnp.where(beside, zero, upper),
                    jnp.where(beside, upper, zero),
                    jnp.where(beside, zero, lower),
                    jnp.where(beside, lower, zero),
                )
                for k, value in enumerate(four):
                    if item == 0:
                        terms[k, part, at] = value
                    else:
                        terms[k, part, at] += value
        for k, target in enumerate(targets):
            store = pltpu.make_async_copy(terms.at[k, :, at], target.at[:, at], out_sems.at[len(stores)])
            store.start()
            stores.append(store)
    whole = []
    for part in range(2):
        total = None
        for item in range(2):
            down, along = where_ref[0, item], where_ref[1, item]
            value = pltpu.roll(grad[item, part], (SIDE - down) % SIDE, 0)
            value = pltpu.roll(value, (SIDE - along) % SIDE, 1)
            total = value if total is None else total + value
        whole.append(total)
    keep_ref[:, :SIDE] = jnp.where(core == 0, whole[0], whole[1])
    send_ref[:, :SIDE] = jnp.where(core == 0, whole[1], whole[0])
    peak = jnp.broadcast_to(peaks_ref[0, :1, :], (SIDE, 128))
    keep_ref[:, SIDE:] = peak
    send_ref[:, SIDE:] = peak
    for store in stores:
        store.wait()


def vm():
    return pl.BlockSpec(memory_space=pltpu.VMEM)


def sm():
    return pl.BlockSpec(memory_space=pltpu.SMEM)


def anywhere():
    return pl.BlockSpec(memory_space=pl.ANY)


def params(mebibytes=16):
    return pltpu.CompilerParams(vmem_limit_bytes=mebibytes * 2**20)


def ready(where, probe, own, amplitudes):
    return pl.pallas_call(
        ready_kernel,
        out_shape=tuple(jax.ShapeDtypeStruct((2, 2, size, SIDE), F32) for size in SIZES)
        + (
            jax.ShapeDtypeStruct((2, SIDE, SIDE), F32),
            jax.ShapeDtypeStruct((2, 8, 128), F32),
        ),
        in_specs=[sm()] + [vm()] * 4,
        out_specs=(vm(),) * (PIECES + 2),
        scratch_shapes=[pltpu.VMEM((4, SIDE, QUARTER), F32)],
        compiler_params=params(32),
        cost_estimate=COST,
    )(where, probe, own, amplitudes, jnp.asarray(order_matrix()))


def update(where, specs, wrapped, rolled, amps, peaks, matrices):
    full = jax.ShapeDtypeStruct((2, SIDE, SIDE), F32)
    plane = jax.ShapeDtypeStruct((SIDE, WIDE), F32)
    out_shape = (full,) * 4 + (plane, plane)
    four = pltpu.VMEM((2, 2, SIDE, SIDE), F32)
    half = pltpu.VMEM((2, SIDE, 2 * SIDE), BF16)
    return pl.pallas_call(
        update_kernel,
        out_shape=out_shape,
        in_specs=[sm()] + [vm()] * (3 * PIECES + 6),
        out_specs=(anywhere(),) * 4 + (vm(), vm()),
        scratch_shapes=[
            half,
            half,
            four,
            pltpu.VMEM((4, 2, SIDE, SIDE), F32),
            pltpu.SemaphoreType.DMA((4 * PIECES,)),
        ],
        compiler_params=params(36),
        cost_estimate=COST,
    )(where, *specs, *wrapped, *rolled, amps, peaks, *matrices)


def nothing_kernel(*refs):
    del refs


def tied(values, after):
    count = len(values) + len(after)
    return pl.pallas_call(
        nothing_kernel,
        out_shape=[jax.ShapeDtypeStruct(v.shape, v.dtype) for v in values],
        in_specs=[anywhere()] * count,
        out_specs=[anywhere()] * len(values),
        input_output_aliases={k: k for k in range(len(values))},
        cost_estimate=COST,
    )(*values, *after)


def first_kernel(keep_ref, came_ref, half_ref):
    half_ref[:, :SIDE] = keep_ref[:, :SIDE] + came_ref[:, :SIDE]
    half_ref[:, SIDE:] = jnp.maximum(keep_ref[:, SIDE:], came_ref[:, SIDE:])


def first_sum(keep, came):
    return pl.pallas_call(
        first_kernel,
        out_shape=jax.ShapeDtypeStruct(keep.shape, F32),
        in_specs=[vm()] * 2,
        out_specs=vm(),
        compiler_params=params(),
        cost_estimate=COST,
    )(keep, came)


def lower_kernel(below_ref, corner_ref, after_ref, lower_ref):
    del after_ref
    lower_ref[...] = below_ref[...] + corner_ref[...]


def lowered(below, corner, after):
    return pl.pallas_call(
        lower_kernel,
        out_shape=jax.ShapeDtypeStruct(below.shape, F32),
        in_specs=[vm(), vm(), anywhere()],
        out_specs=vm(),
        compiler_params=params(),
        cost_estimate=COST,
    )(below, corner, after)


def share_kernel(terms_ref, start_ref, *refs):
    out_ref = refs[-1]
    total = jnp.sum(terms_ref[:, :, :SIDE], axis=0)
    peak = jnp.max(terms_ref[:, :, SIDE:], axis=0)
    for q in range(4):
        lanes = slice(q * QUARTER, (q + 1) * QUARTER)
        value = start_ref[:, lanes] + 0.5 * total[:, lanes] / (peak + 1e-06)
        out_ref[:, :, lanes] = jnp.broadcast_to(value, out_ref.shape[:2] + (QUARTER,))


def shared(terms, start, after):
    count, share, _ = terms.shape
    return pl.pallas_call(
        share_kernel,
        out_shape=jax.ShapeDtypeStruct((count, share, SIDE), F32),
        in_specs=[vm()] * 2 + [anywhere()] * len(after),
        out_specs=vm(),
        compiler_params=params(),
        cost_estimate=COST,
    )(terms, start, *after)


def shifted(value, axis, steps):
    count = lax.axis_size(axis)
    first, last = (max(0, -steps), min(count, count - steps))
    return lax.ppermute(value, axis, [(source, source + steps) for source in range(first, last)])


def other_core(value):
    return lax.ppermute(value, "core", [(0, 1), (1, 0)])


def base_kernel(scale_ref, own_ref, t_own_ref, base_ref):
    base_ref[...] = own_ref[...] + scale_ref[0, 0] * t_own_ref[...]


def base(scale, own, t_own):
    return pl.pallas_call(
        base_kernel,
        out_shape=jax.ShapeDtypeStruct(own.shape, F32),
        in_specs=[sm(), vm(), vm()],
        out_specs=vm(),
        compiler_params=params(),
        cost_estimate=COST,
    )(scale, own, t_own)


def object_kernel(scale_ref, base_ref, left_ref, above_ref, out_ref):
    out_ref[...] = base_ref[...] + scale_ref[0, 0] * (left_ref[...] + above_ref[...])


def finished_object(scale, start, left, above):
    return pl.pallas_call(
        object_kernel,
        out_shape=jax.ShapeDtypeStruct(start.shape, F32),
        in_specs=[sm()] + [vm()] * 3,
        out_specs=vm(),
        compiler_params=params(),
        cost_estimate=COST,
    )(scale, start, left, above)


def probe_kernel(core_ref, mine_ref, other_ref, out_ref):
    core = core_ref[0, 0]
    out_ref[core] = mine_ref[...]
    out_ref[1 - core] = other_ref[...]


def joined(core, mine, other):
    return pl.pallas_call(
        probe_kernel,
        out_shape=jax.ShapeDtypeStruct((2, SIDE, SIDE), F32),
        in_specs=[sm(), vm(), vm()],
        out_specs=vm(),
        compiler_params=params(),
        cost_estimate=COST,
    )(core, mine, other)


def on_device(object_field, probe, amplitudes, positions):
    row, col, core = lax.axis_index(ROW), lax.axis_index(COL), lax.axis_index("core")
    where = jnp.stack(
        [positions[:, 0] - row * SIDE, positions[:, 1] - col * SIDE, jnp.stack([core, row]).astype(jnp.int32)]
    )
    matrices = [jnp.asarray(m) for m in split_matrices()]
    pieces = [object_field[:, first : first + size] for first, size in zip(FIRSTS, SIZES)]
    below = [shifted(piece, ROW, -1) for piece in pieces]
    right = shifted(object_field, COL, -1)
    *rolled, amps, peaks = ready(where, probe, object_field, amplitudes)
    scale = 0.9 / (peaks[1, :1, :1] + 1e-06)
    specs, wrapped, tokens = [], [], []
    for k in range(PIECES):
        after = (tokens[k - 1],) if k > 1 else (peaks,)
        after += (below[k - 1],) if k else ()
        (below[k],) = tied((below[k],), after)
        corner = shifted(below[k], COL, -1)
        spec, wrap, token = fore(k, where, object_field, right, below[k], corner, rolled[k], matrices)
        specs.append(spec)
        wrapped.append(wrap)
        tokens.append(token)
    t_own, t_right, t_below, t_diag, keep, send = update(
        where, specs, wrapped, rolled, amps, peaks, matrices
    )

    corner = shifted(t_diag, COL, 1)
    half = first_sum(keep, other_core(send))
    share = SIDE // 64
    terms = lax.all_to_all(half.reshape(64, share, WIDE), CHIPS, 0, 0)
    lower = lowered(t_below, corner, half)
    from_above = shifted(lower, ROW, 1)
    (t_right,) = tied((t_right,), (lower,))
    from_left = shifted(t_right, COL, 1)
    at = lax.axis_index(CHIPS) * share
    start = lax.dynamic_slice(probe, (core, at, jnp.zeros_like(at)), (1, share, SIDE))[0]
    shares = shared(terms, start, [lower])
    mine = lax.all_to_all(shares, CHIPS, 0, 0).reshape(SIDE, SIDE)
    begun = base(scale, object_field, t_own)
    (mine,) = tied((mine,), (from_above, from_left, begun))
    new_probe = joined(core.astype(jnp.int32).reshape(1, 1), mine, other_core(mine))
    new_object = finished_object(scale, begun, from_left, from_above)
    return (new_object, new_probe)


CHIPS = ("y", "x", "z")
ROW = ("y", "x")
COL = ("z", "core")


def solution(mesh):
    chips = jax.sharding.Mesh(mesh.devices.reshape(4, 4, 4, 2), ROW + COL)
    in_specs = (P(None, ROW, COL), P(), P(ROW + COL, None, None), P(ROW + COL, None))
    out_specs = (P(None, ROW, COL), P())
    return jax.shard_map(
        on_device, mesh=chips, in_specs=in_specs, out_specs=out_specs, check_vma=False
    )
```

```python
import functools
import math

import jax
import jax.numpy as jnp
import numpy as np
from jax import lax
from jax.experimental import pallas as pl
from jax.experimental.pallas import tpu as pltpu
from jax.sharding import PartitionSpec as P

SIDE = 512
QUARTER = 128
SIZES = (128,) * 4
FIRSTS = (0, 128, 256, 384)
BACK = (128, 384)
WIDE = SIDE + 128
PIECES = len(SIZES)
COST = pl.CostEstimate(flops=0, bytes_accessed=0, transcendentals=0)
F32 = jnp.float32
BF16 = jnp.bfloat16


def split_matrices():
    k = np.arange(QUARTER)[:, None]
    n = np.arange(QUARTER)[None, :]
    parts = []
    for p in range(4):
        angle = 2.0 * np.pi * (((4 * k + p) * n) % SIDE) / SIDE
        re, im = np.cos(angle) / np.sqrt(SIDE), -np.sin(angle) / np.sqrt(SIDE)
        parts.append(np.block([[re, -im], [im, re]]))
    left = np.stack(parts)
    out = []
    for matrix in (left, np.swapaxes(left, 1, 2)):
        high = matrix.astype(np.float32).astype(jnp.bfloat16)
        low = (matrix - high.astype(np.float64)).astype(np.float32).astype(jnp.bfloat16)
        out += [np.ascontiguousarray(high), np.ascontiguousarray(low)]
    return out


def order_matrix():
    at = np.arange(SIDE)
    matrix = np.zeros((SIDE, SIDE), np.float32)
    matrix[at, (at % 4) * QUARTER + at // 4] = 1.0
    return matrix.astype(jnp.bfloat16)


def split(value):
    high = value.astype(BF16)
    return high, (value - high.astype(F32)).astype(BF16)


def mm(left, right):
    return jnp.dot(left, right, preferred_element_type=F32)


def fold(x, sign):
    (r0, i0), (r1, i1), (r2, i2), (r3, i3) = x
    sr, si, dr, di = r0 + r2, i0 + i2, r0 - r2, i0 - i2
    tr, ti, er, ei = r1 + r3, i1 + i3, r1 - r3, i1 - i3
    first = (dr + ei, di - er)
    second = (dr - ei, di + er)
    if sign > 0:
        first, second = second, first
    return [(sr + tr, si + ti), first, (sr - tr, si - ti), second]


def ready_kernel(
    where_ref, probe_ref, own_ref, amp_ref, order_ref, *refs
):
    rolled_refs = refs[:PIECES]
    amps_ref, peaks_ref, columns = refs[PIECES:]
    for item in range(2):
        down, along = where_ref[0, item], where_ref[1, item]
        for part in range(2):
            value = pltpu.roll(probe_ref[part], down, 0)
            value = pltpu.roll(value, along, 1)
            for ref, first, size in zip(rolled_refs, FIRSTS, SIZES):
                ref[item, part] = value[first : first + size]
        rows = amp_ref[item]
        high = rows.astype(BF16)
        rest = rows - high.astype(F32)
        middle = rest.astype(BF16)
        low = (rest - middle.astype(F32)).astype(BF16)
        order = order_ref[...]
        moved = mm(high, order) + mm(middle, order) + mm(low, order)
        for q in range(4):
            lanes = slice(q * QUARTER, (q + 1) * QUARTER)
            columns[q] = moved[:, lanes]
            for p in range(4):
                amps_ref[item, p * QUARTER : (p + 1) * QUARTER, lanes] = columns[
                    q, pl.ds(p, QUARTER, stride=4), :
                ]
    own = own_ref[0] ** 2 + own_ref[1] ** 2
    beam = probe_ref[0] ** 2 + probe_ref[1] ** 2
    peaks_ref[0] = jnp.full((8, 128), jnp.max(own), F32)
    peaks_ref[1] = jnp.full((8, 128), jnp.max(beam), F32)


def fore_kernel(
    piece, where_ref, own_ref, right_ref, below_ref, diag_ref, rolled_ref, mh_ref, ml_ref,
    spec_ref, wrapped_ref, token_ref,
):
    token_ref[...] = jnp.zeros_like(token_ref)
    lane = lax.broadcasted_iota(jnp.int32, (SIZES[piece], SIDE), 1)
    row = lax.broadcasted_iota(jnp.int32, (SIZES[piece], SIDE), 0) + FIRSTS[piece]
    for item in range(2):
        down, along = where_ref[0, item], where_ref[1, item]
        above, beside = row < down, lane < along
        value = []
        for part in range(2):
            lower = jnp.where(beside, diag_ref[part], below_ref[part])
            upper = jnp.where(beside, right_ref[part], own_ref[part])
            value.append(jnp.where(above, lower, upper))
            wrapped_ref[item, part] = value[part]
        beam_r, beam_i = rolled_ref[item, 0], rolled_ref[item, 1]
        psi_r = beam_r * value[0] - beam_i * value[1]
        psi_i = beam_r * value[1] + beam_i * value[0]
        blocks = [
            (psi_r[:, q * QUARTER : (q + 1) * QUARTER], psi_i[:, q * QUARTER : (q + 1) * QUARTER])
            for q in range(4)
        ]
        for p, (br, bi) in enumerate(fold(blocks, -1)):
            hi, lo = split(jnp.concatenate([br, bi], axis=1))
            out = mm(hi, mh_ref[p]) + mm(lo, mh_ref[p]) + mm(hi, ml_ref[p])
            spec_ref[item, 0, :, p * QUARTER : (p + 1) * QUARTER] = out[:, :QUARTER]
            spec_ref[item, 1, :, p * QUARTER : (p + 1) * QUARTER] = out[:, QUARTER:]


def fore(piece, where, own, right, below, diag, rolled, matrices):
    size = SIZES[piece]
    tile = pl.BlockSpec((2, size, SIDE), lambda i: (0, piece, 0))
    full = pl.BlockSpec((2, size, SIDE), lambda i: (0, 0, 0))
    whole = pl.BlockSpec((4, 2 * QUARTER, 2 * QUARTER), lambda i: (0, 0, 0))
    four = pl.BlockSpec((2, 2, size, SIDE), lambda i: (0, 0, 0, 0))
    shape = jax.ShapeDtypeStruct((2, 2, size, SIDE), F32)
    return pl.pallas_call(
        functools.partial(fore_kernel, piece),
        grid=(1,),
        out_shape=[shape, shape, jax.ShapeDtypeStruct((8, 128), F32)],
        in_specs=[sm(), tile, tile, full, full, four, whole, whole],
        out_specs=[four, four, pl.BlockSpec((8, 128), lambda i: (0, 0))],
        compiler_params=params(20),
        cost_estimate=COST,
    )(where, own, right, below, diag, rolled, *matrices[2:])


def rows_of(refs, item, part, first, last, lanes=slice(None)):
    values = []
    for ref, start, size in zip(refs, FIRSTS, SIZES):
        low, high = max(first, start) - start, min(last, start + size) - start
        if low < high:
            values.append(ref[item, part, low:high, lanes])
    return values[0] if len(values) == 1 else jnp.concatenate(values, axis=0)


def update_kernel(where_ref, *refs):
    spec_refs, wrapped_refs, rolled_refs = refs[:PIECES], refs[PIECES : 2 * PIECES], refs[2 * PIECES : 3 * PIECES]
    amps_ref, peaks_ref, lh_ref, ll_ref, mh_ref, ml_ref = refs[3 * PIECES : 3 * PIECES + 6]
    outs = refs[3 * PIECES + 6 :]
    targets, keep_ref, send_ref = outs[:6], outs[6], outs[7]
    high, low, grad, terms, out_sems = outs[8:]
    core = where_ref[2, 0]

    wide = 2 * QUARTER
    for item in range(2):
        for chunk in range(SIDE // wide):
            cols = slice(chunk * wide, (chunk + 1) * wide)
            blocks = [
                tuple(
                    rows_of(spec_refs, item, part, q * QUARTER, (q + 1) * QUARTER, cols)
                    for part in range(2)
                )
                for q in range(4)
            ]
            back = []
            for p, (br, bi) in enumerate(fold(blocks, -1)):
                hi, lo = split(jnp.concatenate([br, bi], axis=0))
                out = mm(lh_ref[p], hi) + mm(lh_ref[p], lo) + mm(ll_ref[p], hi)
                sr, si = out[:QUARTER], out[QUARTER:]
                factor = amps_ref[item, p * QUARTER : (p + 1) * QUARTER, cols] * lax.rsqrt(
                    sr * sr + si * si + 0.25
                )
                hi, lo = split(jnp.concatenate([sr * factor, si * factor], axis=0))
                out = mm(mh_ref[p], hi) + mm(mh_ref[p], lo) + mm(ml_ref[p], hi)
                back.append((out[:QUARTER], out[QUARTER:]))
            for q, (xr, xi) in enumerate(fold(back, 1)):
                rows = slice(q * QUARTER, (q + 1) * QUARTER)
                for part, value in enumerate((xr, xi)):
                    hi, lo = split(value)
                    for half in range(2):
                        p = 2 * chunk + half
                        to = slice(p * wide + part * QUARTER, p * wide + (part + 1) * QUARTER)
                        piece = slice(half * QUARTER, (half + 1) * QUARTER)
                        high[item, rows, to] = hi[:, piece]
                        low[item, rows, to] = lo[:, piece]

    stores = []
    size = QUARTER
    for first in range(0, SIDE, size):
        at = slice(first, first + size)
        lane = lax.broadcasted_iota(jnp.int32, (size, SIDE), 1)
        row = lax.broadcasted_iota(jnp.int32, (size, SIDE), 0) + first
        for item in range(2):
            down, along = where_ref[0, item], where_ref[1, item]
            above, beside = row < down, lane < along
            back = []
            for p in range(4):
                cols = slice(p * wide, (p + 1) * wide)
                hi, lo = high[item, at, cols], low[item, at, cols]
                out = mm(hi, lh_ref[p]) + mm(lo, lh_ref[p]) + mm(hi, ll_ref[p])
                back.append((out[:, :QUARTER], out[:, QUARTER:]))
            back = fold(back, 1)
            back_r = jnp.concatenate([b[0] for b in back], axis=1)
            back_i = jnp.concatenate([b[1] for b in back], axis=1)
            beam_r, beam_i = (rows_of(rolled_refs, item, part, first, first + size) for part in range(2))
            patch_r, patch_i = (rows_of(wrapped_refs, item, part, first, first + size) for part in range(2))
            diff_r = back_r - (beam_r * patch_r - beam_i * patch_i)
            diff_i = back_i - (beam_r * patch_i + beam_i * patch_r)
            term = (beam_r * diff_r + beam_i * diff_i, beam_r * diff_i - beam_i * diff_r)
            grad[item, 0, at, :] = patch_r * diff_r + patch_i * diff_i
            grad[item, 1, at, :] = patch_r * diff_i - patch_i * diff_r
            for part in range(2):
                zero = jnp.zeros_like(term[part])
                upper = jnp.where(above, zero, term[part])
                lower = jnp.where(above, term[part], zero)
                four = (
                    jnp.where(beside, zero, upper),
                    jnp.where(beside, upper, zero),
                    jnp.where(beside, zero, lower),
                    jnp.where(beside, lower, zero),
                )
                for k, value in enumerate(four):
                    if item == 0:
                        terms[k, part, at] = value
                    else:
                        terms[k, part, at] += value
        half = int(first >= BACK[0])
        within = slice(first - half * BACK[0], first - half * BACK[0] + size)
        parts = (
            targets[0].at[:, at],
            targets[1].at[:, at],
            targets[2 + half].at[:, within],
            targets[4 + half].at[:, within],
        )
        for k, target in enumerate(parts):
            store = pltpu.make_async_copy(terms.at[k, :, at], target, out_sems.at[len(stores)])
            store.start()
            stores.append(store)
    whole = []
    for part in range(2):
        total = None
        for item in range(2):
            down, along = where_ref[0, item], where_ref[1, item]
            value = pltpu.roll(grad[item, part], (SIDE - down) % SIDE, 0)
            value = pltpu.roll(value, (SIDE - along) % SIDE, 1)
            total = value if total is None else total + value
        whole.append(total)
    keep_ref[:, :SIDE] = jnp.where(core == 0, whole[0], whole[1])
    send_ref[:, :SIDE] = jnp.where(core == 0, whole[1], whole[0])
    peak = jnp.broadcast_to(peaks_ref[0, :1, :], (SIDE, 128))
    keep_ref[:, SIDE:] = peak
    send_ref[:, SIDE:] = peak
    for store in stores:
        store.wait()


def vm():
    return pl.BlockSpec(memory_space=pltpu.VMEM)


def sm():
    return pl.BlockSpec(memory_space=pltpu.SMEM)


def anywhere():
    return pl.BlockSpec(memory_space=pl.ANY)


def params(mebibytes=16):
    return pltpu.CompilerParams(vmem_limit_bytes=mebibytes * 2**20)


def ready(where, probe, own, amplitudes):
    return pl.pallas_call(
        ready_kernel,
        out_shape=tuple(jax.ShapeDtypeStruct((2, 2, size, SIDE), F32) for size in SIZES)
        + (
            jax.ShapeDtypeStruct((2, SIDE, SIDE), F32),
            jax.ShapeDtypeStruct((2, 8, 128), F32),
        ),
        in_specs=[sm()] + [vm()] * 4,
        out_specs=(vm(),) * (PIECES + 2),
        scratch_shapes=[pltpu.VMEM((4, SIDE, QUARTER), F32)],
        compiler_params=params(32),
        cost_estimate=COST,
    )(where, probe, own, amplitudes, jnp.asarray(order_matrix()))


def update(where, specs, wrapped, rolled, amps, peaks, matrices):
    full = jax.ShapeDtypeStruct((2, SIDE, SIDE), F32)
    plane = jax.ShapeDtypeStruct((SIDE, WIDE), F32)
    parts = tuple(jax.ShapeDtypeStruct((2, size, SIDE), F32) for size in BACK)
    out_shape = (full,) * 2 + parts * 2 + (plane, plane)
    four = pltpu.VMEM((2, 2, SIDE, SIDE), F32)
    half = pltpu.VMEM((2, SIDE, 2 * SIDE), BF16)
    return pl.pallas_call(
        update_kernel,
        out_shape=out_shape,
        in_specs=[sm()] + [vm()] * (3 * PIECES + 6),
        out_specs=(anywhere(),) * 6 + (vm(), vm()),
        scratch_shapes=[
            half,
            half,
            four,
            pltpu.VMEM((4, 2, SIDE, SIDE), F32),
            pltpu.SemaphoreType.DMA((16,)),
        ],
        compiler_params=params(36),
        cost_estimate=COST,
    )(where, *specs, *wrapped, *rolled, amps, peaks, *matrices)


def nothing_kernel(*refs):
    del refs


def tied(values, after):
    count = len(values) + len(after)
    return pl.pallas_call(
        nothing_kernel,
        out_shape=[jax.ShapeDtypeStruct(v.shape, v.dtype) for v in values],
        in_specs=[anywhere()] * count,
        out_specs=[anywhere()] * len(values),
        input_output_aliases={k: k for k in range(len(values))},
        cost_estimate=COST,
    )(*values, *after)


def first_kernel(keep_ref, came_ref, below_ref, corner_ref, half_ref, lower_ref):
    half_ref[:, :SIDE] = keep_ref[:, :SIDE] + came_ref[:, :SIDE]
    half_ref[:, SIDE:] = jnp.maximum(keep_ref[:, SIDE:], came_ref[:, SIDE:])
    lower_ref[...] = below_ref[...] + corner_ref[...]


def first_sums(keep, came, below, corner):
    return pl.pallas_call(
        first_kernel,
        out_shape=(jax.ShapeDtypeStruct(keep.shape, F32), jax.ShapeDtypeStruct(below.shape, F32)),
        in_specs=[vm()] * 4,
        out_specs=(vm(), vm()),
        compiler_params=params(),
        cost_estimate=COST,
    )(keep, came, below, corner)


def lower_kernel(below_ref, corner_ref, after_ref, lower_ref):
    del after_ref
    lower_ref[...] = below_ref[...] + corner_ref[...]


def lowered(below, corner, after):
    return pl.pallas_call(
        lower_kernel,
        out_shape=jax.ShapeDtypeStruct(below.shape, F32),
        in_specs=[vm(), vm(), anywhere()],
        out_specs=vm(),
        compiler_params=params(),
        cost_estimate=COST,
    )(below, corner, after)


def share_kernel(terms_ref, start_ref, *refs):
    out_ref = refs[-1]
    total = jnp.sum(terms_ref[:, :, :SIDE], axis=0)
    peak = jnp.max(terms_ref[:, :, SIDE:], axis=0)
    for q in range(4):
        lanes = slice(q * QUARTER, (q + 1) * QUARTER)
        value = start_ref[:, lanes] + 0.5 * total[:, lanes] / (peak + 1e-06)
        out_ref[:, :, lanes] = jnp.broadcast_to(value, out_ref.shape[:2] + (QUARTER,))


def shared(terms, start, after):
    count, share, _ = terms.shape
    return pl.pallas_call(
        share_kernel,
        out_shape=jax.ShapeDtypeStruct((count, share, SIDE), F32),
        in_specs=[vm()] * 2 + [anywhere()] * len(after),
        out_specs=vm(),
        compiler_params=params(),
        cost_estimate=COST,
    )(terms, start, *after)


def shifted(value, axis, steps):
    count = lax.axis_size(axis)
    first, last = (max(0, -steps), min(count, count - steps))
    return lax.ppermute(value, axis, [(source, source + steps) for source in range(first, last)])


def other_core(value):
    return lax.ppermute(value, "core", [(0, 1), (1, 0)])


def base_kernel(scale_ref, own_ref, t_own_ref, base_ref, token_ref):
    base_ref[...] = own_ref[...] + scale_ref[0, 0] * t_own_ref[...]
    token_ref[...] = jnp.zeros_like(token_ref)


def base(scale, own, t_own):
    rows = pl.BlockSpec((2, QUARTER, SIDE), lambda i: (0, i, 0))
    return pl.pallas_call(
        base_kernel,
        grid=(4,),
        out_shape=(jax.ShapeDtypeStruct(own.shape, F32), jax.ShapeDtypeStruct((8, 128), F32)),
        in_specs=[sm(), rows, rows],
        out_specs=(rows, pl.BlockSpec((8, 128), lambda i: (0, 0))),
        compiler_params=params(),
        cost_estimate=COST,
    )(scale, own, t_own)


def object_kernel(scale_ref, base_ref, left_ref, first_ref, second_ref, out_ref):
    above = jnp.where(pl.program_id(0) < 1, first_ref[...], second_ref[...])
    out_ref[...] = base_ref[...] + scale_ref[0, 0] * (left_ref[...] + above)


def finished_object(scale, start, left, above):
    rows = pl.BlockSpec((2, QUARTER, SIDE), lambda i: (0, i, 0))
    first = pl.BlockSpec((2, QUARTER, SIDE), lambda i: (0, 0, 0))
    second = pl.BlockSpec((2, QUARTER, SIDE), lambda i: (0, jnp.maximum(i, 1) - 1, 0))
    return pl.pallas_call(
        object_kernel,
        grid=(4,),
        out_shape=jax.ShapeDtypeStruct(start.shape, F32),
        in_specs=[sm(), rows, rows, first, second],
        out_specs=rows,
        compiler_params=params(),
        cost_estimate=COST,
    )(scale, start, left, *above)


def probe_kernel(core_ref, mine_ref, other_ref, out_ref):
    core = core_ref[0, 0]
    out_ref[core] = mine_ref[...]
    out_ref[1 - core] = other_ref[...]


def joined(core, mine, other):
    return pl.pallas_call(
        probe_kernel,
        out_shape=jax.ShapeDtypeStruct((2, SIDE, SIDE), F32),
        in_specs=[sm(), vm(), vm()],
        out_specs=vm(),
        compiler_params=params(),
        cost_estimate=COST,
    )(core, mine, other)


def on_device(object_field, probe, amplitudes, positions):
    row, col, core = lax.axis_index(ROW), lax.axis_index(COL), lax.axis_index("core")
    where = jnp.stack(
        [positions[:, 0] - row * SIDE, positions[:, 1] - col * SIDE, jnp.stack([core, row]).astype(jnp.int32)]
    )
    matrices = [jnp.asarray(m) for m in split_matrices()]
    pieces = [object_field[:, first : first + size] for first, size in zip(FIRSTS, SIZES)]
    right = shifted(object_field, COL, -1)
    *rolled, amps, peaks = ready(where, probe, object_field, amplitudes)
    scale = 0.9 / (peaks[1, :1, :1] + 1e-06)
    specs, wrapped, tokens = [], [], []
    for k, piece in enumerate(pieces):
        below = shifted(piece, ROW, -1)
        if k == 3:
            (below,) = tied((below,), tokens[:2])
        corner = shifted(below, COL, -1)
        spec, wrap, token = fore(k, where, object_field, right, below, corner, rolled[k], matrices)
        specs.append(spec)
        wrapped.append(wrap)
        tokens.append(token)
    t_own, t_right, *parts, keep, send = update(
        where, specs, wrapped, rolled, amps, peaks, matrices
    )

    corner = shifted(parts[2], COL, 1)
    half, lower = first_sums(keep, other_core(send), parts[0], corner)
    (corner,) = tied((parts[3],), (half,))
    corner = shifted(corner, COL, 1)
    share = SIDE // 64
    terms = lax.all_to_all(half.reshape(64, share, WIDE), CHIPS, 0, 0)
    from_above = [shifted(lower, ROW, 1)]
    at = lax.axis_index(CHIPS) * share
    start = lax.dynamic_slice(probe, (core, at, jnp.zeros_like(at)), (1, share, SIDE))[0]
    shares = shared(terms, start, [from_above[0], corner])
    lower = lowered(parts[1], corner, shares)
    from_above.append(shifted(lower, ROW, 1))
    (t_right,) = tied((t_right,), (lower,))
    from_left = shifted(t_right, COL, 1)
    mine = lax.all_to_all(shares, CHIPS, 0, 0).reshape(SIDE, SIDE)
    begun, token = base(scale, object_field, t_own)
    (mine,) = tied((mine,), (from_above[1], from_left, token))
    new_probe = joined(core.astype(jnp.int32).reshape(1, 1), mine, other_core(mine))
    new_object = finished_object(scale, begun, from_left, from_above)
    return (new_object, new_probe)


CHIPS = ("y", "x", "z")
ROW = ("y", "x")
COL = ("z", "core")


def solution(mesh):
    chips = jax.sharding.Mesh(mesh.devices.reshape(4, 4, 4, 2), ROW + COL)
    in_specs = (P(None, ROW, COL), P(), P(ROW + COL, None, None), P(ROW + COL, None))
    out_specs = (P(None, ROW, COL), P())
    return jax.shard_map(
        on_device, mesh=chips, in_specs=in_specs, out_specs=out_specs, check_vma=False
    )
```

```python
import functools
import math

import jax
import jax.numpy as jnp
import numpy as np
from jax import lax
from jax.experimental import pallas as pl
from jax.experimental.pallas import tpu as pltpu
from jax.sharding import PartitionSpec as P

SIDE = 512
QUARTER = 128
SIZES = (128,) * 4
FIRSTS = (0, 128, 256, 384)
BACK = (320, 192)
CHUNKS = ((0, 160), (160, 160), (320, 192))
WIDE = SIDE + 128
PIECES = len(SIZES)
COST = pl.CostEstimate(flops=0, bytes_accessed=0, transcendentals=0)
F32 = jnp.float32
BF16 = jnp.bfloat16


def split_matrices():
    k = np.arange(QUARTER)[:, None]
    n = np.arange(QUARTER)[None, :]
    parts = []
    for p in range(4):
        angle = 2.0 * np.pi * (((4 * k + p) * n) % SIDE) / SIDE
        re, im = np.cos(angle) / np.sqrt(SIDE), -np.sin(angle) / np.sqrt(SIDE)
        parts.append(np.block([[re, -im], [im, re]]))
    left = np.stack(parts)
    out = []
    for matrix in (left, np.swapaxes(left, 1, 2)):
        high = matrix.astype(np.float32).astype(jnp.bfloat16)
        low = (matrix - high.astype(np.float64)).astype(np.float32).astype(jnp.bfloat16)
        out += [np.ascontiguousarray(high), np.ascontiguousarray(low)]
    return out


def order_matrix():
    at = np.arange(SIDE)
    matrix = np.zeros((SIDE, SIDE), np.float32)
    matrix[at, (at % 4) * QUARTER + at // 4] = 1.0
    return matrix.astype(jnp.bfloat16)


def split(value):
    high = value.astype(BF16)
    return high, (value - high.astype(F32)).astype(BF16)


def mm(left, right):
    return jnp.dot(left, right, preferred_element_type=F32)


def fold(x, sign):
    (r0, i0), (r1, i1), (r2, i2), (r3, i3) = x
    sr, si, dr, di = r0 + r2, i0 + i2, r0 - r2, i0 - i2
    tr, ti, er, ei = r1 + r3, i1 + i3, r1 - r3, i1 - i3
    first = (dr + ei, di - er)
    second = (dr - ei, di + er)
    if sign > 0:
        first, second = second, first
    return [(sr + tr, si + ti), first, (sr - tr, si - ti), second]


def ready_kernel(
    where_ref, probe_ref, own_ref, amp_ref, order_ref, *refs
):
    rolled_refs = refs[:PIECES]
    amps_ref, peaks_ref, columns = refs[PIECES:]
    for item in range(2):
        down, along = where_ref[0, item], where_ref[1, item]
        for part in range(2):
            value = pltpu.roll(probe_ref[part], down, 0)
            value = pltpu.roll(value, along, 1)
            for ref, first, size in zip(rolled_refs, FIRSTS, SIZES):
                ref[item, part] = value[first : first + size]
        rows = amp_ref[item]
        high = rows.astype(BF16)
        rest = rows - high.astype(F32)
        middle = rest.astype(BF16)
        low = (rest - middle.astype(F32)).astype(BF16)
        order = order_ref[...]
        moved = mm(high, order) + mm(middle, order) + mm(low, order)
        for q in range(4):
            lanes = slice(q * QUARTER, (q + 1) * QUARTER)
            columns[q] = moved[:, lanes]
            for p in range(4):
                amps_ref[item, p * QUARTER : (p + 1) * QUARTER, lanes] = columns[
                    q, pl.ds(p, QUARTER, stride=4), :
                ]
    own = own_ref[0] ** 2 + own_ref[1] ** 2
    beam = probe_ref[0] ** 2 + probe_ref[1] ** 2
    peaks_ref[0] = jnp.full((8, 128), jnp.max(own), F32)
    peaks_ref[1] = jnp.full((8, 128), jnp.max(beam), F32)


def fore_kernel(
    piece, where_ref, own_ref, right_ref, below_ref, diag_ref, rolled_ref, mh_ref, ml_ref,
    spec_ref, wrapped_ref, token_ref,
):
    token_ref[...] = jnp.zeros_like(token_ref)
    lane = lax.broadcasted_iota(jnp.int32, (SIZES[piece], SIDE), 1)
    row = lax.broadcasted_iota(jnp.int32, (SIZES[piece], SIDE), 0) + FIRSTS[piece]
    for item in range(2):
        down, along = where_ref[0, item], where_ref[1, item]
        above, beside = row < down, lane < along
        value = []
        for part in range(2):
            lower = jnp.where(beside, diag_ref[part], below_ref[part])
            upper = jnp.where(beside, right_ref[part], own_ref[part])
            value.append(jnp.where(above, lower, upper))
            wrapped_ref[item, part] = value[part]
        beam_r, beam_i = rolled_ref[item, 0], rolled_ref[item, 1]
        psi_r = beam_r * value[0] - beam_i * value[1]
        psi_i = beam_r * value[1] + beam_i * value[0]
        blocks = [
            (psi_r[:, q * QUARTER : (q + 1) * QUARTER], psi_i[:, q * QUARTER : (q + 1) * QUARTER])
            for q in range(4)
        ]
        for p, (br, bi) in enumerate(fold(blocks, -1)):
            hi, lo = split(jnp.concatenate([br, bi], axis=1))
            out = mm(hi, mh_ref[p]) + mm(lo, mh_ref[p]) + mm(hi, ml_ref[p])
            spec_ref[item, 0, :, p * QUARTER : (p + 1) * QUARTER] = out[:, :QUARTER]
            spec_ref[item, 1, :, p * QUARTER : (p + 1) * QUARTER] = out[:, QUARTER:]


def fore(piece, where, own, right, below, diag, rolled, matrices):
    size = SIZES[piece]
    tile = pl.BlockSpec((2, size, SIDE), lambda i: (0, piece, 0))
    full = pl.BlockSpec((2, size, SIDE), lambda i: (0, 0, 0))
    whole = pl.BlockSpec((4, 2 * QUARTER, 2 * QUARTER), lambda i: (0, 0, 0))
    four = pl.BlockSpec((2, 2, size, SIDE), lambda i: (0, 0, 0, 0))
    shape = jax.ShapeDtypeStruct((2, 2, size, SIDE), F32)
    return pl.pallas_call(
        functools.partial(fore_kernel, piece),
        grid=(1,),
        out_shape=[shape, shape, jax.ShapeDtypeStruct((8, 128), F32)],
        in_specs=[sm(), tile, tile, full, full, four, whole, whole],
        out_specs=[four, four, pl.BlockSpec((8, 128), lambda i: (0, 0))],
        compiler_params=params(20),
        cost_estimate=COST,
    )(where, own, right, below, diag, rolled, *matrices[2:])


def rows_of(refs, item, part, first, last, lanes=slice(None)):
    values = []
    for ref, start, size in zip(refs, FIRSTS, SIZES):
        low, high = max(first, start) - start, min(last, start + size) - start
        if low < high:
            values.append(ref[item, part, low:high, lanes])
    return values[0] if len(values) == 1 else jnp.concatenate(values, axis=0)


def update_kernel(where_ref, *refs):
    spec_refs, wrapped_refs, rolled_refs = refs[:PIECES], refs[PIECES : 2 * PIECES], refs[2 * PIECES : 3 * PIECES]
    amps_ref, peaks_ref, lh_ref, ll_ref, mh_ref, ml_ref = refs[3 * PIECES : 3 * PIECES + 6]
    outs = refs[3 * PIECES + 6 :]
    targets, keep_ref, send_ref = outs[:6], outs[6], outs[7]
    high, low, grad, terms, out_sems = outs[8:]
    core = where_ref[2, 0]

    wide = 2 * QUARTER
    for item in range(2):
        for chunk in range(SIDE // wide):
            cols = slice(chunk * wide, (chunk + 1) * wide)
            blocks = [
                tuple(
                    rows_of(spec_refs, item, part, q * QUARTER, (q + 1) * QUARTER, cols)
                    for part in range(2)
                )
                for q in range(4)
            ]
            back = []
            for p, (br, bi) in enumerate(fold(blocks, -1)):
                hi, lo = split(jnp.concatenate([br, bi], axis=0))
                out = mm(lh_ref[p], hi) + mm(lh_ref[p], lo) + mm(ll_ref[p], hi)
                sr, si = out[:QUARTER], out[QUARTER:]
                factor = amps_ref[item, p * QUARTER : (p + 1) * QUARTER, cols] * lax.rsqrt(
                    sr * sr + si * si + 0.25
                )
                hi, lo = split(jnp.concatenate([sr * factor, si * factor], axis=0))
                out = mm(mh_ref[p], hi) + mm(mh_ref[p], lo) + mm(ml_ref[p], hi)
                back.append((out[:QUARTER], out[QUARTER:]))
            for q, (xr, xi) in enumerate(fold(back, 1)):
                rows = slice(q * QUARTER, (q + 1) * QUARTER)
                for part, value in enumerate((xr, xi)):
                    hi, lo = split(value)
                    for half in range(2):
                        p = 2 * chunk + half
                        to = slice(p * wide + part * QUARTER, p * wide + (part + 1) * QUARTER)
                        piece = slice(half * QUARTER, (half + 1) * QUARTER)
                        high[item, rows, to] = hi[:, piece]
                        low[item, rows, to] = lo[:, piece]

    stores = []
    for first, size in CHUNKS:
        at = slice(first, first + size)
        lane = lax.broadcasted_iota(jnp.int32, (size, SIDE), 1)
        row = lax.broadcasted_iota(jnp.int32, (size, SIDE), 0) + first
        for item in range(2):
            down, along = where_ref[0, item], where_ref[1, item]
            above, beside = row < down, lane < along
            back = []
            for p in range(4):
                cols = slice(p * wide, (p + 1) * wide)
                hi, lo = high[item, at, cols], low[item, at, cols]
                out = mm(hi, lh_ref[p]) + mm(lo, lh_ref[p]) + mm(hi, ll_ref[p])
                back.append((out[:, :QUARTER], out[:, QUARTER:]))
            back = fold(back, 1)
            back_r = jnp.concatenate([b[0] for b in back], axis=1)
            back_i = jnp.concatenate([b[1] for b in back], axis=1)
            beam_r, beam_i = (rows_of(rolled_refs, item, part, first, first + size) for part in range(2))
            patch_r, patch_i = (rows_of(wrapped_refs, item, part, first, first + size) for part in range(2))
            diff_r = back_r - (beam_r * patch_r - beam_i * patch_i)
            diff_i = back_i - (beam_r * patch_i + beam_i * patch_r)
            term = (beam_r * diff_r + beam_i * diff_i, beam_r * diff_i - beam_i * diff_r)
            grad[item, 0, at, :] = patch_r * diff_r + patch_i * diff_i
            grad[item, 1, at, :] = patch_r * diff_i - patch_i * diff_r
            for part in range(2):
                zero = jnp.zeros_like(term[part])
                upper = jnp.where(above, zero, term[part])
                lower = jnp.where(above, term[part], zero)
                four = (
                    jnp.where(beside, zero, upper),
                    jnp.where(beside, upper, zero),
                    jnp.where(beside, zero, lower),
                    jnp.where(beside, lower, zero),
                )
                for k, value in enumerate(four):
                    if item == 0:
                        terms[k, part, at] = value
                    else:
                        terms[k, part, at] += value
        half = int(first >= BACK[0])
        within = slice(first - half * BACK[0], first - half * BACK[0] + size)
        parts = (
            targets[0].at[:, at],
            targets[1].at[:, at],
            targets[2 + half].at[:, within],
            targets[4 + half].at[:, within],
        )
        for k, target in enumerate(parts):
            store = pltpu.make_async_copy(terms.at[k, :, at], target, out_sems.at[len(stores)])
            store.start()
            stores.append(store)
    whole = []
    for part in range(2):
        total = None
        for item in range(2):
            down, along = where_ref[0, item], where_ref[1, item]
            value = pltpu.roll(grad[item, part], (SIDE - down) % SIDE, 0)
            value = pltpu.roll(value, (SIDE - along) % SIDE, 1)
            total = value if total is None else total + value
        whole.append(total)
    keep_ref[:, :SIDE] = jnp.where(core == 0, whole[0], whole[1])
    send_ref[:, :SIDE] = jnp.where(core == 0, whole[1], whole[0])
    peak = jnp.broadcast_to(peaks_ref[0, :1, :], (SIDE, 128))
    keep_ref[:, SIDE:] = peak
    send_ref[:, SIDE:] = peak
    for store in stores:
        store.wait()


def vm():
    return pl.BlockSpec(memory_space=pltpu.VMEM)


def sm():
    return pl.BlockSpec(memory_space=pltpu.SMEM)


def anywhere():
    return pl.BlockSpec(memory_space=pl.ANY)


def params(mebibytes=16):
    return pltpu.CompilerParams(vmem_limit_bytes=mebibytes * 2**20)


def ready(where, probe, own, amplitudes):
    return pl.pallas_call(
        ready_kernel,
        out_shape=tuple(jax.ShapeDtypeStruct((2, 2, size, SIDE), F32) for size in SIZES)
        + (
            jax.ShapeDtypeStruct((2, SIDE, SIDE), F32),
            jax.ShapeDtypeStruct((2, 8, 128), F32),
        ),
        in_specs=[sm()] + [vm()] * 4,
        out_specs=(vm(),) * (PIECES + 2),
        scratch_shapes=[pltpu.VMEM((4, SIDE, QUARTER), F32)],
        compiler_params=params(32),
        cost_estimate=COST,
    )(where, probe, own, amplitudes, jnp.asarray(order_matrix()))


def update(where, specs, wrapped, rolled, amps, peaks, matrices):
    full = jax.ShapeDtypeStruct((2, SIDE, SIDE), F32)
    plane = jax.ShapeDtypeStruct((SIDE, WIDE), F32)
    parts = tuple(jax.ShapeDtypeStruct((2, size, SIDE), F32) for size in BACK)
    out_shape = (full,) * 2 + parts * 2 + (plane, plane)
    four = pltpu.VMEM((2, 2, SIDE, SIDE), F32)
    half = pltpu.VMEM((2, SIDE, 2 * SIDE), BF16)
    return pl.pallas_call(
        update_kernel,
        out_shape=out_shape,
        in_specs=[sm()] + [vm()] * (3 * PIECES + 6),
        out_specs=(anywhere(),) * 6 + (vm(), vm()),
        scratch_shapes=[
            half,
            half,
            four,
            pltpu.VMEM((4, 2, SIDE, SIDE), F32),
            pltpu.SemaphoreType.DMA((4 * len(CHUNKS),)),
        ],
        compiler_params=params(36),
        cost_estimate=COST,
    )(where, *specs, *wrapped, *rolled, amps, peaks, *matrices)


def nothing_kernel(*refs):
    del refs


def tied(values, after):
    count = len(values) + len(after)
    return pl.pallas_call(
        nothing_kernel,
        out_shape=[jax.ShapeDtypeStruct(v.shape, v.dtype) for v in values],
        in_specs=[anywhere()] * count,
        out_specs=[anywhere()] * len(values),
        input_output_aliases={k: k for k in range(len(values))},
        cost_estimate=COST,
    )(*values, *after)


def first_kernel(keep_ref, came_ref, below_ref, corner_ref, half_ref, lower_ref):
    half_ref[:, :SIDE] = keep_ref[:, :SIDE] + came_ref[:, :SIDE]
    half_ref[:, SIDE:] = jnp.maximum(keep_ref[:, SIDE:], came_ref[:, SIDE:])
    lower_ref[...] = below_ref[...] + corner_ref[...]


def first_sums(keep, came, below, corner):
    return pl.pallas_call(
        first_kernel,
        out_shape=(jax.ShapeDtypeStruct(keep.shape, F32), jax.ShapeDtypeStruct(below.shape, F32)),
        in_specs=[vm()] * 4,
        out_specs=(vm(), vm()),
        compiler_params=params(),
        cost_estimate=COST,
    )(keep, came, below, corner)


def lower_kernel(below_ref, corner_ref, after_ref, lower_ref):
    del after_ref
    lower_ref[...] = below_ref[...] + corner_ref[...]


def lowered(below, corner, after):
    return pl.pallas_call(
        lower_kernel,
        out_shape=jax.ShapeDtypeStruct(below.shape, F32),
        in_specs=[vm(), vm(), anywhere()],
        out_specs=vm(),
        compiler_params=params(),
        cost_estimate=COST,
    )(below, corner, after)


def share_kernel(terms_ref, start_ref, *refs):
    out_ref = refs[-1]
    total = jnp.sum(terms_ref[:, :, :SIDE], axis=0)
    peak = jnp.max(terms_ref[:, :, SIDE:], axis=0)
    for q in range(4):
        lanes = slice(q * QUARTER, (q + 1) * QUARTER)
        value = start_ref[:, lanes] + 0.5 * total[:, lanes] / (peak + 1e-06)
        out_ref[:, :, lanes] = jnp.broadcast_to(value, out_ref.shape[:2] + (QUARTER,))


def shared(terms, start, after):
    count, share, _ = terms.shape
    return pl.pallas_call(
        share_kernel,
        out_shape=jax.ShapeDtypeStruct((count, share, SIDE), F32),
        in_specs=[vm()] * 2 + [anywhere()] * len(after),
        out_specs=vm(),
        compiler_params=params(),
        cost_estimate=COST,
    )(terms, start, *after)


def shifted(value, axis, steps):
    count = lax.axis_size(axis)
    first, last = (max(0, -steps), min(count, count - steps))
    return lax.ppermute(value, axis, [(source, source + steps) for source in range(first, last)])


def other_core(value):
    return lax.ppermute(value, "core", [(0, 1), (1, 0)])


def base_kernel(scale_ref, own_ref, t_own_ref, base_ref, token_ref):
    base_ref[...] = own_ref[...] + scale_ref[0, 0] * t_own_ref[...]
    token_ref[...] = jnp.zeros_like(token_ref)


def base(scale, own, t_own):
    rows = pl.BlockSpec((2, QUARTER, SIDE), lambda i: (0, i, 0))
    return pl.pallas_call(
        base_kernel,
        grid=(4,),
        out_shape=(jax.ShapeDtypeStruct(own.shape, F32), jax.ShapeDtypeStruct((8, 128), F32)),
        in_specs=[sm(), rows, rows],
        out_specs=(rows, pl.BlockSpec((8, 128), lambda i: (0, 0))),
        compiler_params=params(),
        cost_estimate=COST,
    )(scale, own, t_own)


def object_kernel(scale_ref, base_ref, left_ref, *refs):
    out_ref, first = refs[-1], 0
    for ref, size in zip(refs, BACK):
        at = slice(first, first + size)
        out_ref[at] = base_ref[at] + scale_ref[0, 0] * (left_ref[at] + ref[...])
        first += size


def finished_object(scale, start, left, above):
    parts = [pl.BlockSpec((None, size, SIDE), lambda i: (i, 0, 0)) for size in (SIDE, SIDE) + BACK]
    return pl.pallas_call(
        object_kernel,
        grid=(2,),
        out_shape=jax.ShapeDtypeStruct(start.shape, F32),
        in_specs=[sm()] + parts,
        out_specs=parts[0],
        compiler_params=params(),
        cost_estimate=COST,
    )(scale, start, left, *above)


def probe_kernel(core_ref, mine_ref, other_ref, out_ref):
    core = core_ref[0, 0]
    out_ref[core] = mine_ref[...]
    out_ref[1 - core] = other_ref[...]


def joined(core, mine, other):
    return pl.pallas_call(
        probe_kernel,
        out_shape=jax.ShapeDtypeStruct((2, SIDE, SIDE), F32),
        in_specs=[sm(), vm(), vm()],
        out_specs=vm(),
        compiler_params=params(),
        cost_estimate=COST,
    )(core, mine, other)


def on_device(object_field, probe, amplitudes, positions):
    row, col, core = lax.axis_index(ROW), lax.axis_index(COL), lax.axis_index("core")
    where = jnp.stack(
        [positions[:, 0] - row * SIDE, positions[:, 1] - col * SIDE, jnp.stack([core, row]).astype(jnp.int32)]
    )
    matrices = [jnp.asarray(m) for m in split_matrices()]
    pieces = [object_field[:, first : first + size] for first, size in zip(FIRSTS, SIZES)]
    right = shifted(object_field, COL, -1)
    *rolled, amps, peaks = ready(where, probe, object_field, amplitudes)
    scale = 0.9 / (peaks[1, :1, :1] + 1e-06)
    specs, wrapped, tokens = [], [], []
    for k, piece in enumerate(pieces):
        below = shifted(piece, ROW, -1)
        if k == 3:
            (below,) = tied((below,), (peaks,))
        corner = shifted(below, COL, -1)
        spec, wrap, token = fore(k, where, object_field, right, below, corner, rolled[k], matrices)
        specs.append(spec)
        wrapped.append(wrap)
        tokens.append(token)
    t_own, t_right, *parts, keep, send = update(
        where, specs, wrapped, rolled, amps, peaks, matrices
    )

    corner = shifted(parts[2], COL, 1)
    half, lower = first_sums(keep, other_core(send), parts[0], corner)
    (corner,) = tied((parts[3],), (half,))
    corner = shifted(corner, COL, 1)
    share = SIDE // 64
    terms = lax.all_to_all(half.reshape(64, share, WIDE), CHIPS, 0, 0)
    from_above = [shifted(lower, ROW, 1)]
    at = lax.axis_index(CHIPS) * share
    start = lax.dynamic_slice(probe, (core, at, jnp.zeros_like(at)), (1, share, SIDE))[0]
    shares = shared(terms, start, [from_above[0], corner])
    lower = lowered(parts[1], corner, shares)
    from_above.append(shifted(lower, ROW, 1))
    (t_right,) = tied((t_right,), (lower,))
    from_left = shifted(t_right, COL, 1)
    mine = lax.all_to_all(shares, CHIPS, 0, 0).reshape(SIDE, SIDE)
    begun, token = base(scale, object_field, t_own)
    (mine,) = tied((mine,), (from_above[1], from_left, token))
    new_probe = joined(core.astype(jnp.int32).reshape(1, 1), mine, other_core(mine))
    new_object = finished_object(scale, begun, from_left, from_above)
    return (new_object, new_probe)


CHIPS = ("y", "x", "z")
ROW = ("y", "x")
COL = ("z", "core")


def solution(mesh):
    chips = jax.sharding.Mesh(mesh.devices.reshape(4, 4, 4, 2), ROW + COL)
    in_specs = (P(None, ROW, COL), P(), P(ROW + COL, None, None), P(ROW + COL, None))
    out_specs = (P(None, ROW, COL), P())
    return jax.shard_map(
        on_device, mesh=chips, in_specs=in_specs, out_specs=out_specs, check_vma=False
    )
```

```python
import functools
import math

import jax
import jax.numpy as jnp
import numpy as np
from jax import lax
from jax.experimental import pallas as pl
from jax.experimental.pallas import tpu as pltpu
from jax.sharding import PartitionSpec as P

SIDE = 512
QUARTER = 128
SIZES = (128,) * 4
FIRSTS = (0, 128, 256, 384)
WIDE = SIDE + 128
PIECES = len(SIZES)
COST = pl.CostEstimate(flops=0, bytes_accessed=0, transcendentals=0)
F32 = jnp.float32
BF16 = jnp.bfloat16


def split_matrices():
    k = np.arange(QUARTER)[:, None]
    n = np.arange(QUARTER)[None, :]
    parts = []
    for p in range(4):
        angle = 2.0 * np.pi * (((4 * k + p) * n) % SIDE) / SIDE
        re, im = np.cos(angle) / np.sqrt(SIDE), -np.sin(angle) / np.sqrt(SIDE)
        parts.append(np.block([[re, -im], [im, re]]))
    left = np.stack(parts)
    out = []
    for matrix in (left, np.swapaxes(left, 1, 2)):
        high = matrix.astype(np.float32).astype(jnp.bfloat16)
        low = (matrix - high.astype(np.float64)).astype(np.float32).astype(jnp.bfloat16)
        out += [np.ascontiguousarray(high), np.ascontiguousarray(low)]
    return out


def order_matrix():
    at = np.arange(SIDE)
    matrix = np.zeros((SIDE, SIDE), np.float32)
    matrix[at, (at % 4) * QUARTER + at // 4] = 1.0
    return matrix.astype(jnp.bfloat16)


def split(value):
    high = value.astype(BF16)
    return high, (value - high.astype(F32)).astype(BF16)


def mm(left, right):
    return jnp.dot(left, right, preferred_element_type=F32)


def fold(x, sign):
    (r0, i0), (r1, i1), (r2, i2), (r3, i3) = x
    sr, si, dr, di = r0 + r2, i0 + i2, r0 - r2, i0 - i2
    tr, ti, er, ei = r1 + r3, i1 + i3, r1 - r3, i1 - i3
    first = (dr + ei, di - er)
    second = (dr - ei, di + er)
    if sign > 0:
        first, second = second, first
    return [(sr + tr, si + ti), first, (sr - tr, si - ti), second]


def ready_kernel(
    where_ref, probe_ref, own_ref, amp_ref, order_ref, *refs
):
    rolled_refs = refs[:PIECES]
    amps_ref, peaks_ref, columns = refs[PIECES:]
    for item in range(2):
        down, along = where_ref[0, item], where_ref[1, item]
        for part in range(2):
            value = pltpu.roll(probe_ref[part], down, 0)
            value = pltpu.roll(value, along, 1)
            for ref, first, size in zip(rolled_refs, FIRSTS, SIZES):
                ref[item, part] = value[first : first + size]
        rows = amp_ref[item]
        high = rows.astype(BF16)
        rest = rows - high.astype(F32)
        middle = rest.astype(BF16)
        low = (rest - middle.astype(F32)).astype(BF16)
        order = order_ref[...]
        moved = mm(high, order) + mm(middle, order) + mm(low, order)
        for q in range(4):
            lanes = slice(q * QUARTER, (q + 1) * QUARTER)
            columns[q] = moved[:, lanes]
            for p in range(4):
                amps_ref[item, p * QUARTER : (p + 1) * QUARTER, lanes] = columns[
                    q, pl.ds(p, QUARTER, stride=4), :
                ]
    own = own_ref[0] ** 2 + own_ref[1] ** 2
    beam = probe_ref[0] ** 2 + probe_ref[1] ** 2
    peaks_ref[0] = jnp.full((8, 128), jnp.max(own), F32)
    peaks_ref[1] = jnp.full((8, 128), jnp.max(beam), F32)


def fore_kernel(
    piece, where_ref, own_ref, right_ref, below_ref, diag_ref, rolled_ref, mh_ref, ml_ref,
    spec_ref, wrapped_ref, token_ref,
):
    token_ref[...] = jnp.zeros_like(token_ref)
    lane = lax.broadcasted_iota(jnp.int32, (SIZES[piece], SIDE), 1)
    row = lax.broadcasted_iota(jnp.int32, (SIZES[piece], SIDE), 0) + FIRSTS[piece]
    for item in range(2):
        down, along = where_ref[0, item], where_ref[1, item]
        above, beside = row < down, lane < along
        value = []
        for part in range(2):
            lower = jnp.where(beside, diag_ref[part], below_ref[part])
            upper = jnp.where(beside, right_ref[part], own_ref[part])
            value.append(jnp.where(above, lower, upper))
            wrapped_ref[item, part] = value[part]
        beam_r, beam_i = rolled_ref[item, 0], rolled_ref[item, 1]
        psi_r = beam_r * value[0] - beam_i * value[1]
        psi_i = beam_r * value[1] + beam_i * value[0]
        blocks = [
            (psi_r[:, q * QUARTER : (q + 1) * QUARTER], psi_i[:, q * QUARTER : (q + 1) * QUARTER])
            for q in range(4)
        ]
        for p, (br, bi) in enumerate(fold(blocks, -1)):
            hi, lo = split(jnp.concatenate([br, bi], axis=1))
            out = mm(hi, mh_ref[p]) + mm(lo, mh_ref[p]) + mm(hi, ml_ref[p])
            spec_ref[item, 0, :, p * QUARTER : (p + 1) * QUARTER] = out[:, :QUARTER]
            spec_ref[item, 1, :, p * QUARTER : (p + 1) * QUARTER] = out[:, QUARTER:]


def fore(piece, where, own, right, below, diag, rolled, matrices):
    size = SIZES[piece]
    tile = pl.BlockSpec((2, size, SIDE), lambda i: (0, piece, 0))
    full = pl.BlockSpec((2, size, SIDE), lambda i: (0, 0, 0))
    whole = pl.BlockSpec((4, 2 * QUARTER, 2 * QUARTER), lambda i: (0, 0, 0))
    four = pl.BlockSpec((2, 2, size, SIDE), lambda i: (0, 0, 0, 0))
    shape = jax.ShapeDtypeStruct((2, 2, size, SIDE), F32)
    return pl.pallas_call(
        functools.partial(fore_kernel, piece),
        grid=(1,),
        out_shape=[shape, shape, jax.ShapeDtypeStruct((8, 128), F32)],
        in_specs=[sm(), tile, tile, full, full, four, whole, whole],
        out_specs=[four, four, pl.BlockSpec((8, 128), lambda i: (0, 0))],
        compiler_params=params(20),
        cost_estimate=COST,
    )(where, own, right, below, diag, rolled, *matrices[2:])


def rows_of(refs, item, part, first, last, lanes=slice(None)):
    values = []
    for ref, start, size in zip(refs, FIRSTS, SIZES):
        low, high = max(first, start) - start, min(last, start + size) - start
        if low < high:
            values.append(ref[item, part, low:high, lanes])
    return values[0] if len(values) == 1 else jnp.concatenate(values, axis=0)


def update_kernel(where_ref, *refs):
    spec_refs, wrapped_refs, rolled_refs = refs[:PIECES], refs[PIECES : 2 * PIECES], refs[2 * PIECES : 3 * PIECES]
    amps_ref, peaks_ref, lh_ref, ll_ref, mh_ref, ml_ref = refs[3 * PIECES : 3 * PIECES + 6]
    outs = refs[3 * PIECES + 6 :]
    targets, keep_ref, send_ref = outs[:4], outs[4], outs[5]
    high, low, grad, terms, out_sems = outs[6:]
    core = where_ref[2, 0]

    wide = 2 * QUARTER
    for item in range(2):
        for chunk in range(SIDE // wide):
            cols = slice(chunk * wide, (chunk + 1) * wide)
            blocks = [
                tuple(
                    rows_of(spec_refs, item, part, q * QUARTER, (q + 1) * QUARTER, cols)
                    for part in range(2)
                )
                for q in range(4)
            ]
            back = []
            for p, (br, bi) in enumerate(fold(blocks, -1)):
                hi, lo = split(jnp.concatenate([br, bi], axis=0))
                out = mm(lh_ref[p], hi) + mm(lh_ref[p], lo) + mm(ll_ref[p], hi)
                sr, si = out[:QUARTER], out[QUARTER:]
                factor = amps_ref[item, p * QUARTER : (p + 1) * QUARTER, cols] * lax.rsqrt(
                    sr * sr + si * si + 0.25
                )
                hi, lo = split(jnp.concatenate([sr * factor, si * factor], axis=0))
                out = mm(mh_ref[p], hi) + mm(mh_ref[p], lo) + mm(ml_ref[p], hi)
                back.append((out[:QUARTER], out[QUARTER:]))
            for q, (xr, xi) in enumerate(fold(back, 1)):
                rows = slice(q * QUARTER, (q + 1) * QUARTER)
                for part, value in enumerate((xr, xi)):
                    hi, lo = split(value)
                    for half in range(2):
                        p = 2 * chunk + half
                        to = slice(p * wide + part * QUARTER, p * wide + (part + 1) * QUARTER)
                        piece = slice(half * QUARTER, (half + 1) * QUARTER)
                        high[item, rows, to] = hi[:, piece]
                        low[item, rows, to] = lo[:, piece]

    stores = []
    for first, size in zip(FIRSTS, SIZES):
        at = slice(first, first + size)
        lane = lax.broadcasted_iota(jnp.int32, (size, SIDE), 1)
        row = lax.broadcasted_iota(jnp.int32, (size, SIDE), 0) + first
        for item in range(2):
            down, along = where_ref[0, item], where_ref[1, item]
            above, beside = row < down, lane < along
            back = []
            for p in range(4):
                cols = slice(p * wide, (p + 1) * wide)
                hi, lo = high[item, at, cols], low[item, at, cols]
                out = mm(hi, lh_ref[p]) + mm(lo, lh_ref[p]) + mm(hi, ll_ref[p])
                back.append((out[:, :QUARTER], out[:, QUARTER:]))
            back = fold(back, 1)
            back_r = jnp.concatenate([b[0] for b in back], axis=1)
            back_i = jnp.concatenate([b[1] for b in back], axis=1)
            beam_r, beam_i = (rows_of(rolled_refs, item, part, first, first + size) for part in range(2))
            patch_r, patch_i = (rows_of(wrapped_refs, item, part, first, first + size) for part in range(2))
            diff_r = back_r - (beam_r * patch_r - beam_i * patch_i)
            diff_i = back_i - (beam_r * patch_i + beam_i * patch_r)
            term = (beam_r * diff_r + beam_i * diff_i, beam_r * diff_i - beam_i * diff_r)
            grad[item, 0, at, :] = patch_r * diff_r + patch_i * diff_i
            grad[item, 1, at, :] = patch_r * diff_i - patch_i * diff_r
            for part in range(2):
                zero = jnp.zeros_like(term[part])
                upper = jnp.where(above, zero, term[part])
                lower = jnp.where(above, term[part], zero)
                four = (
                    jnp.where(beside, zero, upper),
                    jnp.where(beside, upper, zero),
                    jnp.where(beside, zero, lower),
                    jnp.where(beside, lower, zero),
                )
                for k, value in enumerate(four):
                    if item == 0:
                        terms[k, part, at] = value
                    else:
                        terms[k, part, at] += value
        for k, target in enumerate(targets):
            store = pltpu.make_async_copy(terms.at[k, :, at], target.at[:, at], out_sems.at[len(stores)])
            store.start()
            stores.append(store)
    whole = []
    for part in range(2):
        total = None
        for item in range(2):
            down, along = where_ref[0, item], where_ref[1, item]
            value = pltpu.roll(grad[item, part], (SIDE - down) % SIDE, 0)
            value = pltpu.roll(value, (SIDE - along) % SIDE, 1)
            total = value if total is None else total + value
        whole.append(total)
    keep_ref[:, :SIDE] = jnp.where(core == 0, whole[0], whole[1])
    send_ref[:, :SIDE] = jnp.where(core == 0, whole[1], whole[0])
    peak = jnp.broadcast_to(peaks_ref[0, :1, :], (SIDE, 128))
    keep_ref[:, SIDE:] = peak
    send_ref[:, SIDE:] = peak
    for store in stores:
        store.wait()


def vm():
    return pl.BlockSpec(memory_space=pltpu.VMEM)


def sm():
    return pl.BlockSpec(memory_space=pltpu.SMEM)


def anywhere():
    return pl.BlockSpec(memory_space=pl.ANY)


def params(mebibytes=16):
    return pltpu.CompilerParams(vmem_limit_bytes=mebibytes * 2**20)


def ready(where, probe, own, amplitudes):
    return pl.pallas_call(
        ready_kernel,
        out_shape=tuple(jax.ShapeDtypeStruct((2, 2, size, SIDE), F32) for size in SIZES)
        + (
            jax.ShapeDtypeStruct((2, SIDE, SIDE), F32),
            jax.ShapeDtypeStruct((2, 8, 128), F32),
        ),
        in_specs=[sm()] + [vm()] * 4,
        out_specs=(vm(),) * (PIECES + 2),
        scratch_shapes=[pltpu.VMEM((4, SIDE, QUARTER), F32)],
        compiler_params=params(32),
        cost_estimate=COST,
    )(where, probe, own, amplitudes, jnp.asarray(order_matrix()))


def update(where, specs, wrapped, rolled, amps, peaks, matrices):
    full = jax.ShapeDtypeStruct((2, SIDE, SIDE), F32)
    plane = jax.ShapeDtypeStruct((SIDE, WIDE), F32)
    out_shape = (full,) * 4 + (plane, plane)
    four = pltpu.VMEM((2, 2, SIDE, SIDE), F32)
    half = pltpu.VMEM((2, SIDE, 2 * SIDE), BF16)
    return pl.pallas_call(
        update_kernel,
        out_shape=out_shape,
        in_specs=[sm()] + [vm()] * (3 * PIECES + 6),
        out_specs=(anywhere(),) * 4 + (vm(), vm()),
        scratch_shapes=[
            half,
            half,
            four,
            pltpu.VMEM((4, 2, SIDE, SIDE), F32),
            pltpu.SemaphoreType.DMA((4 * PIECES,)),
        ],
        compiler_params=params(36),
        cost_estimate=COST,
    )(where, *specs, *wrapped, *rolled, amps, peaks, *matrices)


def nothing_kernel(*refs):
    del refs


def tied(values, after):
    count = len(values) + len(after)
    return pl.pallas_call(
        nothing_kernel,
        out_shape=[jax.ShapeDtypeStruct(v.shape, v.dtype) for v in values],
        in_specs=[anywhere()] * count,
        out_specs=[anywhere()] * len(values),
        input_output_aliases={k: k for k in range(len(values))},
        cost_estimate=COST,
    )(*values, *after)


def first_kernel(keep_ref, came_ref, half_ref):
    half_ref[:, :SIDE] = keep_ref[:, :SIDE] + came_ref[:, :SIDE]
    half_ref[:, SIDE:] = jnp.maximum(keep_ref[:, SIDE:], came_ref[:, SIDE:])


def first_sum(keep, came):
    return pl.pallas_call(
        first_kernel,
        out_shape=jax.ShapeDtypeStruct(keep.shape, F32),
        in_specs=[vm()] * 2,
        out_specs=vm(),
        compiler_params=params(),
        cost_estimate=COST,
    )(keep, came)


def lower_kernel(below_ref, corner_ref, after_ref, lower_ref):
    del after_ref
    lower_ref[...] = below_ref[...] + corner_ref[...]


def lowered(below, corner, after):
    return pl.pallas_call(
        lower_kernel,
        out_shape=jax.ShapeDtypeStruct(below.shape, F32),
        in_specs=[vm(), vm(), anywhere()],
        out_specs=vm(),
        compiler_params=params(),
        cost_estimate=COST,
    )(below, corner, after)


def middle_kernel(terms_ref, *refs):
    out_ref = refs[-1]
    total = jnp.sum(terms_ref[:, :, :SIDE], axis=0)
    peak = jnp.max(terms_ref[:, :, SIDE:], axis=0)
    out_ref[:, :, :SIDE] = jnp.broadcast_to(total, (out_ref.shape[0],) + total.shape)
    out_ref[:, :, SIDE:] = jnp.broadcast_to(peak, (out_ref.shape[0],) + peak.shape)


def middle(terms, count, after):
    return pl.pallas_call(
        middle_kernel,
        out_shape=jax.ShapeDtypeStruct((count,) + terms.shape[1:], F32),
        in_specs=[vm()] + [anywhere()] * len(after),
        out_specs=vm(),
        compiler_params=params(),
        cost_estimate=COST,
    )(terms, *after)


def share_kernel(terms_ref, start_ref, out_ref):
    total = jnp.sum(terms_ref[:, :, :SIDE], axis=0)
    peak = jnp.max(terms_ref[:, :, SIDE:], axis=0)
    for q in range(4):
        lanes = slice(q * QUARTER, (q + 1) * QUARTER)
        value = start_ref[:, lanes] + 0.5 * total[:, lanes] / (peak + 1e-06)
        out_ref[:, :, lanes] = jnp.broadcast_to(value, out_ref.shape[:2] + (QUARTER,))


def shared(terms, start, count):
    return pl.pallas_call(
        share_kernel,
        out_shape=jax.ShapeDtypeStruct((count,) + start.shape, F32),
        in_specs=[vm()] * 2,
        out_specs=vm(),
        compiler_params=params(),
        cost_estimate=COST,
    )(terms, start)


def shifted(value, axis, steps):
    count = lax.axis_size(axis)
    first, last = (max(0, -steps), min(count, count - steps))
    return lax.ppermute(value, axis, [(source, source + steps) for source in range(first, last)])


def other_core(value):
    return lax.ppermute(value, "core", [(0, 1), (1, 0)])


def base_kernel(scale_ref, own_ref, t_own_ref, base_ref, token_ref):
    base_ref[...] = own_ref[...] + scale_ref[0, 0] * t_own_ref[...]
    token_ref[...] = jnp.zeros_like(token_ref)


def base(scale, own, t_own):
    rows = pl.BlockSpec((2, QUARTER, SIDE), lambda i: (0, i, 0))
    return pl.pallas_call(
        base_kernel,
        grid=(4,),
        out_shape=(jax.ShapeDtypeStruct(own.shape, F32), jax.ShapeDtypeStruct((8, 128), F32)),
        in_specs=[sm(), rows, rows],
        out_specs=(rows, pl.BlockSpec((8, 128), lambda i: (0, 0))),
        compiler_params=params(),
        cost_estimate=COST,
    )(scale, own, t_own)


def object_kernel(scale_ref, base_ref, left_ref, above_ref, out_ref):
    out_ref[...] = base_ref[...] + scale_ref[0, 0] * (left_ref[...] + above_ref[...])


def finished_object(scale, start, left, above):
    rows = pl.BlockSpec((2, QUARTER, SIDE), lambda i: (0, i, 0))
    return pl.pallas_call(
        object_kernel,
        grid=(4,),
        out_shape=jax.ShapeDtypeStruct(start.shape, F32),
        in_specs=[sm()] + [rows] * 3,
        out_specs=rows,
        compiler_params=params(),
        cost_estimate=COST,
    )(scale, start, left, above)


def probe_kernel(core_ref, mine_ref, other_ref, out_ref):
    core = core_ref[0, 0]
    out_ref[core] = mine_ref[...]
    out_ref[1 - core] = other_ref[...]


def joined(core, mine, other):
    return pl.pallas_call(
        probe_kernel,
        out_shape=jax.ShapeDtypeStruct((2, SIDE, SIDE), F32),
        in_specs=[sm(), vm(), vm()],
        out_specs=vm(),
        compiler_params=params(),
        cost_estimate=COST,
    )(core, mine, other)


def on_device(object_field, probe, amplitudes, positions):
    row, col, core = lax.axis_index(ROW), lax.axis_index(COL), lax.axis_index("core")
    where = jnp.stack(
        [positions[:, 0] - row * SIDE, positions[:, 1] - col * SIDE, jnp.stack([core, row]).astype(jnp.int32)]
    )
    matrices = [jnp.asarray(m) for m in split_matrices()]
    pieces = [object_field[:, first : first + size] for first, size in zip(FIRSTS, SIZES)]
    right = shifted(object_field, COL, -1)
    *rolled, amps, peaks = ready(where, probe, object_field, amplitudes)
    scale = 0.9 / (peaks[1, :1, :1] + 1e-06)
    specs, wrapped, tokens = [], [], []
    for k, piece in enumerate(pieces):
        below = shifted(piece, ROW, -1)
        if k in (0, 3):
            (below,) = tied((below,), tokens[:2] if k else (peaks,))
        corner = shifted(below, COL, -1)
        spec, wrap, token = fore(k, where, object_field, right, below, corner, rolled[k], matrices)
        specs.append(spec)
        wrapped.append(wrap)
        tokens.append(token)
    t_own, t_right, t_below, t_corner, keep, send = update(
        where, specs, wrapped, rolled, amps, peaks, matrices
    )

    corner = shifted(t_corner, COL, 1)
    half = first_sum(keep, other_core(send))
    share = SIDE // 16
    terms = lax.all_to_all(half.reshape(16, share, WIDE), SIDES, 0, 0)
    lower = lowered(t_below, corner, half)
    from_above = shifted(lower, ROW, 1)
    terms = middle(terms, 4, (lower,))
    (t_right,) = tied((t_right,), (terms,))
    from_left = shifted(t_right, COL, 1)
    terms = lax.all_to_all(terms, "x", 0, 0)
    at = lax.axis_index(SIDES) * share
    start = lax.dynamic_slice(probe, (core, at, jnp.zeros_like(at)), (1, share, SIDE))[0]
    mine = lax.all_to_all(shared(terms, start, 16), SIDES, 0, 0).reshape(SIDE, SIDE)
    begun, token = base(scale, object_field, t_own)
    (mine,) = tied((mine,), (from_above, from_left, token))
    new_probe = joined(core.astype(jnp.int32).reshape(1, 1), mine, other_core(mine))
    new_object = finished_object(scale, begun, from_left, from_above)
    return (new_object, new_probe)


SIDES = ("y", "z")
ROW = ("y", "x")
COL = ("z", "core")


def solution(mesh):
    chips = jax.sharding.Mesh(mesh.devices.reshape(4, 4, 4, 2), ROW + COL)
    in_specs = (P(None, ROW, COL), P(), P(ROW + COL, None, None), P(ROW + COL, None))
    out_specs = (P(None, ROW, COL), P())
    return jax.shard_map(
        on_device, mesh=chips, in_specs=in_specs, out_specs=out_specs, check_vma=False
    )
```

```python
import functools
import math

import jax
import jax.numpy as jnp
import numpy as np
from jax import lax
from jax.experimental import pallas as pl
from jax.experimental.pallas import tpu as pltpu
from jax.sharding import PartitionSpec as P

SIDE = 512
QUARTER = 128
SIZES = (128,) * 4
FIRSTS = (0, 128, 256, 384)
WIDE = SIDE + 128
PIECES = len(SIZES)
COST = pl.CostEstimate(flops=0, bytes_accessed=0, transcendentals=0)
F32 = jnp.float32
BF16 = jnp.bfloat16


def split_matrices():
    k = np.arange(QUARTER)[:, None]
    n = np.arange(QUARTER)[None, :]
    parts = []
    for p in range(4):
        angle = 2.0 * np.pi * (((4 * k + p) * n) % SIDE) / SIDE
        re, im = np.cos(angle) / np.sqrt(SIDE), -np.sin(angle) / np.sqrt(SIDE)
        parts.append(np.block([[re, -im], [im, re]]))
    left = np.stack(parts)
    out = []
    for matrix in (left, np.swapaxes(left, 1, 2)):
        high = matrix.astype(np.float32).astype(jnp.bfloat16)
        low = (matrix - high.astype(np.float64)).astype(np.float32).astype(jnp.bfloat16)
        out += [np.ascontiguousarray(high), np.ascontiguousarray(low)]
    return out


def order_matrix():
    at = np.arange(SIDE)
    matrix = np.zeros((SIDE, SIDE), np.float32)
    matrix[at, (at % 4) * QUARTER + at // 4] = 1.0
    return matrix.astype(jnp.bfloat16)


def split(value):
    high = value.astype(BF16)
    return high, (value - high.astype(F32)).astype(BF16)


def mm(left, right):
    return jnp.dot(left, right, preferred_element_type=F32)


def fold(x, sign):
    (r0, i0), (r1, i1), (r2, i2), (r3, i3) = x
    sr, si, dr, di = r0 + r2, i0 + i2, r0 - r2, i0 - i2
    tr, ti, er, ei = r1 + r3, i1 + i3, r1 - r3, i1 - i3
    first = (dr + ei, di - er)
    second = (dr - ei, di + er)
    if sign > 0:
        first, second = second, first
    return [(sr + tr, si + ti), first, (sr - tr, si - ti), second]


def ready_kernel(
    where_ref, probe_ref, own_ref, amp_ref, order_ref, *refs
):
    rolled_refs = refs[:PIECES]
    amps_ref, peaks_ref, columns = refs[PIECES:]
    for item in range(2):
        down, along = where_ref[0, item], where_ref[1, item]
        for part in range(2):
            value = pltpu.roll(probe_ref[part], down, 0)
            value = pltpu.roll(value, along, 1)
            for ref, first, size in zip(rolled_refs, FIRSTS, SIZES):
                ref[item, part] = value[first : first + size]
        rows = amp_ref[item]
        high = rows.astype(BF16)
        rest = rows - high.astype(F32)
        middle = rest.astype(BF16)
        low = (rest - middle.astype(F32)).astype(BF16)
        order = order_ref[...]
        moved = mm(high, order) + mm(middle, order) + mm(low, order)
        for q in range(4):
            lanes = slice(q * QUARTER, (q + 1) * QUARTER)
            columns[q] = moved[:, lanes]
            for p in range(4):
                amps_ref[item, p * QUARTER : (p + 1) * QUARTER, lanes] = columns[
                    q, pl.ds(p, QUARTER, stride=4), :
                ]
    own = own_ref[0] ** 2 + own_ref[1] ** 2
    beam = probe_ref[0] ** 2 + probe_ref[1] ** 2
    peaks_ref[0] = jnp.full((8, 128), jnp.max(own), F32)
    peaks_ref[1] = jnp.full((8, 128), jnp.max(beam), F32)


def fore_kernel(
    piece, where_ref, own_ref, right_ref, below_ref, diag_ref, rolled_ref, mh_ref, ml_ref,
    spec_ref, wrapped_ref, token_ref,
):
    token_ref[...] = jnp.zeros_like(token_ref)
    lane = lax.broadcasted_iota(jnp.int32, (SIZES[piece], SIDE), 1)
    row = lax.broadcasted_iota(jnp.int32, (SIZES[piece], SIDE), 0) + FIRSTS[piece]
    for item in range(2):
        down, along = where_ref[0, item], where_ref[1, item]
        above, beside = row < down, lane < along
        value = []
        for part in range(2):
            lower = jnp.where(beside, diag_ref[part], below_ref[part])
            upper = jnp.where(beside, right_ref[part], own_ref[part])
            value.append(jnp.where(above, lower, upper))
            wrapped_ref[item, part] = value[part]
        beam_r, beam_i = rolled_ref[item, 0], rolled_ref[item, 1]
        psi_r = beam_r * value[0] - beam_i * value[1]
        psi_i = beam_r * value[1] + beam_i * value[0]
        blocks = [
            (psi_r[:, q * QUARTER : (q + 1) * QUARTER], psi_i[:, q * QUARTER : (q + 1) * QUARTER])
            for q in range(4)
        ]
        for p, (br, bi) in enumerate(fold(blocks, -1)):
            hi, lo = split(jnp.concatenate([br, bi], axis=1))
            out = mm(hi, mh_ref[p]) + mm(lo, mh_ref[p]) + mm(hi, ml_ref[p])
            spec_ref[item, 0, :, p * QUARTER : (p + 1) * QUARTER] = out[:, :QUARTER]
            spec_ref[item, 1, :, p * QUARTER : (p + 1) * QUARTER] = out[:, QUARTER:]


def fore(piece, where, own, right, below, diag, rolled, matrices):
    size = SIZES[piece]
    tile = pl.BlockSpec((2, size, SIDE), lambda i: (0, piece, 0))
    full = pl.BlockSpec((2, size, SIDE), lambda i: (0, 0, 0))
    whole = pl.BlockSpec((4, 2 * QUARTER, 2 * QUARTER), lambda i: (0, 0, 0))
    four = pl.BlockSpec((2, 2, size, SIDE), lambda i: (0, 0, 0, 0))
    shape = jax.ShapeDtypeStruct((2, 2, size, SIDE), F32)
    return pl.pallas_call(
        functools.partial(fore_kernel, piece),
        grid=(1,),
        out_shape=[shape, shape, jax.ShapeDtypeStruct((8, 128), F32)],
        in_specs=[sm(), tile, tile, full, full, four, whole, whole],
        out_specs=[four, four, pl.BlockSpec((8, 128), lambda i: (0, 0))],
        compiler_params=params(20),
        cost_estimate=COST,
    )(where, own, right, below, diag, rolled, *matrices[2:])


def rows_of(refs, item, part, first, last, lanes=slice(None)):
    values = []
    for ref, start, size in zip(refs, FIRSTS, SIZES):
        low, high = max(first, start) - start, min(last, start + size) - start
        if low < high:
            values.append(ref[item, part, low:high, lanes])
    return values[0] if len(values) == 1 else jnp.concatenate(values, axis=0)


def update_kernel(where_ref, *refs):
    spec_refs, wrapped_refs, rolled_refs = refs[:PIECES], refs[PIECES : 2 * PIECES], refs[2 * PIECES : 3 * PIECES]
    amps_ref, peaks_ref, lh_ref, ll_ref, mh_ref, ml_ref = refs[3 * PIECES : 3 * PIECES + 6]
    outs = refs[3 * PIECES + 6 :]
    targets, keep_ref, send_ref = outs[:4], outs[4], outs[5]
    high, low, grad, terms, out_sems = outs[6:]
    core = where_ref[2, 0]

    wide = 2 * QUARTER
    for item in range(2):
        for chunk in range(SIDE // wide):
            cols = slice(chunk * wide, (chunk + 1) * wide)
            blocks = [
                tuple(
                    rows_of(spec_refs, item, part, q * QUARTER, (q + 1) * QUARTER, cols)
                    for part in range(2)
                )
                for q in range(4)
            ]
            back = []
            for p, (br, bi) in enumerate(fold(blocks, -1)):
                hi, lo = split(jnp.concatenate([br, bi], axis=0))
                out = mm(lh_ref[p], hi) + mm(lh_ref[p], lo) + mm(ll_ref[p], hi)
                sr, si = out[:QUARTER], out[QUARTER:]
                factor = amps_ref[item, p * QUARTER : (p + 1) * QUARTER, cols] * lax.rsqrt(
                    sr * sr + si * si + 0.25
                )
                hi, lo = split(jnp.concatenate([sr * factor, si * factor], axis=0))
                out = mm(mh_ref[p], hi) + mm(mh_ref[p], lo) + mm(ml_ref[p], hi)
                back.append((out[:QUARTER], out[QUARTER:]))
            for q, (xr, xi) in enumerate(fold(back, 1)):
                rows = slice(q * QUARTER, (q + 1) * QUARTER)
                for part, value in enumerate((xr, xi)):
                    hi, lo = split(value)
                    for half in range(2):
                        p = 2 * chunk + half
                        to = slice(p * wide + part * QUARTER, p * wide + (part + 1) * QUARTER)
                        piece = slice(half * QUARTER, (half + 1) * QUARTER)
                        high[item, rows, to] = hi[:, piece]
                        low[item, rows, to] = lo[:, piece]

    stores = []
    for first, size in zip(FIRSTS, SIZES):
        at = slice(first, first + size)
        lane = lax.broadcasted_iota(jnp.int32, (size, SIDE), 1)
        row = lax.broadcasted_iota(jnp.int32, (size, SIDE), 0) + first
        for item in range(2):
            down, along = where_ref[0, item], where_ref[1, item]
            above, beside = row < down, lane < along
            back = []
            for p in range(4):
                cols = slice(p * wide, (p + 1) * wide)
                hi, lo = high[item, at, cols], low[item, at, cols]
                out = mm(hi, lh_ref[p]) + mm(lo, lh_ref[p]) + mm(hi, ll_ref[p])
                back.append((out[:, :QUARTER], out[:, QUARTER:]))
            back = fold(back, 1)
            back_r = jnp.concatenate([b[0] for b in back], axis=1)
            back_i = jnp.concatenate([b[1] for b in back], axis=1)
            beam_r, beam_i = (rows_of(rolled_refs, item, part, first, first + size) for part in range(2))
            patch_r, patch_i = (rows_of(wrapped_refs, item, part, first, first + size) for part in range(2))
            diff_r = back_r - (beam_r * patch_r - beam_i * patch_i)
            diff_i = back_i - (beam_r * patch_i + beam_i * patch_r)
            term = (beam_r * diff_r + beam_i * diff_i, beam_r * diff_i - beam_i * diff_r)
            grad[item, 0, at, :] = patch_r * diff_r + patch_i * diff_i
            grad[item, 1, at, :] = patch_r * diff_i - patch_i * diff_r
            for part in range(2):
                zero = jnp.zeros_like(term[part])
                upper = jnp.where(above, zero, term[part])
                lower = jnp.where(above, term[part], zero)
                four = (
                    jnp.where(beside, zero, upper),
                    jnp.where(beside, upper, zero),
                    jnp.where(beside, zero, lower),
                    jnp.where(beside, lower, zero),
                )
                for k, value in enumerate(four):
                    if item == 0:
                        terms[k, part, at] = value
                    else:
                        terms[k, part, at] += value
        for k, target in enumerate(targets):
            store = pltpu.make_async_copy(terms.at[k, :, at], target.at[:, at], out_sems.at[len(stores)])
            store.start()
            stores.append(store)
    whole = []
    for part in range(2):
        total = None
        for item in range(2):
            down, along = where_ref[0, item], where_ref[1, item]
            value = pltpu.roll(grad[item, part], (SIDE - down) % SIDE, 0)
            value = pltpu.roll(value, (SIDE - along) % SIDE, 1)
            total = value if total is None else total + value
        whole.append(total)
    keep_ref[:, :SIDE] = jnp.where(core == 0, whole[0], whole[1])
    send_ref[:, :SIDE] = jnp.where(core == 0, whole[1], whole[0])
    peak = jnp.broadcast_to(peaks_ref[0, :1, :], (SIDE, 128))
    keep_ref[:, SIDE:] = peak
    send_ref[:, SIDE:] = peak
    for store in stores:
        store.wait()


def vm():
    return pl.BlockSpec(memory_space=pltpu.VMEM)


def sm():
    return pl.BlockSpec(memory_space=pltpu.SMEM)


def anywhere():
    return pl.BlockSpec(memory_space=pl.ANY)


def params(mebibytes=16):
    return pltpu.CompilerParams(vmem_limit_bytes=mebibytes * 2**20)


def ready(where, probe, own, amplitudes):
    return pl.pallas_call(
        ready_kernel,
        out_shape=tuple(jax.ShapeDtypeStruct((2, 2, size, SIDE), F32) for size in SIZES)
        + (
            jax.ShapeDtypeStruct((2, SIDE, SIDE), F32),
            jax.ShapeDtypeStruct((2, 8, 128), F32),
        ),
        in_specs=[sm()] + [vm()] * 4,
        out_specs=(vm(),) * (PIECES + 2),
        scratch_shapes=[pltpu.VMEM((4, SIDE, QUARTER), F32)],
        compiler_params=params(32),
        cost_estimate=COST,
    )(where, probe, own, amplitudes, jnp.asarray(order_matrix()))


def update(where, specs, wrapped, rolled, amps, peaks, matrices):
    full = jax.ShapeDtypeStruct((2, SIDE, SIDE), F32)
    plane = jax.ShapeDtypeStruct((SIDE, WIDE), F32)
    out_shape = (full,) * 4 + (plane, plane)
    four = pltpu.VMEM((2, 2, SIDE, SIDE), F32)
    half = pltpu.VMEM((2, SIDE, 2 * SIDE), BF16)
    return pl.pallas_call(
        update_kernel,
        out_shape=out_shape,
        in_specs=[sm()] + [vm()] * (3 * PIECES + 6),
        out_specs=(anywhere(),) * 4 + (vm(), vm()),
        scratch_shapes=[
            half,
            half,
            four,
            pltpu.VMEM((4, 2, SIDE, SIDE), F32),
            pltpu.SemaphoreType.DMA((4 * PIECES,)),
        ],
        compiler_params=params(36),
        cost_estimate=COST,
    )(where, *specs, *wrapped, *rolled, amps, peaks, *matrices)


def nothing_kernel(*refs):
    del refs


def tied(values, after):
    count = len(values) + len(after)
    return pl.pallas_call(
        nothing_kernel,
        out_shape=[jax.ShapeDtypeStruct(v.shape, v.dtype) for v in values],
        in_specs=[anywhere()] * count,
        out_specs=[anywhere()] * len(values),
        input_output_aliases={k: k for k in range(len(values))},
        cost_estimate=COST,
    )(*values, *after)


def first_kernel(keep_ref, came_ref, half_ref):
    half_ref[:, :SIDE] = keep_ref[:, :SIDE] + came_ref[:, :SIDE]
    half_ref[:, SIDE:] = jnp.maximum(keep_ref[:, SIDE:], came_ref[:, SIDE:])


def first_sum(keep, came):
    return pl.pallas_call(
        first_kernel,
        out_shape=jax.ShapeDtypeStruct(keep.shape, F32),
        in_specs=[vm()] * 2,
        out_specs=vm(),
        compiler_params=params(),
        cost_estimate=COST,
    )(keep, came)


def lower_kernel(below_ref, corner_ref, after_ref, lower_ref):
    del after_ref
    lower_ref[...] = below_ref[...] + corner_ref[...]


def lowered(below, corner, after):
    rows = pl.BlockSpec((2, QUARTER, SIDE), lambda i: (0, i, 0))
    return pl.pallas_call(
        lower_kernel,
        grid=(4,),
        out_shape=jax.ShapeDtypeStruct(below.shape, F32),
        in_specs=[rows, rows, anywhere()],
        out_specs=rows,
        compiler_params=params(),
        cost_estimate=COST,
    )(below, corner, after)


def middle_kernel(terms_ref, *refs):
    out_ref = refs[-1]
    total = jnp.sum(terms_ref[:, :, :SIDE], axis=0)
    peak = jnp.max(terms_ref[:, :, SIDE:], axis=0)
    out_ref[:, :, :SIDE] = jnp.broadcast_to(total, (out_ref.shape[0],) + total.shape)
    out_ref[:, :, SIDE:] = jnp.broadcast_to(peak, (out_ref.shape[0],) + peak.shape)


def middle(terms, count, after):
    return pl.pallas_call(
        middle_kernel,
        out_shape=jax.ShapeDtypeStruct((count,) + terms.shape[1:], F32),
        in_specs=[vm()] + [anywhere()] * len(after),
        out_specs=vm(),
        compiler_params=params(),
        cost_estimate=COST,
    )(terms, *after)


def share_kernel(terms_ref, start_ref, out_ref):
    total = jnp.sum(terms_ref[:, :, :SIDE], axis=0)
    peak = jnp.max(terms_ref[:, :, SIDE:], axis=0)
    for q in range(4):
        lanes = slice(q * QUARTER, (q + 1) * QUARTER)
        value = start_ref[:, lanes] + 0.5 * total[:, lanes] / (peak + 1e-06)
        out_ref[:, :, lanes] = jnp.broadcast_to(value, out_ref.shape[:2] + (QUARTER,))


def shared(terms, start, count):
    return pl.pallas_call(
        share_kernel,
        out_shape=jax.ShapeDtypeStruct((count,) + start.shape, F32),
        in_specs=[vm()] * 2,
        out_specs=vm(),
        compiler_params=params(),
        cost_estimate=COST,
    )(terms, start)


def shifted(value, axis, steps):
    count = lax.axis_size(axis)
    first, last = (max(0, -steps), min(count, count - steps))
    return lax.ppermute(value, axis, [(source, source + steps) for source in range(first, last)])


def other_core(value):
    return lax.ppermute(value, "core", [(0, 1), (1, 0)])


def base_kernel(scale_ref, own_ref, t_own_ref, base_ref, token_ref):
    base_ref[...] = own_ref[...] + scale_ref[0, 0] * t_own_ref[...]
    token_ref[...] = jnp.zeros_like(token_ref)


def base(scale, own, t_own):
    rows = pl.BlockSpec((2, QUARTER, SIDE), lambda i: (0, i, 0))
    return pl.pallas_call(
        base_kernel,
        grid=(4,),
        out_shape=(jax.ShapeDtypeStruct(own.shape, F32), jax.ShapeDtypeStruct((8, 128), F32)),
        in_specs=[sm(), rows, rows],
        out_specs=(rows, pl.BlockSpec((8, 128), lambda i: (0, 0))),
        compiler_params=params(),
        cost_estimate=COST,
    )(scale, own, t_own)


def object_kernel(scale_ref, base_ref, left_ref, above_ref, out_ref):
    out_ref[...] = base_ref[...] + scale_ref[0, 0] * (left_ref[...] + above_ref[...])


def finished_object(scale, start, left, above):
    rows = pl.BlockSpec((2, QUARTER, SIDE), lambda i: (0, i, 0))
    return pl.pallas_call(
        object_kernel,
        grid=(4,),
        out_shape=jax.ShapeDtypeStruct(start.shape, F32),
        in_specs=[sm()] + [rows] * 3,
        out_specs=rows,
        compiler_params=params(),
        cost_estimate=COST,
    )(scale, start, left, above)


def probe_kernel(core_ref, mine_ref, other_ref, out_ref):
    core = core_ref[0, 0]
    out_ref[core] = mine_ref[...]
    out_ref[1 - core] = other_ref[...]


def joined(core, mine, other):
    return pl.pallas_call(
        probe_kernel,
        out_shape=jax.ShapeDtypeStruct((2, SIDE, SIDE), F32),
        in_specs=[sm(), vm(), vm()],
        out_specs=vm(),
        compiler_params=params(),
        cost_estimate=COST,
    )(core, mine, other)


def on_device(object_field, probe, amplitudes, positions):
    row, col, core = lax.axis_index(ROW), lax.axis_index(COL), lax.axis_index("core")
    where = jnp.stack(
        [positions[:, 0] - row * SIDE, positions[:, 1] - col * SIDE, jnp.stack([core, row]).astype(jnp.int32)]
    )
    matrices = [jnp.asarray(m) for m in split_matrices()]
    pieces = [object_field[:, first : first + size] for first, size in zip(FIRSTS, SIZES)]
    right = shifted(object_field, COL, -1)
    *rolled, amps, peaks = ready(where, probe, object_field, amplitudes)
    scale = 0.9 / (peaks[1, :1, :1] + 1e-06)
    specs, wrapped, tokens = [], [], []
    for k, piece in enumerate(pieces):
        below = shifted(piece, ROW, -1)
        if k in (0, 3):
            (below,) = tied((below,), tokens[:1] if k else (peaks,))
        corner = shifted(below, COL, -1)
        spec, wrap, token = fore(k, where, object_field, right, below, corner, rolled[k], matrices)
        specs.append(spec)
        wrapped.append(wrap)
        tokens.append(token)
    t_own, t_right, t_below, t_corner, keep, send = update(
        where, specs, wrapped, rolled, amps, peaks, matrices
    )

    corner = shifted(t_corner, COL, 1)
    half = first_sum(keep, other_core(send))
    share = SIDE // 16
    terms = lax.all_to_all(half.reshape(16, share, WIDE), ROW, 0, 0)
    lower = lowered(t_below, corner, half)
    from_above = shifted(lower, ROW, 1)
    (t_right,) = tied((t_right,), (half,))
    from_left = shifted(t_right, COL, 1)
    terms = middle(terms, 4, (lower,))
    terms = lax.all_to_all(terms, "z", 0, 0)
    at = lax.axis_index(ROW) * share
    start = lax.dynamic_slice(probe, (core, at, jnp.zeros_like(at)), (1, share, SIDE))[0]
    shares = shared(terms, start, 16)
    mine = lax.all_to_all(shares, ROW, 0, 0).reshape(SIDE, SIDE)
    begun, token = base(scale, object_field, t_own)
    (mine,) = tied((mine,), (from_above, from_left, token))
    new_probe = joined(core.astype(jnp.int32).reshape(1, 1), mine, other_core(mine))
    new_object = finished_object(scale, begun, from_left, from_above)
    return (new_object, new_probe)


ROW = ("y", "x")
COL = ("z", "core")


def solution(mesh):
    chips = jax.sharding.Mesh(mesh.devices.reshape(4, 4, 4, 2), ROW + COL)
    in_specs = (P(None, ROW, COL), P(), P(ROW + COL, None, None), P(ROW + COL, None))
    out_specs = (P(None, ROW, COL), P())
    return jax.shard_map(
        on_device, mesh=chips, in_specs=in_specs, out_specs=out_specs, check_vma=False
    )
```

```python
import functools
import math

import jax
import jax.numpy as jnp
import numpy as np
from jax import lax
from jax.experimental import pallas as pl
from jax.experimental.pallas import tpu as pltpu
from jax.sharding import PartitionSpec as P

SIDE = 512
QUARTER = 128
SIZES = (144, 144, 128, 96)
FIRSTS = (0, 144, 288, 416)
WIDE = SIDE + 128
PIECES = len(SIZES)
COST = pl.CostEstimate(flops=0, bytes_accessed=0, transcendentals=0)
F32 = jnp.float32
BF16 = jnp.bfloat16


def split_matrices():
    k = np.arange(QUARTER)[:, None]
    n = np.arange(QUARTER)[None, :]
    parts = []
    for p in range(4):
        angle = 2.0 * np.pi * (((4 * k + p) * n) % SIDE) / SIDE
        re, im = np.cos(angle) / np.sqrt(SIDE), -np.sin(angle) / np.sqrt(SIDE)
        parts.append(np.block([[re, -im], [im, re]]))
    left = np.stack(parts)
    out = []
    for matrix in (left, np.swapaxes(left, 1, 2)):
        high = matrix.astype(np.float32).astype(jnp.bfloat16)
        low = (matrix - high.astype(np.float64)).astype(np.float32).astype(jnp.bfloat16)
        out += [np.ascontiguousarray(high), np.ascontiguousarray(low)]
    return out


def order_matrix():
    at = np.arange(SIDE)
    matrix = np.zeros((SIDE, SIDE), np.float32)
    matrix[at, (at % 4) * QUARTER + at // 4] = 1.0
    return matrix.astype(jnp.bfloat16)


def split(value):
    high = value.astype(BF16)
    return high, (value - high.astype(F32)).astype(BF16)


def mm(left, right):
    return jnp.dot(left, right, preferred_element_type=F32)


def fold(x, sign):
    (r0, i0), (r1, i1), (r2, i2), (r3, i3) = x
    sr, si, dr, di = r0 + r2, i0 + i2, r0 - r2, i0 - i2
    tr, ti, er, ei = r1 + r3, i1 + i3, r1 - r3, i1 - i3
    first = (dr + ei, di - er)
    second = (dr - ei, di + er)
    if sign > 0:
        first, second = second, first
    return [(sr + tr, si + ti), first, (sr - tr, si - ti), second]


def ready_kernel(
    where_ref, probe_ref, own_ref, amp_ref, order_ref, *refs
):
    rolled_refs = refs[:PIECES]
    amps_ref, peaks_ref, columns = refs[PIECES:]
    for item in range(2):
        down, along = where_ref[0, item], where_ref[1, item]
        for part in range(2):
            value = pltpu.roll(probe_ref[part], down, 0)
            value = pltpu.roll(value, along, 1)
            for ref, first, size in zip(rolled_refs, FIRSTS, SIZES):
                ref[item, part] = value[first : first + size]
        rows = amp_ref[item]
        high = rows.astype(BF16)
        rest = rows - high.astype(F32)
        middle = rest.astype(BF16)
        low = (rest - middle.astype(F32)).astype(BF16)
        order = order_ref[...]
        moved = mm(high, order) + mm(middle, order) + mm(low, order)
        for q in range(4):
            lanes = slice(q * QUARTER, (q + 1) * QUARTER)
            columns[q] = moved[:, lanes]
            for p in range(4):
                amps_ref[item, p * QUARTER : (p + 1) * QUARTER, lanes] = columns[
                    q, pl.ds(p, QUARTER, stride=4), :
                ]
    own = own_ref[0] ** 2 + own_ref[1] ** 2
    beam = probe_ref[0] ** 2 + probe_ref[1] ** 2
    peaks_ref[0] = jnp.full((8, 128), jnp.max(own), F32)
    peaks_ref[1] = jnp.full((8, 128), jnp.max(beam), F32)


def fore_kernel(
    piece, where_ref, own_ref, right_ref, below_ref, diag_ref, rolled_ref, mh_ref, ml_ref,
    spec_ref, wrapped_ref, token_ref,
):
    token_ref[...] = jnp.zeros_like(token_ref)
    at = slice(FIRSTS[piece], FIRSTS[piece] + SIZES[piece])
    lane = lax.broadcasted_iota(jnp.int32, (SIZES[piece], SIDE), 1)
    row = lax.broadcasted_iota(jnp.int32, (SIZES[piece], SIDE), 0) + FIRSTS[piece]
    for item in range(2):
        down, along = where_ref[0, item], where_ref[1, item]
        above, beside = row < down, lane < along
        value = []
        for part in range(2):
            lower = jnp.where(beside, diag_ref[part], below_ref[part])
            upper = jnp.where(beside, right_ref[part, at, :], own_ref[part, at, :])
            value.append(jnp.where(above, lower, upper))
            wrapped_ref[item, part] = value[part]
        beam_r, beam_i = rolled_ref[item, 0], rolled_ref[item, 1]
        psi_r = beam_r * value[0] - beam_i * value[1]
        psi_i = beam_r * value[1] + beam_i * value[0]
        blocks = [
            (psi_r[:, q * QUARTER : (q + 1) * QUARTER], psi_i[:, q * QUARTER : (q + 1) * QUARTER])
            for q in range(4)
        ]
        for p, (br, bi) in enumerate(fold(blocks, -1)):
            hi, lo = split(jnp.concatenate([br, bi], axis=1))
            out = mm(hi, mh_ref[p]) + mm(lo, mh_ref[p]) + mm(hi, ml_ref[p])
            spec_ref[item, 0, :, p * QUARTER : (p + 1) * QUARTER] = out[:, :QUARTER]
            spec_ref[item, 1, :, p * QUARTER : (p + 1) * QUARTER] = out[:, QUARTER:]


def fore(piece, where, own, right, below, diag, rolled, matrices):
    size = SIZES[piece]
    tile = pl.BlockSpec((2, SIDE, SIDE), lambda i: (0, 0, 0))
    full = pl.BlockSpec((2, size, SIDE), lambda i: (0, 0, 0))
    whole = pl.BlockSpec((4, 2 * QUARTER, 2 * QUARTER), lambda i: (0, 0, 0))
    four = pl.BlockSpec((2, 2, size, SIDE), lambda i: (0, 0, 0, 0))
    shape = jax.ShapeDtypeStruct((2, 2, size, SIDE), F32)
    return pl.pallas_call(
        functools.partial(fore_kernel, piece),
        grid=(1,),
        out_shape=[shape, shape, jax.ShapeDtypeStruct((8, 128), F32)],
        in_specs=[sm(), tile, tile, full, full, four, whole, whole],
        out_specs=[four, four, pl.BlockSpec((8, 128), lambda i: (0, 0))],
        compiler_params=params(20),
        cost_estimate=COST,
    )(where, own, right, below, diag, rolled, *matrices[2:])


def rows_of(refs, item, part, first, last, lanes=slice(None)):
    values = []
    for ref, start, size in zip(refs, FIRSTS, SIZES):
        low, high = max(first, start) - start, min(last, start + size) - start
        if low < high:
            values.append(ref[item, part, low:high, lanes])
    return values[0] if len(values) == 1 else jnp.concatenate(values, axis=0)


def update_kernel(where_ref, *refs):
    spec_refs, wrapped_refs, rolled_refs = refs[:PIECES], refs[PIECES : 2 * PIECES], refs[2 * PIECES : 3 * PIECES]
    amps_ref, peaks_ref, lh_ref, ll_ref, mh_ref, ml_ref = refs[3 * PIECES : 3 * PIECES + 6]
    outs = refs[3 * PIECES + 6 :]
    targets, keep_ref, send_ref = outs[:4], outs[4], outs[5]
    high, low, grad, terms, out_sems = outs[6:]
    core = where_ref[2, 0]

    wide = 2 * QUARTER
    for item in range(2):
        for chunk in range(SIDE // wide):
            cols = slice(chunk * wide, (chunk + 1) * wide)
            blocks = [
                tuple(
                    rows_of(spec_refs, item, part, q * QUARTER, (q + 1) * QUARTER, cols)
                    for part in range(2)
                )
                for q in range(4)
            ]
            back = []
            for p, (br, bi) in enumerate(fold(blocks, -1)):
                hi, lo = split(jnp.concatenate([br, bi], axis=0))
                out = mm(lh_ref[p], hi) + mm(lh_ref[p], lo) + mm(ll_ref[p], hi)
                sr, si = out[:QUARTER], out[QUARTER:]
                factor = amps_ref[item, p * QUARTER : (p + 1) * QUARTER, cols] * lax.rsqrt(
                    sr * sr + si * si + 0.25
                )
                hi, lo = split(jnp.concatenate([sr * factor, si * factor], axis=0))
                out = mm(mh_ref[p], hi) + mm(mh_ref[p], lo) + mm(ml_ref[p], hi)
                back.append((out[:QUARTER], out[QUARTER:]))
            for q, (xr, xi) in enumerate(fold(back, 1)):
                rows = slice(q * QUARTER, (q + 1) * QUARTER)
                for part, value in enumerate((xr, xi)):
                    hi, lo = split(value)
                    for half in range(2):
                        p = 2 * chunk + half
                        to = slice(p * wide + part * QUARTER, p * wide + (part + 1) * QUARTER)
                        piece = slice(half * QUARTER, (half + 1) * QUARTER)
                        high[item, rows, to] = hi[:, piece]
                        low[item, rows, to] = lo[:, piece]

    stores = []
    size = QUARTER
    for first in range(0, SIDE, size):
        at = slice(first, first + size)
        lane = lax.broadcasted_iota(jnp.int32, (size, SIDE), 1)
        row = lax.broadcasted_iota(jnp.int32, (size, SIDE), 0) + first
        for item in range(2):
            down, along = where_ref[0, item], where_ref[1, item]
            above, beside = row < down, lane < along
            back = []
            for p in range(4):
                cols = slice(p * wide, (p + 1) * wide)
                hi, lo = high[item, at, cols], low[item, at, cols]
                out = mm(hi, lh_ref[p]) + mm(lo, lh_ref[p]) + mm(hi, ll_ref[p])
                back.append((out[:, :QUARTER], out[:, QUARTER:]))
            back = fold(back, 1)
            back_r = jnp.concatenate([b[0] for b in back], axis=1)
            back_i = jnp.concatenate([b[1] for b in back], axis=1)
            beam_r, beam_i = (rows_of(rolled_refs, item, part, first, first + size) for part in range(2))
            patch_r, patch_i = (rows_of(wrapped_refs, item, part, first, first + size) for part in range(2))
            diff_r = back_r - (beam_r * patch_r - beam_i * patch_i)
            diff_i = back_i - (beam_r * patch_i + beam_i * patch_r)
            term = (beam_r * diff_r + beam_i * diff_i, beam_r * diff_i - beam_i * diff_r)
            grad[item, 0, at, :] = patch_r * diff_r + patch_i * diff_i
            grad[item, 1, at, :] = patch_r * diff_i - patch_i * diff_r
            for part in range(2):
                zero = jnp.zeros_like(term[part])
                upper = jnp.where(above, zero, term[part])
                lower = jnp.where(above, term[part], zero)
                four = (
                    jnp.where(beside, zero, upper),
                    jnp.where(beside, upper, zero),
                    jnp.where(beside, zero, lower),
                    jnp.where(beside, lower, zero),
                )
                for k, value in enumerate(four):
                    if item == 0:
                        terms[k, part, at] = value
                    else:
                        terms[k, part, at] += value
        for k, target in enumerate(targets):
            store = pltpu.make_async_copy(terms.at[k, :, at], target.at[:, at], out_sems.at[len(stores)])
            store.start()
            stores.append(store)
    whole = []
    for part in range(2):
        total = None
        for item in range(2):
            down, along = where_ref[0, item], where_ref[1, item]
            value = pltpu.roll(grad[item, part], (SIDE - down) % SIDE, 0)
            value = pltpu.roll(value, (SIDE - along) % SIDE, 1)
            total = value if total is None else total + value
        whole.append(total)
    keep_ref[:, :SIDE] = jnp.where(core == 0, whole[0], whole[1])
    send_ref[:, :SIDE] = jnp.where(core == 0, whole[1], whole[0])
    peak = jnp.broadcast_to(peaks_ref[0, :1, :], (SIDE, 128))
    keep_ref[:, SIDE:] = peak
    send_ref[:, SIDE:] = peak
    for store in stores:
        store.wait()


def vm():
    return pl.BlockSpec(memory_space=pltpu.VMEM)


def sm():
    return pl.BlockSpec(memory_space=pltpu.SMEM)


def anywhere():
    return pl.BlockSpec(memory_space=pl.ANY)


def params(mebibytes=16):
    return pltpu.CompilerParams(vmem_limit_bytes=mebibytes * 2**20)


def ready(where, probe, own, amplitudes):
    return pl.pallas_call(
        ready_kernel,
        out_shape=tuple(jax.ShapeDtypeStruct((2, 2, size, SIDE), F32) for size in SIZES)
        + (
            jax.ShapeDtypeStruct((2, SIDE, SIDE), F32),
            jax.ShapeDtypeStruct((2, 8, 128), F32),
        ),
        in_specs=[sm()] + [vm()] * 4,
        out_specs=(vm(),) * (PIECES + 2),
        scratch_shapes=[pltpu.VMEM((4, SIDE, QUARTER), F32)],
        compiler_params=params(32),
        cost_estimate=COST,
    )(where, probe, own, amplitudes, jnp.asarray(order_matrix()))


def update(where, specs, wrapped, rolled, amps, peaks, matrices):
    full = jax.ShapeDtypeStruct((2, SIDE, SIDE), F32)
    plane = jax.ShapeDtypeStruct((SIDE, WIDE), F32)
    out_shape = (full,) * 4 + (plane, plane)
    four = pltpu.VMEM((2, 2, SIDE, SIDE), F32)
    half = pltpu.VMEM((2, SIDE, 2 * SIDE), BF16)
    return pl.pallas_call(
        update_kernel,
        out_shape=out_shape,
        in_specs=[sm()] + [vm()] * (3 * PIECES + 6),
        out_specs=(anywhere(),) * 4 + (vm(), vm()),
        scratch_shapes=[
            half,
            half,
            four,
            pltpu.VMEM((4, 2, SIDE, SIDE), F32),
            pltpu.SemaphoreType.DMA((4 * PIECES,)),
        ],
        compiler_params=params(36),
        cost_estimate=COST,
    )(where, *specs, *wrapped, *rolled, amps, peaks, *matrices)


def nothing_kernel(*refs):
    del refs


def tied(values, after):
    count = len(values) + len(after)
    return pl.pallas_call(
        nothing_kernel,
        out_shape=[jax.ShapeDtypeStruct(v.shape, v.dtype) for v in values],
        in_specs=[anywhere()] * count,
        out_specs=[anywhere()] * len(values),
        input_output_aliases={k: k for k in range(len(values))},
        cost_estimate=COST,
    )(*values, *after)


def first_kernel(keep_ref, came_ref, half_ref):
    half_ref[:, :SIDE] = keep_ref[:, :SIDE] + came_ref[:, :SIDE]
    half_ref[:, SIDE:] = jnp.maximum(keep_ref[:, SIDE:], came_ref[:, SIDE:])


def first_sum(keep, came):
    return pl.pallas_call(
        first_kernel,
        out_shape=jax.ShapeDtypeStruct(keep.shape, F32),
        in_specs=[vm()] * 2,
        out_specs=vm(),
        compiler_params=params(),
        cost_estimate=COST,
    )(keep, came)


def lower_kernel(below_ref, corner_ref, after_ref, lower_ref):
    del after_ref
    lower_ref[...] = below_ref[...] + corner_ref[...]


def lowered(below, corner, after):
    rows = pl.BlockSpec((2, QUARTER, SIDE), lambda i: (0, i, 0))
    return pl.pallas_call(
        lower_kernel,
        grid=(4,),
        out_shape=jax.ShapeDtypeStruct(below.shape, F32),
        in_specs=[rows, rows, anywhere()],
        out_specs=rows,
        compiler_params=params(),
        cost_estimate=COST,
    )(below, corner, after)


def middle_kernel(terms_ref, *refs):
    out_ref = refs[-1]
    total = jnp.sum(terms_ref[:, :, :SIDE], axis=0)
    peak = jnp.max(terms_ref[:, :, SIDE:], axis=0)
    out_ref[:, :, :SIDE] = jnp.broadcast_to(total, (out_ref.shape[0],) + total.shape)
    out_ref[:, :, SIDE:] = jnp.broadcast_to(peak, (out_ref.shape[0],) + peak.shape)


def middle(terms, count, after):
    return pl.pallas_call(
        middle_kernel,
        out_shape=jax.ShapeDtypeStruct((count,) + terms.shape[1:], F32),
        in_specs=[vm()] + [anywhere()] * len(after),
        out_specs=vm(),
        compiler_params=params(),
        cost_estimate=COST,
    )(terms, *after)


def share_kernel(terms_ref, start_ref, out_ref):
    total = jnp.sum(terms_ref[:, :, :SIDE], axis=0)
    peak = jnp.max(terms_ref[:, :, SIDE:], axis=0)
    for q in range(4):
        lanes = slice(q * QUARTER, (q + 1) * QUARTER)
        value = start_ref[:, lanes] + 0.5 * total[:, lanes] / (peak + 1e-06)
        out_ref[:, :, lanes] = jnp.broadcast_to(value, out_ref.shape[:2] + (QUARTER,))


def shared(terms, start, count):
    return pl.pallas_call(
        share_kernel,
        out_shape=jax.ShapeDtypeStruct((count,) + start.shape, F32),
        in_specs=[vm()] * 2,
        out_specs=vm(),
        compiler_params=params(),
        cost_estimate=COST,
    )(terms, start)


def shifted(value, axis, steps):
    count = lax.axis_size(axis)
    first, last = (max(0, -steps), min(count, count - steps))
    return lax.ppermute(value, axis, [(source, source + steps) for source in range(first, last)])


def the_long_way(value):
    for _ in range(2):
        value = lax.ppermute(value, "x", [(x, (x + 1) % 4) for x in range(4)])
    return lax.ppermute(value, ROW, [(r // 4 * 4 + (r + 2) % 4, r - 1) for r in range(1, 16)])


def other_core(value):
    return lax.ppermute(value, "core", [(0, 1), (1, 0)])


def base_kernel(scale_ref, own_ref, t_own_ref, base_ref, token_ref):
    base_ref[...] = own_ref[...] + scale_ref[0, 0] * t_own_ref[...]
    token_ref[...] = jnp.zeros_like(token_ref)


def base(scale, own, t_own):
    rows = pl.BlockSpec((2, QUARTER, SIDE), lambda i: (0, i, 0))
    return pl.pallas_call(
        base_kernel,
        grid=(4,),
        out_shape=(jax.ShapeDtypeStruct(own.shape, F32), jax.ShapeDtypeStruct((8, 128), F32)),
        in_specs=[sm(), rows, rows],
        out_specs=(rows, pl.BlockSpec((8, 128), lambda i: (0, 0))),
        compiler_params=params(),
        cost_estimate=COST,
    )(scale, own, t_own)


def object_kernel(scale_ref, base_ref, left_ref, above_ref, out_ref, token_ref):
    out_ref[...] = base_ref[...] + scale_ref[0, 0] * (left_ref[...] + above_ref[...])
    token_ref[...] = jnp.zeros_like(token_ref)


def finished_object(scale, start, left, above):
    rows = pl.BlockSpec((2, QUARTER, SIDE), lambda i: (0, i, 0))
    return pl.pallas_call(
        object_kernel,
        grid=(4,),
        out_shape=(jax.ShapeDtypeStruct(start.shape, F32), jax.ShapeDtypeStruct((8, 128), F32)),
        in_specs=[sm()] + [rows] * 3,
        out_specs=(rows, pl.BlockSpec((8, 128), lambda i: (0, 0))),
        compiler_params=params(),
        cost_estimate=COST,
    )(scale, start, left, above)


def probe_kernel(core_ref, mine_ref, other_ref, out_ref):
    core = core_ref[0, 0]
    out_ref[core] = mine_ref[...]
    out_ref[1 - core] = other_ref[...]


def joined(core, mine, other):
    return pl.pallas_call(
        probe_kernel,
        out_shape=jax.ShapeDtypeStruct((2, SIDE, SIDE), F32),
        in_specs=[sm(), vm(), vm()],
        out_specs=vm(),
        compiler_params=params(),
        cost_estimate=COST,
    )(core, mine, other)


def on_device(object_field, probe, amplitudes, positions):
    row, col, core = lax.axis_index(ROW), lax.axis_index(COL), lax.axis_index("core")
    where = jnp.stack(
        [positions[:, 0] - row * SIDE, positions[:, 1] - col * SIDE, jnp.stack([core, row]).astype(jnp.int32)]
    )
    matrices = [jnp.asarray(m) for m in split_matrices()]
    pieces = [object_field[:, first : first + size] for first, size in zip(FIRSTS, SIZES)]
    right = shifted(object_field, COL, -1)
    *rolled, amps, peaks = ready(where, probe, object_field, amplitudes)
    scale = 0.9 / (peaks[1, :1, :1] + 1e-06)
    specs, wrapped, tokens = [], [], []
    for k, piece in enumerate(pieces):
        below = the_long_way(piece) if k == 3 else shifted(piece, ROW, -1)
        if k in (0, 2):
            (below,) = tied((below,), tokens[:1] if k else (peaks,))
        corner = shifted(below, COL, -1)
        spec, wrap, token = fore(k, where, object_field, right, below, corner, rolled[k], matrices)
        specs.append(spec)
        wrapped.append(wrap)
        tokens.append(token)
    t_own, t_right, t_below, t_corner, keep, send = update(
        where, specs, wrapped, rolled, amps, peaks, matrices
    )

    corner = shifted(t_corner, COL, 1)
    half = first_sum(keep, other_core(send))
    share = SIDE // 16
    terms = lax.all_to_all(half.reshape(16, share, WIDE), ROW, 0, 0)
    lower = lowered(t_below, corner, half)
    from_above = shifted(lower, ROW, 1)
    (t_right,) = tied((t_right,), (half,))
    from_left = shifted(t_right, COL, 1)
    terms = middle(terms, 4, (lower,))
    terms = lax.all_to_all(terms, "z", 0, 0)
    at = lax.axis_index(ROW) * share
    start = lax.dynamic_slice(probe, (core, at, jnp.zeros_like(at)), (1, share, SIDE))[0]
    shares = shared(terms, start, 16)
    mine = lax.all_to_all(shares, ROW, 0, 0).reshape(SIDE, SIDE)
    begun, _ = base(scale, object_field, t_own)
    new_object, token = finished_object(scale, begun, from_left, from_above)
    (mine,) = tied((mine,), (token,))
    new_probe = joined(core.astype(jnp.int32).reshape(1, 1), mine, other_core(mine))
    return (new_object, new_probe)


ROW = ("y", "x")
COL = ("z", "core")


def solution(mesh):
    chips = jax.sharding.Mesh(mesh.devices.reshape(4, 4, 4, 2), ROW + COL)
    in_specs = (P(None, ROW, COL), P(), P(ROW + COL, None, None), P(ROW + COL, None))
    out_specs = (P(None, ROW, COL), P())
    return jax.shard_map(
        on_device, mesh=chips, in_specs=in_specs, out_specs=out_specs, check_vma=False
    )
```

```python
import functools
import math

import jax
import jax.numpy as jnp
import numpy as np
from jax import lax
from jax.experimental import pallas as pl
from jax.experimental.pallas import tpu as pltpu
from jax.sharding import PartitionSpec as P

SIDE = 512
QUARTER = 128
SIZES = (144, 144, 128, 96)
FIRSTS = (0, 144, 288, 416)
WIDE = SIDE + 128
PIECES = len(SIZES)
COST = pl.CostEstimate(flops=0, bytes_accessed=0, transcendentals=0)
F32 = jnp.float32
BF16 = jnp.bfloat16


def split_matrices():
    k = np.arange(QUARTER)[:, None]
    n = np.arange(QUARTER)[None, :]
    parts = []
    for p in range(4):
        angle = 2.0 * np.pi * (((4 * k + p) * n) % SIDE) / SIDE
        re, im = np.cos(angle) / np.sqrt(SIDE), -np.sin(angle) / np.sqrt(SIDE)
        parts.append(np.block([[re, -im], [im, re]]))
    left = np.stack(parts)
    out = []
    for matrix in (left, np.swapaxes(left, 1, 2)):
        high = matrix.astype(np.float32).astype(jnp.bfloat16)
        low = (matrix - high.astype(np.float64)).astype(np.float32).astype(jnp.bfloat16)
        out += [np.ascontiguousarray(high), np.ascontiguousarray(low)]
    return out


def order_matrix():
    at = np.arange(SIDE)
    matrix = np.zeros((SIDE, SIDE), np.float32)
    matrix[at, (at % 4) * QUARTER + at // 4] = 1.0
    return matrix.astype(jnp.bfloat16)


def split(value):
    high = value.astype(BF16)
    return high, (value - high.astype(F32)).astype(BF16)


def mm(left, right):
    return jnp.dot(left, right, preferred_element_type=F32)


def fold(x, sign):
    (r0, i0), (r1, i1), (r2, i2), (r3, i3) = x
    sr, si, dr, di = r0 + r2, i0 + i2, r0 - r2, i0 - i2
    tr, ti, er, ei = r1 + r3, i1 + i3, r1 - r3, i1 - i3
    first = (dr + ei, di - er)
    second = (dr - ei, di + er)
    if sign > 0:
        first, second = second, first
    return [(sr + tr, si + ti), first, (sr - tr, si - ti), second]


def ready_kernel(
    where_ref, probe_ref, own_ref, amp_ref, order_ref, *refs
):
    rolled_refs = refs[:PIECES]
    amps_ref, peaks_ref, columns = refs[PIECES:]
    for item in range(2):
        down, along = where_ref[0, item], where_ref[1, item]
        for part in range(2):
            value = pltpu.roll(probe_ref[part], down, 0)
            value = pltpu.roll(value, along, 1)
            for ref, first, size in zip(rolled_refs, FIRSTS, SIZES):
                ref[item, part] = value[first : first + size]
        rows = amp_ref[item]
        high = rows.astype(BF16)
        rest = rows - high.astype(F32)
        middle = rest.astype(BF16)
        low = (rest - middle.astype(F32)).astype(BF16)
        order = order_ref[...]
        moved = mm(high, order) + mm(middle, order) + mm(low, order)
        for q in range(4):
            lanes = slice(q * QUARTER, (q + 1) * QUARTER)
            columns[q] = moved[:, lanes]
            for p in range(4):
                amps_ref[item, p * QUARTER : (p + 1) * QUARTER, lanes] = columns[
                    q, pl.ds(p, QUARTER, stride=4), :
                ]
    own = own_ref[0] ** 2 + own_ref[1] ** 2
    beam = probe_ref[0] ** 2 + probe_ref[1] ** 2
    peaks_ref[0] = jnp.full((8, 128), jnp.max(own), F32)
    peaks_ref[1] = jnp.full((8, 128), jnp.max(beam), F32)


def fore_kernel(
    piece, where_ref, own_ref, right_ref, below_ref, diag_ref, rolled_ref, mh_ref, ml_ref,
    spec_ref, wrapped_ref, token_ref,
):
    token_ref[...] = jnp.zeros_like(token_ref)
    at = slice(FIRSTS[piece], FIRSTS[piece] + SIZES[piece])
    lane = lax.broadcasted_iota(jnp.int32, (SIZES[piece], SIDE), 1)
    row = lax.broadcasted_iota(jnp.int32, (SIZES[piece], SIDE), 0) + FIRSTS[piece]
    for item in range(2):
        down, along = where_ref[0, item], where_ref[1, item]
        above, beside = row < down, lane < along
        value = []
        for part in range(2):
            lower = jnp.where(beside, diag_ref[part], below_ref[part])
            upper = jnp.where(beside, right_ref[part, at, :], own_ref[part, at, :])
            value.append(jnp.where(above, lower, upper))
            wrapped_ref[item, part] = value[part]
        beam_r, beam_i = rolled_ref[item, 0], rolled_ref[item, 1]
        psi_r = beam_r * value[0] - beam_i * value[1]
        psi_i = beam_r * value[1] + beam_i * value[0]
        blocks = [
            (psi_r[:, q * QUARTER : (q + 1) * QUARTER], psi_i[:, q * QUARTER : (q + 1) * QUARTER])
            for q in range(4)
        ]
        for p, (br, bi) in enumerate(fold(blocks, -1)):
            hi, lo = split(jnp.concatenate([br, bi], axis=1))
            out = mm(hi, mh_ref[p]) + mm(lo, mh_ref[p]) + mm(hi, ml_ref[p])
            spec_ref[item, 0, :, p * QUARTER : (p + 1) * QUARTER] = out[:, :QUARTER]
            spec_ref[item, 1, :, p * QUARTER : (p + 1) * QUARTER] = out[:, QUARTER:]


def fore(piece, where, own, right, below, diag, rolled, matrices):
    size = SIZES[piece]
    tile = pl.BlockSpec((2, SIDE, SIDE), lambda i: (0, 0, 0))
    full = pl.BlockSpec((2, size, SIDE), lambda i: (0, 0, 0))
    whole = pl.BlockSpec((4, 2 * QUARTER, 2 * QUARTER), lambda i: (0, 0, 0))
    four = pl.BlockSpec((2, 2, size, SIDE), lambda i: (0, 0, 0, 0))
    shape = jax.ShapeDtypeStruct((2, 2, size, SIDE), F32)
    return pl.pallas_call(
        functools.partial(fore_kernel, piece),
        grid=(1,),
        out_shape=[shape, shape, jax.ShapeDtypeStruct((8, 128), F32)],
        in_specs=[sm(), tile, tile, full, full, four, whole, whole],
        out_specs=[four, four, pl.BlockSpec((8, 128), lambda i: (0, 0))],
        compiler_params=params(20),
        cost_estimate=COST,
    )(where, own, right, below, diag, rolled, *matrices[2:])


def rows_of(refs, item, part, first, last, lanes=slice(None)):
    values = []
    for ref, start, size in zip(refs, FIRSTS, SIZES):
        low, high = max(first, start) - start, min(last, start + size) - start
        if low < high:
            values.append(ref[item, part, low:high, lanes])
    return values[0] if len(values) == 1 else jnp.concatenate(values, axis=0)


def update_kernel(where_ref, *refs):
    spec_refs, wrapped_refs, rolled_refs = refs[:PIECES], refs[PIECES : 2 * PIECES], refs[2 * PIECES : 3 * PIECES]
    amps_ref, peaks_ref, lh_ref, ll_ref, mh_ref, ml_ref = refs[3 * PIECES : 3 * PIECES + 6]
    outs = refs[3 * PIECES + 6 :]
    targets, keep_ref, send_ref = outs[:4], outs[4], outs[5]
    high, low, grad, terms, out_sems = outs[6:]
    core = where_ref[2, 0]

    wide = 2 * QUARTER
    for item in range(2):
        for chunk in range(SIDE // wide):
            cols = slice(chunk * wide, (chunk + 1) * wide)
            blocks = [
                tuple(
                    rows_of(spec_refs, item, part, q * QUARTER, (q + 1) * QUARTER, cols)
                    for part in range(2)
                )
                for q in range(4)
            ]
            back = []
            for p, (br, bi) in enumerate(fold(blocks, -1)):
                hi, lo = split(jnp.concatenate([br, bi], axis=0))
                out = mm(lh_ref[p], hi) + mm(lh_ref[p], lo) + mm(ll_ref[p], hi)
                sr, si = out[:QUARTER], out[QUARTER:]
                factor = amps_ref[item, p * QUARTER : (p + 1) * QUARTER, cols] * lax.rsqrt(
                    sr * sr + si * si + 0.25
                )
                hi, lo = split(jnp.concatenate([sr * factor, si * factor], axis=0))
                out = mm(mh_ref[p], hi) + mm(mh_ref[p], lo) + mm(ml_ref[p], hi)
                back.append((out[:QUARTER], out[QUARTER:]))
            for q, (xr, xi) in enumerate(fold(back, 1)):
                rows = slice(q * QUARTER, (q + 1) * QUARTER)
                for part, value in enumerate((xr, xi)):
                    hi, lo = split(value)
                    for half in range(2):
                        p = 2 * chunk + half
                        to = slice(p * wide + part * QUARTER, p * wide + (part + 1) * QUARTER)
                        piece = slice(half * QUARTER, (half + 1) * QUARTER)
                        high[item, rows, to] = hi[:, piece]
                        low[item, rows, to] = lo[:, piece]

    stores = []
    size = QUARTER
    for first in range(0, SIDE, size):
        at = slice(first, first + size)
        lane = lax.broadcasted_iota(jnp.int32, (size, SIDE), 1)
        row = lax.broadcasted_iota(jnp.int32, (size, SIDE), 0) + first
        for item in range(2):
            down, along = where_ref[0, item], where_ref[1, item]
            above, beside = row < down, lane < along
            back = []
            for p in range(4):
                cols = slice(p * wide, (p + 1) * wide)
                hi, lo = high[item, at, cols], low[item, at, cols]
                out = mm(hi, lh_ref[p]) + mm(lo, lh_ref[p]) + mm(hi, ll_ref[p])
                back.append((out[:, :QUARTER], out[:, QUARTER:]))
            back = fold(back, 1)
            back_r = jnp.concatenate([b[0] for b in back], axis=1)
            back_i = jnp.concatenate([b[1] for b in back], axis=1)
            beam_r, beam_i = (rows_of(rolled_refs, item, part, first, first + size) for part in range(2))
            patch_r, patch_i = (rows_of(wrapped_refs, item, part, first, first + size) for part in range(2))
            diff_r = back_r - (beam_r * patch_r - beam_i * patch_i)
            diff_i = back_i - (beam_r * patch_i + beam_i * patch_r)
            term = (beam_r * diff_r + beam_i * diff_i, beam_r * diff_i - beam_i * diff_r)
            grad[item, 0, at, :] = patch_r * diff_r + patch_i * diff_i
            grad[item, 1, at, :] = patch_r * diff_i - patch_i * diff_r
            for part in range(2):
                zero = jnp.zeros_like(term[part])
                upper = jnp.where(above, zero, term[part])
                lower = jnp.where(above, term[part], zero)
                four = (
                    jnp.where(beside, zero, upper),
                    jnp.where(beside, upper, zero),
                    jnp.where(beside, zero, lower),
                    jnp.where(beside, lower, zero),
                )
                for k, value in enumerate(four):
                    if item == 0:
                        terms[k, part, at] = value
                    else:
                        terms[k, part, at] += value
        for k, target in enumerate(targets):
            store = pltpu.make_async_copy(terms.at[k, :, at], target.at[:, at], out_sems.at[len(stores)])
            store.start()
            stores.append(store)
    whole = []
    for part in range(2):
        total = None
        for item in range(2):
            down, along = where_ref[0, item], where_ref[1, item]
            value = pltpu.roll(grad[item, part], (SIDE - down) % SIDE, 0)
            value = pltpu.roll(value, (SIDE - along) % SIDE, 1)
            total = value if total is None else total + value
        whole.append(total)
    keep_ref[:, :SIDE] = jnp.where(core == 0, whole[0], whole[1])
    send_ref[:, :SIDE] = jnp.where(core == 0, whole[1], whole[0])
    peak = jnp.broadcast_to(peaks_ref[0, :1, :], (SIDE, 128))
    keep_ref[:, SIDE:] = peak
    send_ref[:, SIDE:] = peak
    for store in stores:
        store.wait()


def vm():
    return pl.BlockSpec(memory_space=pltpu.VMEM)


def sm():
    return pl.BlockSpec(memory_space=pltpu.SMEM)


def anywhere():
    return pl.BlockSpec(memory_space=pl.ANY)


def params(mebibytes=16):
    return pltpu.CompilerParams(vmem_limit_bytes=mebibytes * 2**20)


def ready(where, probe, own, amplitudes):
    return pl.pallas_call(
        ready_kernel,
        out_shape=tuple(jax.ShapeDtypeStruct((2, 2, size, SIDE), F32) for size in SIZES)
        + (
            jax.ShapeDtypeStruct((2, SIDE, SIDE), F32),
            jax.ShapeDtypeStruct((2, 8, 128), F32),
        ),
        in_specs=[sm()] + [vm()] * 4,
        out_specs=(vm(),) * (PIECES + 2),
        scratch_shapes=[pltpu.VMEM((4, SIDE, QUARTER), F32)],
        compiler_params=params(32),
        cost_estimate=COST,
    )(where, probe, own, amplitudes, jnp.asarray(order_matrix()))


def update(where, specs, wrapped, rolled, amps, peaks, matrices):
    full = jax.ShapeDtypeStruct((2, SIDE, SIDE), F32)
    plane = jax.ShapeDtypeStruct((SIDE, WIDE), F32)
    out_shape = (full,) * 4 + (plane, plane)
    four = pltpu.VMEM((2, 2, SIDE, SIDE), F32)
    half = pltpu.VMEM((2, SIDE, 2 * SIDE), BF16)
    return pl.pallas_call(
        update_kernel,
        out_shape=out_shape,
        in_specs=[sm()] + [vm()] * (3 * PIECES + 6),
        out_specs=(anywhere(),) * 4 + (vm(), vm()),
        scratch_shapes=[
            half,
            half,
            four,
            pltpu.VMEM((4, 2, SIDE, SIDE), F32),
            pltpu.SemaphoreType.DMA((4 * PIECES,)),
        ],
        compiler_params=params(36),
        cost_estimate=COST,
    )(where, *specs, *wrapped, *rolled, amps, peaks, *matrices)


def nothing_kernel(*refs):
    del refs


def tied(values, after):
    count = len(values) + len(after)
    return pl.pallas_call(
        nothing_kernel,
        out_shape=[jax.ShapeDtypeStruct(v.shape, v.dtype) for v in values],
        in_specs=[anywhere()] * count,
        out_specs=[anywhere()] * len(values),
        input_output_aliases={k: k for k in range(len(values))},
        cost_estimate=COST,
    )(*values, *after)


def first_kernel(keep_ref, came_ref, half_ref):
    half_ref[:, :SIDE] = keep_ref[:, :SIDE] + came_ref[:, :SIDE]
    half_ref[:, SIDE:] = jnp.maximum(keep_ref[:, SIDE:], came_ref[:, SIDE:])


def first_sum(keep, came):
    return pl.pallas_call(
        first_kernel,
        out_shape=jax.ShapeDtypeStruct(keep.shape, F32),
        in_specs=[vm()] * 2,
        out_specs=vm(),
        compiler_params=params(),
        cost_estimate=COST,
    )(keep, came)


def lower_kernel(below_ref, corner_ref, after_ref, lower_ref):
    del after_ref
    lower_ref[...] = below_ref[...] + corner_ref[...]


def lowered(below, corner, after):
    rows = pl.BlockSpec((2, QUARTER, SIDE), lambda i: (0, i, 0))
    return pl.pallas_call(
        lower_kernel,
        grid=(4,),
        out_shape=jax.ShapeDtypeStruct(below.shape, F32),
        in_specs=[rows, rows, anywhere()],
        out_specs=rows,
        compiler_params=params(),
        cost_estimate=COST,
    )(below, corner, after)


def middle_kernel(terms_ref, *refs):
    out_ref = refs[-1]
    total = jnp.sum(terms_ref[:, :, :SIDE], axis=0)
    peak = jnp.max(terms_ref[:, :, SIDE:], axis=0)
    out_ref[:, :, :SIDE] = jnp.broadcast_to(total, (out_ref.shape[0],) + total.shape)
    out_ref[:, :, SIDE:] = jnp.broadcast_to(peak, (out_ref.shape[0],) + peak.shape)


def middle(terms, count, after):
    return pl.pallas_call(
        middle_kernel,
        out_shape=jax.ShapeDtypeStruct((count,) + terms.shape[1:], F32),
        in_specs=[vm()] + [anywhere()] * len(after),
        out_specs=vm(),
        compiler_params=params(),
        cost_estimate=COST,
    )(terms, *after)


def share_kernel(terms_ref, start_ref, out_ref):
    total = jnp.sum(terms_ref[:, :, :SIDE], axis=0)
    peak = jnp.max(terms_ref[:, :, SIDE:], axis=0)
    for q in range(4):
        lanes = slice(q * QUARTER, (q + 1) * QUARTER)
        value = start_ref[:, lanes] + 0.5 * total[:, lanes] / (peak + 1e-06)
        out_ref[:, :, lanes] = jnp.broadcast_to(value, out_ref.shape[:2] + (QUARTER,))


def shared(terms, start, count):
    return pl.pallas_call(
        share_kernel,
        out_shape=jax.ShapeDtypeStruct((count,) + start.shape, F32),
        in_specs=[vm()] * 2,
        out_specs=vm(),
        compiler_params=params(),
        cost_estimate=COST,
    )(terms, start)


def shifted(value, axis, steps):
    count = lax.axis_size(axis)
    first, last = (max(0, -steps), min(count, count - steps))
    return lax.ppermute(value, axis, [(source, source + steps) for source in range(first, last)])


def other_core(value):
    return lax.ppermute(value, "core", [(0, 1), (1, 0)])


def base_kernel(scale_ref, own_ref, t_own_ref, base_ref, token_ref):
    base_ref[...] = own_ref[...] + scale_ref[0, 0] * t_own_ref[...]
    token_ref[...] = jnp.zeros_like(token_ref)


def base(scale, own, t_own):
    rows = pl.BlockSpec((2, QUARTER, SIDE), lambda i: (0, i, 0))
    return pl.pallas_call(
        base_kernel,
        grid=(4,),
        out_shape=(jax.ShapeDtypeStruct(own.shape, F32), jax.ShapeDtypeStruct((8, 128), F32)),
        in_specs=[sm(), rows, rows],
        out_specs=(rows, pl.BlockSpec((8, 128), lambda i: (0, 0))),
        compiler_params=params(),
        cost_estimate=COST,
    )(scale, own, t_own)


def object_kernel(scale_ref, base_ref, left_ref, above_ref, out_ref, token_ref):
    out_ref[...] = base_ref[...] + scale_ref[0, 0] * (left_ref[...] + above_ref[...])
    token_ref[...] = jnp.zeros_like(token_ref)


def finished_object(scale, start, left, above):
    rows = pl.BlockSpec((2, QUARTER, SIDE), lambda i: (0, i, 0))
    return pl.pallas_call(
        object_kernel,
        grid=(4,),
        out_shape=(jax.ShapeDtypeStruct(start.shape, F32), jax.ShapeDtypeStruct((8, 128), F32)),
        in_specs=[sm()] + [rows] * 3,
        out_specs=(rows, pl.BlockSpec((8, 128), lambda i: (0, 0))),
        compiler_params=params(),
        cost_estimate=COST,
    )(scale, start, left, above)


def probe_kernel(core_ref, mine_ref, other_ref, out_ref):
    core = core_ref[0, 0]
    out_ref[core] = mine_ref[...]
    out_ref[1 - core] = other_ref[...]


def joined(core, mine, other):
    return pl.pallas_call(
        probe_kernel,
        out_shape=jax.ShapeDtypeStruct((2, SIDE, SIDE), F32),
        in_specs=[sm(), vm(), vm()],
        out_specs=vm(),
        compiler_params=params(),
        cost_estimate=COST,
    )(core, mine, other)


def on_device(object_field, probe, amplitudes, positions):
    row, col, core = lax.axis_index(ROW), lax.axis_index(COL), lax.axis_index("core")
    where = jnp.stack(
        [positions[:, 0] - row * SIDE, positions[:, 1] - col * SIDE, jnp.stack([core, row]).astype(jnp.int32)]
    )
    matrices = [jnp.asarray(m) for m in split_matrices()]
    pieces = [object_field[:, first : first + size] for first, size in zip(FIRSTS, SIZES)]
    right = shifted(object_field, COL, -1)
    *rolled, amps, peaks = ready(where, probe, object_field, amplitudes)
    scale = 0.9 / (peaks[1, :1, :1] + 1e-06)
    specs, wrapped, tokens = [], [], []
    for k, piece in enumerate(pieces):
        below = shifted(piece, ROW, -1)
        if k in (0, 3):
            (below,) = tied((below,), tokens[:1] if k else (peaks,))
        corner = shifted(below, COL, -1)
        spec, wrap, token = fore(k, where, object_field, right, below, corner, rolled[k], matrices)
        specs.append(spec)
        wrapped.append(wrap)
        tokens.append(token)
    t_own, t_right, t_below, t_corner, keep, send = update(
        where, specs, wrapped, rolled, amps, peaks, matrices
    )

    corner = shifted(t_corner, COL, 1)
    half = first_sum(keep, other_core(send))
    share = SIDE // 16
    terms = lax.all_to_all(half.reshape(16, share, WIDE), ROW, 0, 0)
    lower = lowered(t_below, corner, half)
    from_above = shifted(lower, ROW, 1)
    (t_right,) = tied((t_right,), (half,))
    from_left = shifted(t_right, COL, 1)
    terms = middle(terms, 4, (lower,))
    terms = lax.all_to_all(terms, "z", 0, 0)
    at = lax.axis_index(ROW) * share
    start = lax.dynamic_slice(probe, (core, at, jnp.zeros_like(at)), (1, share, SIDE))[0]
    shares = shared(terms, start, 16)
    mine = lax.all_to_all(shares, ROW, 0, 0).reshape(SIDE, SIDE)
    begun, _ = base(scale, object_field, t_own)
    new_object, token = finished_object(scale, begun, from_left, from_above)
    (mine,) = tied((mine,), (token,))
    new_probe = joined(core.astype(jnp.int32).reshape(1, 1), mine, other_core(mine))
    return (new_object, new_probe)


ROW = ("y", "x")
COL = ("z", "core")


def solution(mesh):
    chips = jax.sharding.Mesh(mesh.devices.reshape(4, 4, 4, 2), ROW + COL)
    in_specs = (P(None, ROW, COL), P(), P(ROW + COL, None, None), P(ROW + COL, None))
    out_specs = (P(None, ROW, COL), P())
    return jax.shard_map(
        on_device, mesh=chips, in_specs=in_specs, out_specs=out_specs, check_vma=False
    )
```
